32 devices in a mesh: seq: 8 (over y, x, core), fsdp: 4 (over z).
Axes of the slice: x: 2, y: 2, z: 4, core: 2. Of those that a mesh axis runs over, the one named last changes fastest.
Arguments:
- tokens: bfloat16 [4, 4096, 1536], P('fsdp', 'seq'), may hold values from -6 to 6
- cotangent: bfloat16 [4, 4096, 1536], P('fsdp', 'seq'), may hold values from -6 to 6
- arrival_order: int32 [4, 4096], P('fsdp', 'seq'), may hold values from 0 to 4095, as said below
- lengths: int32 [4, 4], P('fsdp'), may hold values from 1 to 3840, 4096 in all within a row
- norm_gain: bfloat16 [1536], P('fsdp'), may hold values from 0.5 to 1.5
- w_query: bfloat16 [1536, 1536], P('fsdp'), may hold values from -0.15625 to 0.15625
- w_kv: bfloat16 [1536, 384], P('fsdp'), may hold values from -0.15625 to 0.15625
- w_out: bfloat16 [1536, 1536], P('fsdp'), may hold values from -1.25 to 1.25
- ffn_gain: bfloat16 [1536], P('fsdp'), may hold values from 0.5 to 1.5
- w_gate_up: bfloat16 [1536, 9216], P('fsdp'), may hold values from -0.15625 to 0.15625
- w_down: bfloat16 [4608, 1536], P('fsdp'), may hold values from -0.09375 to 0.09375
Outputs:
- block_out: bfloat16 [4, 4096, 1536], P('fsdp', 'seq')
- grad_tokens: bfloat16 [4, 4096, 1536], P('fsdp', 'seq')
- grad_norm_gain: float32 [1536], P('fsdp')
- grad_w_query: float32 [1536, 1536], P('fsdp')
- grad_w_kv: float32 [1536, 384], P('fsdp')
- grad_w_out: float32 [1536, 1536], P('fsdp')
- grad_ffn_gain: float32 [1536], P('fsdp')
- grad_w_gate_up: float32 [1536, 9216], P('fsdp')
- grad_w_down: float32 [4608, 1536], P('fsdp')
The draws below stay inside these ranges and needn't reach their ends.
Inputs may be any that keep to these rules, and one draw needn't show every extreme that they name: `arrival_order`: in each group the entries are a permutation of the packed places. Of the 512 rows that one index of seq holds, exactly 128 have packed places on each of half the indices of seq (places s * 512 to (s + 1) * 512 - 1 belong to index s) and none on the others. Each group's 4 lengths sum to 4096, and one of them is 3840.
All inputs are finite; a program needn't handle non-finite values.
Results may differ from the reference program's by a relative error of at most 0.02.
Values may be sent and summed in bfloat16 or wider, within the bound.
No kernel may reach another device: no remote copies, remote signals or barrier semaphores. Data moves between devices by JAX's collectives and lax.ppermute only.
A program may use at most 320 MiB of HBM per device.

```python
import math
import jax
import jax.numpy as jnp
import numpy as np
from jax import lax

D = 1536
H = 8
HD = 192
FF = 4608
WINDOW = 1024
SEQS = 4
TOK_DEV = 512
NB = 4
TOKENS = 4096
MOST = 3840
N_SEQ = 8


def draw_arrival_order(key, part):
    key = jax.random.fold_in(key, 11)
    half = N_SEQ // 2
    capacity = 2 * TOK_DEV // N_SEQ

    def one_group(group_key):
        shift_key, owner_key, shuffle_key = jax.random.split(group_key, 3)
        shifts = jax.random.permutation(shift_key, N_SEQ)[:half]
        owner_keys = jax.random.split(owner_key, N_SEQ)
        owned = jax.vmap(lambda member_key: jax.random.permutation(member_key, TOK_DEV))(owner_keys)
        owned = owned.reshape(N_SEQ, half, capacity)
        sources = jnp.arange(N_SEQ)
        owners = (sources[:, None] + shifts[None, :]) % N_SEQ
        picked = owned[owners, jnp.arange(half)[None, :]]
        placed = (owners[:, :, None] * TOK_DEV + picked).reshape(N_SEQ, TOK_DEV)
        shuffle_keys = jax.random.split(shuffle_key, N_SEQ)
        placed = jax.vmap(lambda member_key, member_rows: jax.random.permutation(member_key, member_rows))(shuffle_keys, placed)
        return placed.reshape(TOKENS)
    return jax.vmap(one_group)(jax.random.split(key, NB)).astype(jnp.int32)


def block_scale(own_key, shape, cuts, least, high):
    loudness = 1.0
    for position, shards_of in cuts:
        heights = jax.random.uniform(jax.random.fold_in(jax.random.fold_in(own_key, 6), position), (shards_of,), jnp.float32, least / len(cuts), high / len(cuts))
        loudness = loudness * jnp.repeat(jnp.exp(heights), shape[position] // shards_of).reshape((-1,) + (1,) * (len(shape) - 1 - position))
    return loudness


def split_up(amount, total, limit, slope):
    weights = [(1 << 20) // math.isqrt(standing ** slope) + 1 for standing in range(2, amount + 1)]
    spare, holding = total - limit - (amount - 1), [1] * (amount - 1)
    while spare > 0:
        movable = [i for i in range(amount - 1) if holding[i] < limit]
        pool, left = sum([weights[i] for i in movable]), spare
        for i in movable:
            addition = min(limit - holding[i], max(1, left * weights[i] // pool), spare)
            holding[i] = holding[i] + addition
            spare = spare - addition
    return np.array([limit] + holding)


def ragged_sizes(stream_key, count, total, most, skew):
    if count == 2:
        one = jax.random.randint(stream_key, (), max(1, total - most), min(most, total - 1) + 1)
        return jnp.stack([one, total - one])
    sizes = jnp.asarray(split_up(count, total, most, skew), jnp.int32)
    pairs = (count - 1) // 2
    donor, taker = sizes[1:1 + 2 * pairs:2], sizes[2:2 + 2 * pairs:2]
    slack = jnp.minimum(donor - 1, most - taker)
    passed = jax.random.randint(jax.random.fold_in(stream_key, 1), (pairs,), 0, 1 << 20) % (slack + 1)
    sizes = sizes.at[1:1 + 2 * pairs:2].set(donor - passed).at[2:2 + 2 * pairs:2].set(taker + passed)
    return sizes[jax.random.permutation(jax.random.fold_in(stream_key, 2), count)]


def noise(rng, extent, spread, most, cuts=(), kind=jnp.bfloat16):
    factor_of = block_scale(rng, extent, cuts, -0.22, 0.18) if cuts else 1.0
    result = jax.random.normal(rng, extent, jnp.float32) * spread * factor_of
    return jnp.minimum(jnp.maximum(result, -most), most).astype(kind)


def setup_inputs(seed: int = 0) -> dict:
    seeds = jax.random.split(jax.random.key(seed), 12)
    tokens = noise(seeds[0], (NB, TOKENS, D), 1.0, 6.0, ((0, 4), (1, 8)))
    cotangent = noise(seeds[1], (NB, TOKENS, D), 1.0, 6.0, ((0, 4), (1, 8)))
    arrival_order = draw_arrival_order(jax.random.fold_in(seeds[11], 71), 0)
    lengths = jax.vmap(lambda own: ragged_sizes(own, SEQS, TOKENS, MOST, 2))(jax.random.split(seeds[3], NB)).reshape((NB, SEQS)).astype(jnp.int32)
    norm_gain = jnp.clip(1.0 + 0.1 * jax.random.normal(seeds[4], (D,), jnp.float32), 0.5, 1.5).astype(jnp.bfloat16)
    w_query = noise(seeds[5], (D, D), D ** -0.5, 0.15625, ((0, 4),))
    w_kv = noise(seeds[6], (D, 2 * HD), D ** -0.5, 0.15625, ((0, 4),))
    w_out = noise(seeds[7], (D, D), (D // 64) ** -0.5, 1.25, ((0, 4),))
    ffn_gain = jnp.clip(1.0 + 0.1 * jax.random.normal(seeds[8], (D,), jnp.float32), 0.5, 1.5).astype(jnp.bfloat16)
    w_gate_up = noise(seeds[9], (D, 2 * FF), D ** -0.5, 0.15625, ((0, 4),))
    w_down = noise(seeds[10], (FF, D), FF ** -0.5, 0.09375, ((0, 4),))
    return {"tokens": tokens, "cotangent": cotangent, "arrival_order": arrival_order, "lengths": lengths, "norm_gain": norm_gain, "w_query": w_query, "w_kv": w_kv, "w_out": w_out, "ffn_gain": ffn_gain, "w_gate_up": w_gate_up, "w_down": w_down}


EPSILON = 1e-06
ROPE_BASE = 10000.0
MASKED = -1e+30
HIGHEST = lax.Precision.HIGHEST

@jax.custom_vjp
def low(v):
    return lax.optimization_barrier(v.astype(jnp.bfloat16)).astype(jnp.float32)

@jax.custom_vjp
def low_back(v):
    return v

def low_keep(v):
    return (low(v), None)

def low_pass(kept, grad):
    return (grad,)

def back_keep(v):
    return (v, None)

def back_low(kept, grad):
    return (low(grad),)
low.defvjp(low_keep, low_pass)
low_back.defvjp(back_keep, back_low)

def rms_scale(values, gain):
    return values * lax.rsqrt(lax.optimization_barrier(jnp.mean(values * values, axis=-1, keepdims=True)) + EPSILON) * gain

def rotate(heads, cosine, sine):
    half = heads.shape[-1] // 2
    first_half = heads[..., :half]
    second_half = heads[..., half:]
    return jnp.concatenate([first_half * cosine - second_half * sine, second_half * cosine + first_half * sine], axis=-1)

def angles(places, head_width):
    steps_half = jnp.arange(head_width // 2, dtype=jnp.float32)
    inverse = ROPE_BASE ** (-2.0 * steps_half / head_width)
    theta = places[:, None] * inverse[None, :]
    return (jnp.cos(theta), jnp.sin(theta))

def layout(lengths, places):
    ends = jnp.cumsum(lengths).astype(jnp.int32)
    starts = ends - lengths
    inside = (places[:, None] >= starts[None, :]) & (places[:, None] < ends[None, :])
    numbers = jnp.arange(1, lengths.shape[0] + 1, dtype=jnp.int32)
    document = lax.optimization_barrier(jnp.sum(jnp.where(inside, numbers[None, :], 0), axis=1)).astype(jnp.int32) - 1
    offset = places - lax.optimization_barrier(jnp.sum(jnp.where(inside, starts[None, :], 0), axis=1)).astype(jnp.int32)
    return (document, offset)

def window_block(pieces):
    queries, keys, values, doc_query, place_query, doc_key, place_key = pieces
    scores = low_back(jnp.einsum('qhd,kd->hqk', queries, keys, precision=HIGHEST))
    distance = place_query[:, None] - place_key[None, :]
    allowed = (doc_query[:, None] == doc_key[None, :]) & (distance >= 0) & (distance < WINDOW)
    probs = low(jax.nn.softmax(jnp.where(allowed[None], scores, MASKED), axis=-1))
    return jnp.einsum('hqk,kd->qhd', probs, values, precision=HIGHEST)

def windows(padded, block_count, reach):
    blocked = padded.reshape((block_count + reach, padded.shape[0] // (block_count + reach)) + padded.shape[1:])
    return jnp.concatenate([blocked[shift_at:shift_at + block_count] for shift_at in range(reach + 1)], axis=1)

def reference(tokens, cotangent, arrival_order, lengths, norm_gain, w_query, w_kv, w_out, ffn_gain, w_gate_up, w_down):
    groups = tokens.shape[0]
    total_rows = groups * TOKENS
    reach = WINDOW // TOK_DEV
    block_count = total_rows // TOK_DEV
    places = jnp.arange(TOKENS, dtype=jnp.int32)
    documents, offsets = jax.vmap(lambda single: layout(single, places))(lengths)
    documents = (documents + SEQS * jnp.arange(groups, dtype=jnp.int32)[:, None]).astype(jnp.int32).reshape(total_rows)
    offsets = offsets.astype(jnp.int32).reshape(total_rows)
    targets = (arrival_order + TOKENS * jnp.arange(groups, dtype=jnp.int32)[:, None]).astype(jnp.int32).reshape(total_rows)
    cosine, sine = angles(offsets.astype(jnp.float32), HD)
    doc_keys = windows(jnp.concatenate([jnp.full((WINDOW,), -1, jnp.int32), documents]), block_count, reach)
    place_keys = windows(jnp.concatenate([jnp.zeros((WINDOW,), jnp.int32), offsets]), block_count, reach)
    doc_queries = documents.reshape(block_count, TOK_DEV)
    place_queries = offsets.reshape(block_count, TOK_DEV)

    def forward(arrived, gain_attn, query_w, kv_w, out_w, gain_ffn, gate_up_w, down_w):
        packed = jnp.zeros((total_rows, D), jnp.float32).at[targets].set(arrived)
        normed = low(rms_scale(packed, gain_attn))
        query_lin = low_back(jnp.dot(normed, query_w, precision=HIGHEST))
        kv_lin = low_back(jnp.dot(normed, kv_w, precision=HIGHEST))
        queries = low(rotate(query_lin.reshape(total_rows, H, HD), cosine[:, None, :], sine[:, None, :]) * HD ** (-0.5))
        keys = low(rotate(kv_lin[:, :HD], cosine, sine))
        values = low(kv_lin[:, HD:])
        zero_rows = jnp.zeros((WINDOW, HD), jnp.float32)
        key_win = windows(jnp.concatenate([zero_rows, keys]), block_count, reach)
        value_win = windows(jnp.concatenate([zero_rows, values]), block_count, reach)
        attended = lax.map(jax.checkpoint(window_block), (queries.reshape(block_count, TOK_DEV, H, HD), key_win, value_win, doc_queries, place_queries, doc_keys, place_keys))
        mixed = low_back(low(attended.reshape(total_rows, D)))
        branch = low_back(jnp.dot(mixed, out_w, precision=HIGHEST))
        hidden_state = packed + branch
        ffn_in = low(rms_scale(hidden_state, gain_ffn))
        gate_up = low_back(jnp.dot(ffn_in, gate_up_w, precision=HIGHEST))
        activated = low(jax.nn.gelu(gate_up[:, :FF], approximate=True) * gate_up[:, FF:])
        ffn_out = low_back(jnp.dot(activated, down_w, precision=HIGHEST))
        return (hidden_state + ffn_out)[targets]
    floats = tuple((argument.astype(jnp.float32) for argument in (tokens.reshape(total_rows, D), norm_gain, w_query, w_kv, w_out, ffn_gain, w_gate_up, w_down)))
    outputs, pull = jax.vjp(forward, *floats)
    grads = pull(cotangent.reshape(total_rows, D).astype(jnp.float32))
    return (outputs.astype(jnp.bfloat16).reshape(groups, TOKENS, D), grads[0].astype(jnp.bfloat16).reshape(groups, TOKENS, D), grads[1], grads[2], grads[3], grads[4], grads[5], grads[6], grads[7])
```

```python
import jax
import jax.numpy as jnp
from jax import lax
from jax.sharding import PartitionSpec as P

HD = 192
FF = 4608
WINDOW = 1024


EPSILON = 1e-06
ROPE_BASE = 10000.0
MASKED = -1e30


def passed_along(x, axis, by):
    length = lax.axis_size(axis)
    pairs = [(i, i + by) for i in range(length) if 0 <= i + by < length]
    return lax.ppermute(x, axis, pairs)


def rms_scale(values, gain):
    return values * lax.rsqrt(jnp.mean(values * values, axis=-1, keepdims=True) + EPSILON) * gain


def rotate(heads, cosine, sine):
    half = heads.shape[-1] // 2
    first_half = heads[..., :half]
    second_half = heads[..., half:]
    return jnp.concatenate(
        [first_half * cosine - second_half * sine, second_half * cosine + first_half * sine],
        axis=-1,
    )


def unrotate(heads, cosine, sine):
    half = heads.shape[-1] // 2
    first_half = heads[..., :half]
    second_half = heads[..., half:]
    return jnp.concatenate(
        [first_half * cosine + second_half * sine, second_half * cosine - first_half * sine],
        axis=-1,
    )


def angles(places, head_width):
    steps_half = jnp.arange(head_width // 2, dtype=jnp.float32)
    inverse = ROPE_BASE ** (-2.0 * steps_half / head_width)
    theta = places[:, None] * inverse[None, :]
    return (jnp.cos(theta), jnp.sin(theta))


def layout(lengths, places):
    ends = jnp.cumsum(lengths)
    starts = ends - lengths
    inside = (places[:, None] >= starts[None, :]) & (places[:, None] < ends[None, :])
    numbers = jnp.arange(1, lengths.shape[0] + 1, dtype=jnp.int32)
    document = jnp.sum(jnp.where(inside, numbers[None, :], 0), axis=1) - 1
    offset = places - jnp.sum(jnp.where(inside, starts[None, :], 0), axis=1)
    return (document, offset)


def gelu_product(gate_up):
    return jax.nn.gelu(gate_up[:, :FF], approximate=True) * gate_up[:, FF:]


def body(
    tokens,
    cotangent,
    arrival_order,
    lengths,
    norm_gain,
    w_query,
    w_kv,
    w_out,
    ffn_gain,
    w_gate_up,
    w_down,
):
    row_count = tokens.shape[1]
    model_width = tokens.shape[2]
    head_count = model_width // HD
    ranks = lax.axis_size("seq")
    capacity = 2 * row_count // ranks
    reach = WINDOW // row_count
    position = lax.axis_index("seq")
    arrived_at = arrival_order[0]
    owner = arrived_at // row_count
    owner_hits = (owner[:, None] == jnp.arange(ranks, dtype=jnp.int32)[None, :]).astype(jnp.int32)
    within = jnp.sum(jnp.cumsum(owner_hits, axis=0) * owner_hits, axis=1) - 1
    send_slot = owner * capacity + within

    def to_slots(source_rows):
        return (
            jnp.zeros((ranks * capacity, model_width), source_rows.dtype)
            .at[send_slot]
            .set(source_rows)
            .reshape(ranks, capacity, model_width)
        )

    slot_place = (
        jnp.full((ranks * capacity,), -1, jnp.int32)
        .at[send_slot]
        .set(arrived_at % row_count)
        .reshape(ranks, capacity)
    )
    got_tokens, got_cotangent, got_place = (
        lax.all_to_all(to_slots(tokens[0]), "seq", split_axis=0, concat_axis=0, tiled=True),
        lax.all_to_all(to_slots(cotangent[0]), "seq", split_axis=0, concat_axis=0, tiled=True),
        lax.all_to_all(slot_place, "seq", split_axis=0, concat_axis=0, tiled=True),
    )
    recv_place = got_place.reshape(ranks * capacity)
    is_live = recv_place >= 0
    landing = jnp.where(is_live, recv_place, row_count)
    safe_place = jnp.where(is_live, recv_place, 0)

    def from_slots(slot_rows):
        return (
            jnp.zeros((row_count, model_width), slot_rows.dtype)
            .at[landing]
            .set(slot_rows.reshape(ranks * capacity, model_width), mode="drop")
        )

    def to_owner(local_rows):
        return jnp.where(
            is_live[:, None], local_rows[safe_place], jnp.zeros((), local_rows.dtype)
        ).reshape(ranks, capacity, model_width)

    packed = from_slots(got_tokens)
    packed_grad = from_slots(got_cotangent)
    def whole(shard):
        part = shard.shape[0] // ranks
        mine = lax.dynamic_slice_in_dim(shard, position * part, part, axis=0)
        return lax.all_gather(mine, ("fsdp", "seq"), axis=0, tiled=True)

    def shared(grad):
        mine = lax.psum_scatter(
            grad.astype(jnp.bfloat16), ("fsdp", "seq"), scatter_dimension=0, tiled=True
        )
        return lax.all_gather(mine, "seq", axis=0, tiled=True).astype(jnp.float32)

    query_w, kv_w, out_w, gate_up_w, down_w = (
        whole(w_query),
        whole(w_kv),
        whole(w_out),
        whole(w_gate_up),
        whole(w_down),
    )
    gain_attn, gain_ffn = (
        lax.all_gather(norm_gain, "fsdp", axis=0, tiled=True),
        lax.all_gather(ffn_gain, "fsdp", axis=0, tiled=True),
    )
    places = position * row_count + jnp.arange(row_count, dtype=jnp.int32)
    doc_query, offset_query = layout(lengths[0], places)
    key_places = (
        position * row_count
        - reach * row_count
        + jnp.arange((reach + 1) * row_count, dtype=jnp.int32)
    )
    doc_key, unused_offset = layout(lengths[0], key_places)
    gap = places[:, None] - key_places[None, :]
    allowed = (
        (doc_query[:, None] == doc_key[None, :])
        & (doc_key[None, :] >= 0)
        & (gap >= 0)
        & (gap < WINDOW)
    )
    cosine, sine = angles(offset_query.astype(jnp.float32), HD)
    packed_f = packed.astype(jnp.float32)
    normed = rms_scale(packed_f, gain_attn.astype(jnp.float32)).astype(jnp.bfloat16)
    query_lin = jnp.dot(normed, query_w, preferred_element_type=jnp.float32)
    kv_lin = jnp.dot(normed, kv_w, preferred_element_type=jnp.float32)
    queries = (
        rotate(query_lin.reshape(row_count, head_count, HD), cosine[:, None, :], sine[:, None, :])
        * HD ** (-0.5)
    ).astype(jnp.bfloat16)
    own_keys = rotate(kv_lin[:, :HD], cosine, sine).astype(jnp.bfloat16)
    own_values = kv_lin[:, HD:].astype(jnp.bfloat16)
    own_pair = jnp.concatenate([own_keys, own_values], axis=1)
    earlier = []
    for distance in range(reach, 0, -1):
        earlier.append(passed_along(own_pair, "seq", distance))
    pair_rows = jnp.concatenate(earlier + [own_pair], axis=0)
    keys_all = pair_rows[:, :HD]
    values_all = pair_rows[:, HD:]

    def masked_scores():
        raw = jnp.einsum("qhd,kd->hqk", queries, keys_all, preferred_element_type=jnp.float32)
        return jnp.where(allowed[None], raw, MASKED)

    scores = masked_scores()
    top_score = jnp.max(scores, axis=-1, keepdims=True)
    log_total = top_score + jnp.log(jnp.sum(jnp.exp(scores - top_score), axis=-1, keepdims=True))
    probs_low = jnp.exp(scores - log_total).astype(jnp.bfloat16)
    mixed = (
        jnp.einsum("hqk,kd->qhd", probs_low, values_all, preferred_element_type=jnp.float32)
        .reshape(row_count, model_width)
        .astype(jnp.bfloat16)
    )
    hidden_state = packed_f + jnp.dot(mixed, out_w, preferred_element_type=jnp.float32)
    ffn_in = rms_scale(hidden_state, gain_ffn.astype(jnp.float32)).astype(jnp.bfloat16)
    gate_up = jnp.dot(ffn_in, gate_up_w, preferred_element_type=jnp.float32)
    activated = gelu_product(gate_up).astype(jnp.bfloat16)
    block_rows = (
        hidden_state + jnp.dot(activated, down_w, preferred_element_type=jnp.float32)
    ).astype(jnp.bfloat16)
    grad_down = jnp.einsum("tf,td->fd", activated, packed_grad, preferred_element_type=jnp.float32)
    d_activated = jnp.einsum("td,fd->tf", packed_grad, down_w, preferred_element_type=jnp.float32)
    unused_product, glu_pull = jax.vjp(gelu_product, gate_up)
    d_gate_up = glu_pull(d_activated)[0].astype(jnp.bfloat16)
    grad_gate_up = jnp.einsum("td,tf->df", ffn_in, d_gate_up, preferred_element_type=jnp.float32)
    d_ffn_in = jnp.einsum("tf,df->td", d_gate_up, gate_up_w, preferred_element_type=jnp.float32)
    unused_scaled, ffn_norm_pull = jax.vjp(rms_scale, hidden_state, gain_ffn.astype(jnp.float32))
    d_hidden_norm, grad_gain_ffn = ffn_norm_pull(d_ffn_in)
    d_hidden = packed_grad.astype(jnp.float32) + d_hidden_norm
    d_branch = d_hidden.astype(jnp.bfloat16)
    grad_out = jnp.einsum("te,td->ed", mixed, d_branch, preferred_element_type=jnp.float32)
    d_mixed = (
        jnp.einsum("td,ed->te", d_branch, out_w, preferred_element_type=jnp.float32)
        .astype(jnp.bfloat16)
        .reshape(row_count, head_count, HD)
    )
    probs = jnp.exp(masked_scores() - log_total)
    d_probs = jnp.einsum("qhd,kd->hqk", d_mixed, values_all, preferred_element_type=jnp.float32)
    weighted = jnp.sum(probs * d_probs, axis=-1, keepdims=True)
    d_scores = (probs * (d_probs - weighted)).astype(jnp.bfloat16)
    d_queries = jnp.einsum("hqk,kd->qhd", d_scores, keys_all, preferred_element_type=jnp.float32)
    d_keys = jnp.einsum("hqk,qhd->kd", d_scores, queries, preferred_element_type=jnp.float32)
    d_values = jnp.einsum(
        "hqk,qhd->kd", probs.astype(jnp.bfloat16), d_mixed, preferred_element_type=jnp.float32
    )
    d_pairs = jnp.concatenate([d_keys, d_values], axis=1)
    d_own = d_pairs[reach * row_count :]
    for distance in range(reach, 0, -1):
        start_row = (reach - distance) * row_count
        d_own = d_own + passed_along(
            d_pairs[start_row : start_row + row_count].astype(jnp.bfloat16), "seq", -distance
        ).astype(jnp.float32)
    d_kv_lin = jnp.concatenate(
        [unrotate(d_own[:, :HD], cosine, sine), d_own[:, HD:]], axis=1
    ).astype(jnp.bfloat16)
    d_query_lin = (
        (unrotate(d_queries, cosine[:, None, :], sine[:, None, :]) * HD ** (-0.5))
        .reshape(row_count, model_width)
        .astype(jnp.bfloat16)
    )
    grad_query = jnp.einsum("te,tf->ef", normed, d_query_lin, preferred_element_type=jnp.float32)
    grad_kv = jnp.einsum("te,tf->ef", normed, d_kv_lin, preferred_element_type=jnp.float32)
    d_normed = jnp.einsum(
        "tf,ef->te", d_query_lin, query_w, preferred_element_type=jnp.float32
    ) + jnp.einsum("tf,ef->te", d_kv_lin, kv_w, preferred_element_type=jnp.float32)
    unused_normed, attn_norm_pull = jax.vjp(rms_scale, packed_f, gain_attn.astype(jnp.float32))
    d_packed_norm, grad_gain_attn = attn_norm_pull(d_normed)
    grad_rows = (d_hidden + d_packed_norm).astype(jnp.bfloat16)
    home_out, home_grad = (
        lax.all_to_all(to_owner(block_rows), "seq", split_axis=0, concat_axis=0, tiled=True),
        lax.all_to_all(to_owner(grad_rows), "seq", split_axis=0, concat_axis=0, tiled=True),
    )
    block_arrived = home_out.reshape(ranks * capacity, model_width)[send_slot]
    grad_arrived = home_grad.reshape(ranks * capacity, model_width)[send_slot]
    total_query, total_kv, total_out, total_gate_up, total_down = (
        shared(grad_query),
        shared(grad_kv),
        shared(grad_out),
        shared(grad_gate_up),
        shared(grad_down),
    )
    total_gain_attn, total_gain_ffn = (
        lax.psum(
            lax.psum_scatter(gain, "fsdp", scatter_dimension=0, tiled=True), "seq"
        )
        for gain in (grad_gain_attn, grad_gain_ffn)
    )
    return (
        block_arrived[None],
        grad_arrived[None],
        total_gain_attn,
        total_query,
        total_kv,
        total_out,
        total_gain_ffn,
        total_gate_up,
        total_down,
    )


def solution(mesh):
    placed = (
        P("fsdp", "seq", None),
        P("fsdp", "seq", None),
        P("fsdp", "seq"),
        P("fsdp", None),
        P("fsdp"),
        P("fsdp", None),
        P("fsdp", None),
        P("fsdp", None),
        P("fsdp"),
        P("fsdp", None),
        P("fsdp", None),
    )
    return jax.shard_map(
        body,
        mesh=mesh,
        in_specs=placed,
        out_specs=(
            P("fsdp", "seq", None),
            P("fsdp", "seq", None),
            P("fsdp"),
            P("fsdp", None),
            P("fsdp", None),
            P("fsdp", None),
            P("fsdp"),
            P("fsdp", None),
            P("fsdp", None),
        ),
        check_vma=False,
    )
```

```python
import jax
import jax.numpy as jnp
from jax import lax
from jax.experimental import pallas as pl
from jax.experimental.pallas import tpu as pltpu
from jax.sharding import PartitionSpec as P

HD = 192
FF = 4608
WINDOW = 1024


EPSILON = 1e-06
ROPE_BASE = 10000.0
MASKED = -1e30


def passed_along(x, axis, by):
    length = lax.axis_size(axis)
    pairs = [(i, i + by) for i in range(length) if 0 <= i + by < length]
    return lax.ppermute(x, axis, pairs)


def rms_scale(values, gain):
    return values * lax.rsqrt(jnp.mean(values * values, axis=-1, keepdims=True) + EPSILON) * gain


def rotate(heads, cosine, sine):
    half = heads.shape[-1] // 2
    first_half = heads[..., :half]
    second_half = heads[..., half:]
    return jnp.concatenate(
        [first_half * cosine - second_half * sine, second_half * cosine + first_half * sine],
        axis=-1,
    )


def unrotate(heads, cosine, sine):
    half = heads.shape[-1] // 2
    first_half = heads[..., :half]
    second_half = heads[..., half:]
    return jnp.concatenate(
        [first_half * cosine + second_half * sine, second_half * cosine - first_half * sine],
        axis=-1,
    )


def angles(places, head_width):
    steps_half = jnp.arange(head_width // 2, dtype=jnp.float32)
    inverse = ROPE_BASE ** (-2.0 * steps_half / head_width)
    theta = places[:, None] * inverse[None, :]
    return (jnp.cos(theta), jnp.sin(theta))


def layout(lengths, places):
    ends = jnp.cumsum(lengths)
    starts = ends - lengths
    inside = (places[:, None] >= starts[None, :]) & (places[:, None] < ends[None, :])
    numbers = jnp.arange(1, lengths.shape[0] + 1, dtype=jnp.int32)
    document = jnp.sum(jnp.where(inside, numbers[None, :], 0), axis=1) - 1
    offset = places - jnp.sum(jnp.where(inside, starts[None, :], 0), axis=1)
    return (document, offset)


def after(x, *done):
    return lax.optimization_barrier((x, *done))[0]


def after_all(xs, *done):
    return lax.optimization_barrier((*xs, *done))[: len(xs)]


def rounded(x):
    return x.astype(jnp.bfloat16)


def widened(x):
    return x.astype(jnp.float32)


def added(*terms):
    return rounded(sum(widened(term) for term in terms))


def dot(a, b):
    return jnp.dot(a, b, preferred_element_type=jnp.float32)


def dot_rows(a, b):
    return jnp.einsum("td,tf->df", a, b, preferred_element_type=jnp.float32)


def dot_across(a, b):
    return jnp.einsum("tf,df->td", a, b, preferred_element_type=jnp.float32)


def turn(x, tables, back):
    width = x.shape[-1]
    half = HD // 2
    later = pltpu.roll(x, width - half, axis=1)
    sooner = pltpu.roll(x, half, axis=1)
    turned = later * tables[1] + sooner * tables[2]
    return x * tables[0] - turned if back else x * tables[0] + turned


def tables_of(cosine, sine, heads, still):
    none = jnp.zeros_like(sine)
    ones = jnp.ones_like(sine)
    return (
        jnp.concatenate([cosine, cosine] * heads + [ones, ones] * still, axis=1),
        jnp.concatenate([-sine, none] * heads + [none, none] * still, axis=1),
        jnp.concatenate([none, sine] * heads + [none, none] * still, axis=1),
    )


def no_entry(doc_query, doc_key, rows, keys):
    key = lax.broadcasted_iota(jnp.int32, (keys, rows), 0)
    row = lax.broadcasted_iota(jnp.int32, (keys, rows), 1)
    gap = WINDOW + row - key
    seen = (doc_key == doc_query) & (doc_key >= 0) & (gap >= 0) & (gap < WINDOW)
    return jnp.where(seen, 0.0, MASKED)


def dot_last(a, b):
    return lax.dot_general(a, b, (((1,), (1,)), ((), ())), preferred_element_type=jnp.float32)


def attend(query_lin, tables, pairs, pairs_across, doc_query, doc_key):
    rows, width = query_lin.shape
    block = 256
    keys = WINDOW + block
    couples = width // (2 * HD)

    def kernel(q_ref, t0, t1, t2, pairs_ref, across_ref, dq_ref, dk_ref, turned_ref, mixed_ref, total_ref, bias):
        start = pl.multiple_of(pl.program_id(0) * block, block)
        window = pl.ds(start, keys)

        @pl.when(pl.program_id(1) == 0)
        def fill():
            bias[...] = no_entry(dq_ref[...], dk_ref[window, :], block, keys)

        queries = turn(q_ref[...], (t0[...], t1[...], t2[...]), False) * HD ** (-0.5)
        queries = queries.astype(jnp.bfloat16)
        turned_ref[...] = queries
        own_keys = pairs_ref[window, :][:, :HD]
        values = across_ref[pl.ds(HD, HD), window]
        mixed, totals = [], []
        for head in range(2):
            scores = dot_last(own_keys, queries[:, head * HD : (head + 1) * HD]) + bias[...]
            top = jnp.max(scores, axis=0, keepdims=True)
            weights = jnp.exp(scores - top)
            total = jnp.sum(weights, axis=0, keepdims=True)
            totals.append(top + jnp.log(total))
            mixed.append(dot(values, weights.astype(jnp.bfloat16)) * (1.0 / total))
        mixed_ref[...] = jnp.concatenate(mixed, axis=0).T.astype(jnp.bfloat16)
        total_ref[0] = jnp.concatenate(totals, axis=0)

    tile = pl.BlockSpec((block, 2 * HD), lambda i, j: (i, j))
    table = pl.BlockSpec((block, 2 * HD), lambda i, j: (i, 0))
    return pl.pallas_call(
        kernel,
        grid=(rows // block, couples),
        in_specs=[
            tile,
            table,
            table,
            table,
            pl.BlockSpec(pairs.shape, lambda i, j: (0, 0)),
            pl.BlockSpec(pairs_across.shape, lambda i, j: (0, 0)),
            pl.BlockSpec((1, block), lambda i, j: (0, i)),
            pl.BlockSpec(doc_key.shape, lambda i, j: (0, 0)),
        ],
        out_specs=[tile, tile, pl.BlockSpec((1, 2, block), lambda i, j: (j, 0, i))],
        out_shape=[
            jax.ShapeDtypeStruct((rows, width), jnp.bfloat16),
            jax.ShapeDtypeStruct((rows, width), jnp.bfloat16),
            jax.ShapeDtypeStruct((couples, 2, rows), jnp.float32),
        ],
        scratch_shapes=[pltpu.VMEM((keys, block), jnp.float32)],
        compiler_params=pltpu.CompilerParams(vmem_limit_bytes=48 * 2**20),
        cost_estimate=pl.CostEstimate(
            flops=2 * 2 * rows * couples * 2 * keys * HD, bytes_accessed=12 * 2**20, transcendentals=rows * couples * 2 * keys
        ),
    )(query_lin, *tables, pairs, pairs_across, doc_query, doc_key)


def attend_back(queries, d_mixed, totals, tables, pairs, pairs_across, doc_query, doc_key):
    rows, width = queries.shape
    block = 256
    keys = WINDOW + block
    couples = width // (2 * HD)
    last = (rows // block - 1, couples - 1)

    def kernel(q_ref, do_ref, total_ref, t0, t1, t2, pairs_ref, across_ref, dq_ref, dk_ref, d_lin_ref, d_pairs_ref, bias, d_keys, d_values, values):
        start = pl.multiple_of(pl.program_id(0) * block, block)
        window = pl.ds(start, keys)

        @pl.when((pl.program_id(0) == 0) & (pl.program_id(1) == 0))
        def clear():
            d_keys[...] = jnp.zeros_like(d_keys)
            d_values[...] = jnp.zeros_like(d_values)
            values[...] = pairs_ref[...][:, HD:]

        @pl.when(pl.program_id(1) == 0)
        def fill():
            bias[...] = no_entry(dq_ref[...], dk_ref[window, :], block, keys)

        own_keys = pairs_ref[window, :][:, :HD]
        own_values = values[window, :]
        keys_across = across_ref[pl.ds(0, HD), window]
        d_turned = []
        for head in range(2):
            part = slice(head * HD, (head + 1) * HD)
            q, do = q_ref[...][:, part], do_ref[...][:, part]
            scores = dot_last(own_keys, q) + bias[...]
            probs = jnp.exp(scores - total_ref[0][head : head + 1, :])
            d_probs = dot_last(own_values, do)
            product = probs * d_probs
            weighted = jnp.sum(product, axis=0, keepdims=True)
            d_scores = (product - probs * weighted).astype(jnp.bfloat16)
            d_turned.append(dot(keys_across, d_scores))
            d_keys[window, :] += dot(d_scores, q)
            d_values[window, :] += dot(probs.astype(jnp.bfloat16), do)
        d_turned = jnp.concatenate(d_turned, axis=0).T
        d_lin = turn(d_turned, (t0[...], t1[...], t2[...]), True) * HD ** (-0.5)
        d_lin_ref[...] = d_lin.astype(jnp.bfloat16)

        @pl.when((pl.program_id(0) == last[0]) & (pl.program_id(1) == last[1]))
        def finish():
            d_pairs_ref[...] = jnp.concatenate([d_keys[...], d_values[...]], axis=1)

    tile = pl.BlockSpec((block, 2 * HD), lambda i, j: (i, j))
    table = pl.BlockSpec((block, 2 * HD), lambda i, j: (i, 0))
    return pl.pallas_call(
        kernel,
        grid=(rows // block, couples),
        in_specs=[
            tile,
            tile,
            pl.BlockSpec((1, 2, block), lambda i, j: (j, 0, i)),
            table,
            table,
            table,
            pl.BlockSpec(pairs.shape, lambda i, j: (0, 0)),
            pl.BlockSpec(pairs_across.shape, lambda i, j: (0, 0)),
            pl.BlockSpec((1, block), lambda i, j: (0, i)),
            pl.BlockSpec(doc_key.shape, lambda i, j: (0, 0)),
        ],
        out_specs=[tile, pl.BlockSpec(pairs.shape, lambda i, j: (0, 0))],
        out_shape=[
            jax.ShapeDtypeStruct((rows, width), jnp.bfloat16),
            jax.ShapeDtypeStruct(pairs.shape, jnp.float32),
        ],
        scratch_shapes=[
            pltpu.VMEM((keys, block), jnp.float32),
            pltpu.VMEM((pairs.shape[0], HD), jnp.float32),
            pltpu.VMEM((pairs.shape[0], HD), jnp.float32),
            pltpu.VMEM((pairs.shape[0], HD), jnp.bfloat16),
        ],
        compiler_params=pltpu.CompilerParams(vmem_limit_bytes=48 * 2**20),
        cost_estimate=pl.CostEstimate(
            flops=5 * 2 * rows * couples * 2 * keys * HD, bytes_accessed=12 * 2**20, transcendentals=rows * couples * 2 * keys
        ),
    )(queries, d_mixed, totals, *tables, pairs, pairs_across, doc_query, doc_key)


def put_pieces(pieces, positions, shards):
    count = len(pieces)
    others, rows, unused_width = pieces[0].shape
    depth = others + 1
    widths = [shard.shape[2] for shard in shards]

    def kernel(positions_ref, *refs):
        i, j = pl.program_id(0), pl.program_id(1)
        sources, locals_, targets = (
            refs[:count],
            refs[count : count + len(shards)],
            refs[count + len(shards) :],
        )
        for at in range(count):

            @pl.when((i == at) & (j < others))
            def take():
                start = 0
                for target, width in zip(targets, widths):
                    target[0, 0] = sources[at][j, :, pl.ds(start, width)]
                    start += width

        @pl.when(j == others)
        def keep():
            for target, source in zip(targets, locals_):
                target[0, 0] = source[0]

    return pl.pallas_call(
        kernel,
        out_shape=[
            jax.ShapeDtypeStruct((depth, count, rows, width), pieces[0].dtype) for width in widths
        ],
        grid_spec=pltpu.PrefetchScalarGridSpec(
            num_scalar_prefetch=1,
            grid=(count, depth),
            in_specs=[pl.BlockSpec(p.shape, lambda i, j, at: (0, 0, 0)) for p in pieces]
            + [pl.BlockSpec((1, rows, width), lambda i, j, at: (at[i], 0, 0)) for width in widths],
            out_specs=[
                pl.BlockSpec(
                    (1, 1, rows, width),
                    lambda i, j, at: (at[count + j], at[i], 0, 0),
                )
                for width in widths
            ],
        ),
        compiler_params=pltpu.CompilerParams(vmem_limit_bytes=40 * 2**20),
    )(positions, *pieces, *shards)


def rest(x, level):
    depth = x.shape[0]
    block = (1,) + x.shape[1:]
    zeros = (0,) * (x.ndim - 1)

    def kernel(level_ref, source, target):
        target[...] = source[...]

    return pl.pallas_call(
        kernel,
        out_shape=jax.ShapeDtypeStruct((depth - 1,) + x.shape[1:], x.dtype),
        grid_spec=pltpu.PrefetchScalarGridSpec(
            num_scalar_prefetch=1,
            grid=(depth - 1,),
            in_specs=[
                pl.BlockSpec(block, lambda i, at: (lax.rem(at[0] + i + 1, depth), *zeros))
            ],
            out_specs=pl.BlockSpec(block, lambda i, at: (i, *zeros)),
        ),
    )(level[None], x)


def spread(pieces, positions, shape, place):
    count = len(pieces)
    rows, width = pieces[0].shape

    def kernel(positions_ref, *refs):
        for at in range(count):

            @pl.when(pl.program_id(0) == at)
            def take():
                refs[-1][...] = refs[at][...].astype(jnp.float32)

    return pl.pallas_call(
        kernel,
        out_shape=jax.ShapeDtypeStruct(shape, jnp.float32),
        grid_spec=pltpu.PrefetchScalarGridSpec(
            num_scalar_prefetch=1,
            grid=(count,),
            in_specs=[pl.BlockSpec((rows, width), lambda i, at: (0, 0))] * count,
            out_specs=pl.BlockSpec((rows, width), lambda i, at: place(at[i])),
        ),
        compiler_params=pltpu.CompilerParams(vmem_limit_bytes=40 * 2**20),
    )(positions, *pieces)


GELU_SCALE = 0.7978845608028654
GELU_CUBE = 0.044715


def dot_first(a, b):
    return lax.dot_general(a, b, (((0,), (0,)), ((), ())), preferred_element_type=jnp.float32)


def feed(facts, x, grad, first_w, second_w, shard, down_pieces, down_shard, block_sum, back_sum, terms):
    rows, width = x.shape
    hidden = first_w.shape[1]
    half = hidden // 2
    column = width // 4
    depth = down_pieces[0].shape[0] + 1
    level_rows = width // depth
    full = depth * hidden
    started = back_sum is not None
    pieces = 8
    f32, bf16 = jnp.float32, jnp.bfloat16

    def kernel(facts_ref, x_ref, g_ref, *refs):
        wa_in, wb_in, shard_in, down_in, block_in = refs[:5]
        down_pieces_in = refs[5 : 5 + pieces]
        refs = refs[5 + pieces :]
        if started:
            back_in = refs[0]
            refs = refs[1 + pieces :]
        block_out, back_out, ga_out, gb_out = refs[:4]
        term_out = refs[4 : 4 + pieces]
        wa, wb, wd, a, b, d, act, da, db, block, back, ga, gb, gd, sems = refs[4 + pieces :]
        chip = facts_ref[1]
        core, level = facts_ref[2], facts_ref[7]

        def rows_of(source, target, side, sem):
            copies = []
            for i in range(1, depth):
                place = pl.multiple_of(lax.rem(level + i, depth) * level_rows, 16)
                copies.append(
                    pltpu.make_async_copy(
                        source.at[pl.ds((i - 1) * level_rows, level_rows)],
                        target.at[pl.ds(place, level_rows)],
                        sem,
                    )
                )
            place = pl.multiple_of(level * level_rows, 16)
            start = pl.multiple_of(side * full + chip * hidden, 128)
            copies.append(
                pltpu.make_async_copy(
                    shard_in.at[:, pl.ds(start, hidden)],
                    target.at[pl.ds(place, level_rows)],
                    sem,
                )
            )
            return copies

        for copy in rows_of(wa_in, wa, core, sems.at[0]):
            copy.start()
        for copy in rows_of(wb_in, wb, 1 - core, sems.at[1]):
            copy.start()

        @pl.when(chip == level)
        def here():
            pltpu.make_async_copy(down_in, wd, sems.at[2]).start()

        @pl.when(chip != level)
        def elsewhere():
            step = lax.rem(chip - level + depth - 1, depth)
            for i in range(pieces):
                side = jnp.where(i < 4, core, 1 - core)
                pltpu.make_async_copy(
                    down_pieces_in[i].at[step],
                    wd.at[
                        pl.ds(pl.multiple_of(side * half, 16), half),
                        pl.ds(pl.multiple_of(facts_ref[3 + i % 4] * column, 128), column),
                    ],
                    sems.at[2],
                ).start()

        load_block = pltpu.make_async_copy(block_in, block, sems.at[3])
        load_block.start()
        if started:
            load_back = pltpu.make_async_copy(back_in, back, sems.at[4])
            load_back.start()
        pltpu.make_async_copy(wa, wa, sems.at[0]).wait()
        a[...] = dot(x_ref[...], wa[...])
        pltpu.make_async_copy(wb, wb, sems.at[1]).wait()
        b[...] = dot(x_ref[...], wb[...])
        pltpu.make_async_copy(wd, wd, sems.at[2]).wait()
        d[...] = dot_last(g_ref[...], wd[...])
        swapped = facts_ref[0] == 1

        @pl.loop(0, rows // 16)
        def glu(i):
            part = pl.ds(pl.multiple_of(i * 16, 16), 16)
            for j in range(hidden // 384):
                lanes = slice(j * 384, (j + 1) * 384)
                one, two, slope = a[part, lanes], b[part, lanes], d[part, lanes]
                gate = jnp.where(swapped, two, one)
                up = jnp.where(swapped, one, two)
                square = gate * gate
                inner = gate * (square * (GELU_SCALE * GELU_CUBE) + GELU_SCALE)
                share = 0.5 * jnp.tanh(inner) + 0.5
                gelu = gate * share
                bend = square * (6.0 * GELU_SCALE * GELU_CUBE) + 2.0 * GELU_SCALE
                rise = share + gelu * (1.0 - share) * bend
                d_gate = (slope * up) * rise
                d_up = slope * gelu
                act[part, lanes] = (gelu * up).astype(bf16)
                da[part, lanes] = jnp.where(swapped, d_up, d_gate).astype(bf16)
                db[part, lanes] = jnp.where(swapped, d_gate, d_up).astype(bf16)

        for i in range(width // 384):
            part = pl.ds(i * 384, 384)
            gb[part, :] = dot_first(x_ref[:, i * 384 : (i + 1) * 384], db[...]).astype(bf16)
            pltpu.make_async_copy(gb.at[part], gb_out.at[part], sems.at[5]).start()
        for i in range(width // 384):
            part = pl.ds(i * 384, 384)
            ga[part, :] = dot_first(x_ref[:, i * 384 : (i + 1) * 384], da[...]).astype(bf16)
            pltpu.make_async_copy(ga.at[part], ga_out.at[part], sems.at[6]).start()
        for i in range(hidden // 384):
            part = pl.ds(i * 384, 384)
            gd[part, :] = dot_first(act[:, i * 384 : (i + 1) * 384], g_ref[...]).astype(bf16)
        stores = []
        for i in range(pieces):
            side = jnp.where(i < 4, core, 1 - core)
            stores.append(
                pltpu.make_async_copy(
                    gd.at[
                        pl.ds(pl.multiple_of(side * half, 16), half),
                        pl.ds(pl.multiple_of(facts_ref[3 + i % 4] * column, 128), column),
                    ],
                    term_out[i].at[chip],
                    sems.at[7 + i],
                )
            )
        for store in stores:
            store.start()
        if started:
            load_back.wait()

            back[...] += dot_last(da[...], wa[...])
            back[...] += dot_last(db[...], wb[...])
        else:
            back[...] = dot_last(da[...], wa[...])
            back[...] += dot_last(db[...], wb[...])
        store_back = pltpu.make_async_copy(back, back_out, sems.at[15])
        store_back.start()
        load_block.wait()
        for i in range(2):
            part = pl.ds(i * (rows // 2), rows // 2)
            block[part, :] += dot(act[part, :], wd[...])
            pltpu.make_async_copy(block.at[part], block_out.at[part], sems.at[16]).start()
        for store in stores:
            store.wait()
        pltpu.make_async_copy(gb, gb_out, sems.at[5]).wait()
        pltpu.make_async_copy(ga, ga_out, sems.at[6]).wait()
        store_back.wait()
        pltpu.make_async_copy(block, block_out, sems.at[16]).wait()

    anywhere = pl.BlockSpec(memory_space=pl.ANY)
    inside = pl.BlockSpec(memory_space=pltpu.VMEM)
    operands = [facts, x, grad, first_w, second_w, shard, down_shard, block_sum, *down_pieces]
    aliases = {7: 0}
    if started:
        aliases[len(operands)] = 1
        operands.append(back_sum)
        for i, term in enumerate(terms):
            aliases[len(operands)] = 4 + i
            operands.append(term)
    sums = jax.ShapeDtypeStruct((rows, width), f32)
    grads = jax.ShapeDtypeStruct((width, hidden), bf16)
    results = pl.pallas_call(
        kernel,
        in_specs=[pl.BlockSpec(memory_space=pltpu.SMEM), inside, inside]
        + [anywhere] * (len(operands) - 3),
        out_specs=[anywhere] * (4 + pieces),
        out_shape=[sums, sums, grads, grads]
        + [jax.ShapeDtypeStruct((depth, half, column), bf16)] * pieces,
        input_output_aliases=aliases,
        scratch_shapes=[
            pltpu.VMEM((width, hidden), bf16),
            pltpu.VMEM((width, hidden), bf16),
            pltpu.VMEM((hidden, width), bf16),
            pltpu.VMEM((rows, hidden), f32),
            pltpu.VMEM((rows, hidden), f32),
            pltpu.VMEM((rows, hidden), f32),
            pltpu.VMEM((rows, hidden), bf16),
            pltpu.VMEM((rows, hidden), bf16),
            pltpu.VMEM((rows, hidden), bf16),
            pltpu.VMEM((rows, width), f32),
            pltpu.VMEM((rows, width), f32),
            pltpu.VMEM((width, hidden), bf16),
            pltpu.VMEM((width, hidden), bf16),
            pltpu.VMEM((hidden, width), bf16),
            pltpu.SemaphoreType.DMA((17,)),
        ],
        compiler_params=pltpu.CompilerParams(vmem_limit_bytes=56 * 2**20),
        cost_estimate=pl.CostEstimate(
            flops=9 * 2 * rows * width * hidden,
            bytes_accessed=40 * 2**20,
            transcendentals=rows * hidden,
        ),
    )(*operands)
    return results[0], results[1], results[2], results[3], results[4:]


class Plane:
    def __init__(self):
        self.me = lax.axis_index("seq")
        self.core = self.me % 2
        self.chip = self.me // 2
        first = jnp.where(self.core == 0, 1, 2)
        self.chips = [self.chip, self.chip ^ first, self.chip ^ (3 - first), self.chip ^ 3]
        self.first_pairs = [(i, i ^ (2 if i % 2 == 0 else 4)) for i in range(8)]
        self.second_pairs = [(i, i ^ (4 if i % 2 == 0 else 2)) for i in range(8)]
        self.core_pairs = [(i, i ^ 1) for i in range(8)]
        self.sources = jnp.stack(
            [chip * 2 + self.core for chip in self.chips]
            + [chip * 2 + 1 - self.core for chip in self.chips]
        )

    def first(self, x):
        return lax.ppermute(x, "seq", self.first_pairs)

    def second(self, x):
        return lax.ppermute(x, "seq", self.second_pairs)

    def along(self, x):
        depth = lax.axis_size("fsdp")
        return [
            lax.ppermute(x, "fsdp", [((i + k) % depth, i) for i in range(depth)])
            for k in range(1, depth)
        ]

    def swap(self, x):
        return lax.ppermute(x, "seq", self.core_pairs)

    def gather(self, piece):
        u = self.first(piece)
        v = self.second(piece)
        d = self.second(u)
        return [piece, u, v, d], [self.swap(piece), self.swap(v), self.swap(u), self.swap(d)]

    def merge(self, own, other):
        swaps = [self.swap(term) for term in other]
        from_d = self.second(added(own[3], swaps[3]))
        from_v = self.second(added(own[2], swaps[1]))
        from_u = self.first(added(own[1], swaps[2], from_d))
        return added(own[0], swaps[0], from_v, from_u)

    def down_columns(self, x):
        return lax.psum_scatter(x, "fsdp", scatter_dimension=0, tiled=True)


def places_of(arrival_order, ranks):
    row_count = arrival_order.shape[1]
    capacity = 2 * row_count // ranks
    arrived_at = arrival_order[0]
    owner = arrived_at // row_count
    owner_hits = (owner[:, None] == jnp.arange(ranks, dtype=jnp.int32)[None, :]).astype(jnp.int32)
    within = jnp.sum(jnp.cumsum(owner_hits, axis=0) * owner_hits, axis=1) - 1
    return owner * capacity + within, arrived_at % row_count


def to_slots(rows, slots, ranks, empty=0):
    capacity = 2 * rows.shape[0] // ranks
    out = jnp.full((ranks * capacity,) + rows.shape[1:], empty, rows.dtype)
    return out.at[slots].set(rows).reshape((ranks, capacity) + rows.shape[1:])


def from_slots(slots, landing):
    flat = slots.reshape((-1, slots.shape[-1]))
    out = jnp.zeros((flat.shape[0] // 2, flat.shape[1]), flat.dtype)
    return out.at[landing].set(flat, mode="drop")


def back_to_slots(rows, is_live, safe_place, ranks):
    chosen = jnp.where(is_live[:, None], rows[safe_place], jnp.zeros((), rows.dtype))
    return chosen.reshape(ranks, -1, rows.shape[1])


def exchange(x):
    return lax.all_to_all(x, "seq", split_axis=0, concat_axis=0, tiled=True)


def positions_of(lengths, row_count):
    position = lax.axis_index("seq")
    places = position * row_count + jnp.arange(row_count, dtype=jnp.int32)
    doc_query, offset_query = layout(lengths[0], places)
    key_places = (
        position * row_count - WINDOW + jnp.arange(WINDOW + row_count, dtype=jnp.int32)
    )
    doc_key, unused_offset = layout(lengths[0], key_places)
    cosine, sine = angles(offset_query.astype(jnp.float32), HD)
    return (doc_query[None, :], doc_key[:, None]), cosine, sine


def pair_of(kv_lin, cosine, sine):
    own_keys = rounded(rotate(kv_lin[:, :HD], cosine, sine))
    return jnp.concatenate([own_keys, rounded(kv_lin[:, HD:])], axis=1)


def with_earlier(pair, reach):
    return jnp.concatenate(
        [passed_along(pair, "seq", distance) for distance in range(reach, 0, -1)] + [pair], axis=0
    )


def owners_sum(d_pairs, row_count, reach):
    parts = [
        passed_along(
            rounded(d_pairs[(reach - distance) * row_count :][:row_count]), "seq", -distance
        )
        for distance in range(reach, 0, -1)
    ]
    own = d_pairs[reach * row_count :]
    for part in parts:
        own = own + widened(part)
    return own


def body(*operands):
    return square_body(*operands) if lax.axis_size("seq") == 8 else plain_body(*operands)


def plain_body(
    tokens,
    cotangent,
    arrival_order,
    lengths,
    norm_gain,
    w_query,
    w_kv,
    w_out,
    ffn_gain,
    w_gate_up,
    w_down,
):
    row_count = tokens.shape[1]
    ranks = lax.axis_size("seq")
    reach = WINDOW // row_count
    position = lax.axis_index("seq")

    def whole(shard):
        part = shard.shape[0] // ranks
        mine = lax.dynamic_slice_in_dim(shard, position * part, part, axis=0)
        return lax.all_gather(mine, ("fsdp", "seq"), axis=0, tiled=True)

    def summed(grad):
        mine = lax.psum_scatter(rounded(grad), ("fsdp", "seq"), scatter_dimension=0, tiled=True)
        return widened(lax.all_gather(mine, "seq", axis=0, tiled=True))

    send_slot, send_place = places_of(arrival_order, ranks)
    got_tokens = exchange(to_slots(tokens[0], send_slot, ranks))
    got_cotangent = exchange(to_slots(cotangent[0], send_slot, ranks))
    recv_place = exchange(to_slots(send_place, send_slot, ranks, -1)).reshape(-1)
    is_live = recv_place >= 0
    landing = jnp.where(is_live, recv_place, row_count)
    safe_place = jnp.where(is_live, recv_place, 0)
    packed_f = widened(from_slots(got_tokens, landing))
    packed_grad = from_slots(got_cotangent, landing)
    query_w, kv_w, out_w, down_w, gate_up_w = (
        whole(w_query),
        whole(w_kv),
        whole(w_out),
        whole(w_down),
        whole(w_gate_up),
    )
    gain_attn, gain_ffn = (
        widened(lax.all_gather(gain, "fsdp", axis=0, tiled=True)) for gain in (norm_gain, ffn_gain)
    )
    docs, cosine, sine = positions_of(lengths, row_count)
    tables = tables_of(cosine, sine, 2, 0)

    normed = rounded(rms_scale(packed_f, gain_attn))
    pair_rows = with_earlier(pair_of(dot(normed, kv_w), cosine, sine), reach)
    queries, mixed, totals = attend(dot(normed, query_w), tables, pair_rows, pair_rows.T, *docs)
    hidden_state = packed_f + dot(mixed, out_w)
    ffn_in = rounded(rms_scale(hidden_state, gain_ffn))
    gate, up = dot(ffn_in, gate_up_w[:, :FF]), dot(ffn_in, gate_up_w[:, FF:])
    activated, pull = jax.vjp(lambda g, u: jax.nn.gelu(g, approximate=True) * u, gate, up)
    activated = rounded(activated)
    block_rows = rounded(hidden_state + dot(activated, down_w))

    d_gate, d_up = pull(dot_across(packed_grad, down_w))
    d_gate_up = jnp.concatenate([rounded(d_gate), rounded(d_up)], axis=1)
    unused_scaled, ffn_norm_pull = jax.vjp(rms_scale, hidden_state, gain_ffn)
    d_hidden_norm, grad_gain_ffn = ffn_norm_pull(dot_across(d_gate_up, gate_up_w))
    d_hidden = widened(packed_grad) + d_hidden_norm
    d_branch = rounded(d_hidden)
    d_mixed = rounded(dot_across(d_branch, out_w))
    d_query_lin, d_pairs = attend_back(
        queries, d_mixed, totals, tables, pair_rows, pair_rows.T, *docs
    )
    d_own = owners_sum(d_pairs, row_count, reach)
    d_kv_lin = rounded(
        jnp.concatenate([unrotate(d_own[:, :HD], cosine, sine), d_own[:, HD:]], axis=1)
    )
    d_normed = dot_across(d_query_lin, query_w) + dot_across(d_kv_lin, kv_w)
    unused_normed, attn_norm_pull = jax.vjp(rms_scale, packed_f, gain_attn)
    d_packed_norm, grad_gain_attn = attn_norm_pull(d_normed)
    grad_rows = rounded(d_hidden + d_packed_norm)
    block_arrived, grad_arrived = (
        exchange(back_to_slots(rows, is_live, safe_place, ranks)).reshape(-1, rows.shape[1])[
            send_slot
        ]
        for rows in (block_rows, grad_rows)
    )
    total_gain_attn, total_gain_ffn = (
        lax.psum(lax.psum_scatter(gain, "fsdp", scatter_dimension=0, tiled=True), "seq")
        for gain in (grad_gain_attn, grad_gain_ffn)
    )
    return (
        block_arrived[None],
        grad_arrived[None],
        total_gain_attn,
        summed(dot_rows(normed, d_query_lin)),
        summed(dot_rows(normed, d_kv_lin)),
        summed(dot_rows(mixed, d_branch)),
        total_gain_ffn,
        summed(dot_rows(ffn_in, d_gate_up)),
        summed(dot_rows(activated, packed_grad)),
    )


def square_body(
    tokens,
    cotangent,
    arrival_order,
    lengths,
    norm_gain,
    w_query,
    w_kv,
    w_out,
    ffn_gain,
    w_gate_up,
    w_down,
):
    row_count = tokens.shape[1]
    model_width = tokens.shape[2]
    ranks = lax.axis_size("seq")
    depth = lax.axis_size("fsdp")
    reach = WINDOW // row_count
    shard_rows = w_query.shape[0]
    part_rows = shard_rows // ranks
    quarter = FF // 4
    column = model_width // 4
    half_rows = w_down.shape[0] // 2
    split = model_width + 2 * HD
    plane = Plane()
    level = lax.axis_index("fsdp").astype(jnp.int32)
    levels = (level + 1 + jnp.arange(depth, dtype=jnp.int32)) % depth
    at = jnp.concatenate([plane.sources, levels]).astype(jnp.int32)

    def my_rows(shard):
        return lax.dynamic_slice_in_dim(shard, plane.me * part_rows, part_rows, axis=0)

    def by_parts(shard):
        return shard.reshape(ranks, part_rows, shard.shape[1])

    gains = jnp.pad(jnp.stack([norm_gain, ffn_gain]), ((0, 14), (0, 0)))
    early = plane.along(jnp.concatenate([my_rows(w_query), my_rows(w_kv)], axis=1))
    other_gains = plane.along(gains)
    send_slot, send_place = places_of(arrival_order, ranks)
    place_slots = to_slots(send_place, send_slot, ranks, -1)
    token_slots = to_slots(tokens[0], send_slot, ranks)
    cotangent_slots = to_slots(after(cotangent[0], token_slots), send_slot, ranks)
    got_place = exchange(place_slots)
    got_tokens = exchange(token_slots)
    early = jnp.stack(after_all(early, cotangent_slots))
    own, other = plane.gather(early)
    got_cotangent = exchange(after(cotangent_slots, early))
    down_piece = lax.dynamic_slice(
        after(w_down, early), (plane.core * half_rows, plane.chip * column), (half_rows, column)
    )
    down_piece = lax.all_gather(down_piece, "fsdp", axis=0, tiled=False)
    gate_up_piece = lax.dynamic_slice(
        after(w_gate_up, early),
        (0, plane.core * FF + plane.chip * quarter),
        (shard_rows, quarter),
    )
    gate_up_piece = lax.all_gather(gate_up_piece, "fsdp", axis=0, tiled=False)
    out_piece = plane.along(after(my_rows(w_out), early))

    recv_place = got_place.reshape(-1)
    is_live = recv_place >= 0
    landing = jnp.where(is_live, recv_place, row_count)
    safe_place = jnp.where(is_live, recv_place, 0)
    packed_f = widened(from_slots(got_tokens, landing))
    gain_rows = jnp.concatenate([jnp.stack(other_gains), gains[None]], axis=0)[:, :2]
    gain_rows = gain_rows[(jnp.arange(depth, dtype=jnp.int32) + depth - 1 - level) % depth]
    gain_attn = widened(gain_rows[:, 0].reshape(model_width))
    gain_ffn = widened(gain_rows[:, 1].reshape(model_width))
    docs, cosine, sine = positions_of(lengths, row_count)
    tables = tables_of(cosine, sine, 2, 0)
    normed = rounded(rms_scale(packed_f, gain_attn))

    query_w, kv_w = put_pieces(own + other, at, [by_parts(w_query), by_parts(w_kv)])
    query_w = query_w.reshape(model_width, model_width)
    kv_w = kv_w.reshape(model_width, 2 * HD)
    pair = pair_of(dot(normed, kv_w), cosine, sine)
    query_lin = dot(after(normed, pair), query_w)
    out_own, out_other = plane.gather(jnp.stack(after_all(out_piece, own[3])))
    packed_grad = from_slots(after(got_cotangent, pair), landing)
    down_piece = rest(after(down_piece, pair), level)
    down_own, down_other = plane.gather(down_piece)
    down_pieces = down_own + down_other
    pair_rows = with_earlier(pair, reach)
    pairs_across = pair_rows.T
    queries, mixed, totals = attend(
        after(query_lin, packed_grad, down_piece), tables, pair_rows, pairs_across, *docs
    )
    (out_w,) = put_pieces(out_own + out_other, after(at, mixed), [by_parts(w_out)])
    out_w = out_w.reshape(model_width, model_width)
    hidden_state = packed_f + dot(mixed, out_w)
    ffn_in = rounded(rms_scale(hidden_state, gain_ffn))

    gate_up_piece = rest(after(gate_up_piece, ffn_in), level)
    first_ws, second_ws = plane.gather(gate_up_piece.reshape((depth - 1) * shard_rows, quarter))
    block_sum, d_ffn_in, terms = hidden_state, None, None
    firsts, swaps = [], []
    chunk_in = ffn_in
    for slot in range(4):
        if slot >= 2:
            chunk_in = after(chunk_in, swaps[slot - 2])
        facts = [plane.core, plane.chips[slot], plane.core, *plane.chips, level]
        block_sum, d_ffn_in, first_grad, second_grad, terms = feed(
            jnp.stack(facts).astype(jnp.int32),
            chunk_in,
            packed_grad,
            first_ws[slot],
            second_ws[slot],
            w_gate_up,
            down_pieces,
            w_down,
            block_sum,
            d_ffn_in,
            terms,
        )
        firsts.append(first_grad)
        swaps.append(plane.swap(second_grad))
        if slot == 2:
            sum_v = added(firsts[2], swaps[1])
            from_v = plane.second(sum_v)
            chunk_in = after(chunk_in, sum_v)

    terms = [term.reshape(depth * half_rows, column) for term in terms]
    down_swaps = [plane.swap(term) for term in terms[4:]]
    unused_scaled, ffn_norm_pull = jax.vjp(rms_scale, hidden_state, gain_ffn)
    d_hidden_norm, grad_gain_ffn = ffn_norm_pull(d_ffn_in)
    d_hidden = widened(packed_grad) + d_hidden_norm
    d_branch = rounded(d_hidden)
    d_mixed = rounded(dot_across(d_branch, out_w))
    sum_d = added(after(firsts[3], d_mixed), swaps[3])
    from_d = plane.second(sum_d)
    down_sums = [
        added(after(term, sum_d), down_swaps[match])
        for term, match in zip(terms[:4], (0, 2, 1, 3))
    ]
    from_down_d, from_down_v = plane.second(down_sums[3]), plane.second(down_sums[2])
    d_query_lin, d_pairs = attend_back(
        queries, after(d_mixed, *down_sums), totals, tables, pair_rows, pairs_across, *docs
    )
    d_own = owners_sum(d_pairs, row_count, reach)
    sum_u = added(after(firsts[1], d_pairs), swaps[2], from_d)
    from_u = plane.first(sum_u)
    grad_out = dot_rows(mixed, after(d_branch, sum_u))
    grad_query = dot_rows(normed, after(d_query_lin, sum_u))
    block_rows = rounded(after(block_sum, sum_u))
    home_out = exchange(back_to_slots(block_rows, is_live, safe_place, ranks))
    down_u = added(after(down_sums[1], grad_query), from_down_d)
    from_down_u = plane.first(down_u)
    d_kv_lin = rounded(
        jnp.concatenate([unrotate(d_own[:, :HD], cosine, sine), d_own[:, HD:]], axis=1)
    )
    d_kv_lin = after(d_kv_lin, down_u)
    grad_kv = dot_rows(normed, d_kv_lin)
    d_normed = dot_across(d_query_lin, query_w) + dot_across(d_kv_lin, kv_w)
    unused_normed, attn_norm_pull = jax.vjp(rms_scale, packed_f, gain_attn)
    d_packed_norm, grad_gain_attn = attn_norm_pull(d_normed)
    grad_rows = rounded(d_hidden + d_packed_norm)
    home_grad = exchange(back_to_slots(grad_rows, is_live, safe_place, ranks))

    total = added(after(firsts[0], grad_rows), swaps[0], from_v, from_u)
    mine_gate_up = plane.down_columns(total)

    def by_rows(grad):
        pieces = rounded(grad).reshape(depth, ranks, part_rows, grad.shape[1])
        return [
            lax.dynamic_index_in_dim(pieces, plane.sources[i], axis=1, keepdims=False)
            for i in range(8)
        ]

    gain_rows = jnp.concatenate(
        [
            rounded(grad_gain_attn).reshape(depth, 1, shard_rows),
            rounded(grad_gain_ffn).reshape(depth, 1, shard_rows),
        ],
        axis=2,
    )
    gain_rows = jnp.pad(gain_rows, ((0, 0), (0, 15), (0, split - 2 * shard_rows)))
    pieces = [
        jnp.concatenate([jnp.concatenate([q, k], axis=2), gain_rows], axis=1).reshape(
            depth * (part_rows + 16), split
        )
        for q, k in zip(by_rows(grad_query), by_rows(grad_kv))
    ]
    mine_early = plane.down_columns(plane.merge(pieces[:4], pieces[4:]))
    total = added(down_sums[0], from_down_v, from_down_u)
    mine_down = plane.down_columns(total)
    pieces = [p.reshape(depth * part_rows, model_width) for p in by_rows(grad_out)]
    mine_out = plane.down_columns(plane.merge(pieces[:4], pieces[4:]))

    def everywhere(mine, rows, width, place):
        own, other = plane.gather(mine)
        return spread(own + other, plane.sources, (rows, width), place)

    total_gate_up = everywhere(
        mine_gate_up, shard_rows, 2 * FF, lambda p: (0, (p % 2) * 4 + p // 2)
    )
    total_down = everywhere(
        mine_down, 2 * half_rows, model_width, lambda p: (p % 2, p // 2)
    )
    total_out = everywhere(mine_out, shard_rows, model_width, lambda p: (p, 0))
    total_early = everywhere(mine_early[:part_rows], shard_rows, split, lambda p: (p, 0))
    block_arrived = home_out.reshape(-1, model_width)[send_slot]
    grad_arrived = home_grad.reshape(-1, model_width)[send_slot]
    return (
        block_arrived[None],
        grad_arrived[None],
        widened(mine_early[part_rows, :shard_rows]),
        total_early[:, :model_width],
        total_early[:, model_width:],
        total_out,
        widened(mine_early[part_rows, shard_rows : 2 * shard_rows]),
        total_gate_up,
        total_down,
    )


def solution(mesh):
    placed = (
        P("fsdp", "seq", None),
        P("fsdp", "seq", None),
        P("fsdp", "seq"),
        P("fsdp", None),
        P("fsdp"),
        P("fsdp", None),
        P("fsdp", None),
        P("fsdp", None),
        P("fsdp"),
        P("fsdp", None),
        P("fsdp", None),
    )
    return jax.shard_map(
        body,
        mesh=mesh,
        in_specs=placed,
        out_specs=(
            P("fsdp", "seq", None),
            P("fsdp", "seq", None),
            P("fsdp"),
            P("fsdp", None),
            P("fsdp", None),
            P("fsdp", None),
            P("fsdp"),
            P("fsdp", None),
            P("fsdp", None),
        ),
        check_vma=False,
    )
```

```python
import jax
import jax.numpy as jnp
from jax import lax
from jax.experimental import pallas as pl
from jax.experimental.pallas import tpu as pltpu
from jax.sharding import PartitionSpec as P

HD = 192
FF = 4608
WINDOW = 1024


EPSILON = 1e-06
ROPE_BASE = 10000.0
MASKED = -1e30


def passed_along(x, axis, by):
    length = lax.axis_size(axis)
    pairs = [(i, i + by) for i in range(length) if 0 <= i + by < length]
    return lax.ppermute(x, axis, pairs)


def rms_scale(values, gain):
    return values * lax.rsqrt(jnp.mean(values * values, axis=-1, keepdims=True) + EPSILON) * gain


def rotate(heads, cosine, sine):
    half = heads.shape[-1] // 2
    first_half = heads[..., :half]
    second_half = heads[..., half:]
    return jnp.concatenate(
        [first_half * cosine - second_half * sine, second_half * cosine + first_half * sine],
        axis=-1,
    )


def unrotate(heads, cosine, sine):
    half = heads.shape[-1] // 2
    first_half = heads[..., :half]
    second_half = heads[..., half:]
    return jnp.concatenate(
        [first_half * cosine + second_half * sine, second_half * cosine - first_half * sine],
        axis=-1,
    )


def angles(places, head_width):
    steps_half = jnp.arange(head_width // 2, dtype=jnp.float32)
    inverse = ROPE_BASE ** (-2.0 * steps_half / head_width)
    theta = places[:, None] * inverse[None, :]
    return (jnp.cos(theta), jnp.sin(theta))


def layout(lengths, places):
    ends = jnp.cumsum(lengths)
    starts = ends - lengths
    inside = (places[:, None] >= starts[None, :]) & (places[:, None] < ends[None, :])
    numbers = jnp.arange(1, lengths.shape[0] + 1, dtype=jnp.int32)
    document = jnp.sum(jnp.where(inside, numbers[None, :], 0), axis=1) - 1
    offset = places - jnp.sum(jnp.where(inside, starts[None, :], 0), axis=1)
    return (document, offset)


def after(x, *done):
    return lax.optimization_barrier((x, *done))[0]


def fence(*xs):
    return lax.optimization_barrier(xs)


def rounded(x):
    return x.astype(jnp.bfloat16)


def widened(x):
    return x.astype(jnp.float32)


def added(*terms):
    return rounded(sum(widened(term) for term in terms))


def dot(a, b):
    return jnp.dot(a, b, preferred_element_type=jnp.float32)


def dot_rows(a, b):
    return jnp.einsum("td,tf->df", a, b, preferred_element_type=jnp.float32)


def dot_across(a, b):
    return jnp.einsum("tf,df->td", a, b, preferred_element_type=jnp.float32)


def turn(x, tables, back):
    width = x.shape[-1]
    half = HD // 2
    later = pltpu.roll(x, width - half, axis=1)
    sooner = pltpu.roll(x, half, axis=1)
    turned = later * tables[1] + sooner * tables[2]
    return x * tables[0] - turned if back else x * tables[0] + turned


def tables_of(cosine, sine, heads, still):
    none = jnp.zeros_like(sine)
    ones = jnp.ones_like(sine)
    return (
        jnp.concatenate([cosine, cosine] * heads + [ones, ones] * still, axis=1),
        jnp.concatenate([-sine, none] * heads + [none, none] * still, axis=1),
        jnp.concatenate([none, sine] * heads + [none, none] * still, axis=1),
    )


def rows_first(arrays):
    def kernel(*refs):
        for source, target in zip(refs, refs[len(arrays) :]):
            target[...] = source[...]

    return pl.pallas_call(
        kernel, out_shape=[jax.ShapeDtypeStruct(x.shape, x.dtype) for x in arrays]
    )(*arrays)


def no_entry(doc_query, doc_key, rows, keys):
    key = lax.broadcasted_iota(jnp.int32, (keys, rows), 0)
    row = lax.broadcasted_iota(jnp.int32, (keys, rows), 1)
    gap = WINDOW + row - key
    seen = (doc_key == doc_query) & (doc_key >= 0) & (gap >= 0) & (gap < WINDOW)
    return jnp.where(seen, 0.0, MASKED)


def dot_last(a, b):
    return lax.dot_general(a, b, (((1,), (1,)), ((), ())), preferred_element_type=jnp.float32)


def attend(query_lin, tables, pairs, pairs_across, doc_query, doc_key):
    rows, width = query_lin.shape
    block = 256
    keys = WINDOW + block
    couples = width // (2 * HD)

    def kernel(q_ref, t0, t1, t2, pairs_ref, across_ref, dq_ref, dk_ref, turned_ref, mixed_ref, total_ref, bias):
        start = pl.multiple_of(pl.program_id(0) * block, block)
        window = pl.ds(start, keys)

        @pl.when(pl.program_id(1) == 0)
        def fill():
            bias[...] = no_entry(dq_ref[...], dk_ref[window, :], block, keys)

        queries = turn(q_ref[...], (t0[...], t1[...], t2[...]), False) * HD ** (-0.5)
        queries = queries.astype(jnp.bfloat16)
        turned_ref[...] = queries
        own_keys = pairs_ref[window, :][:, :HD]
        values = across_ref[pl.ds(HD, HD), window]
        mixed, totals = [], []
        for head in range(2):
            scores = dot_last(own_keys, queries[:, head * HD : (head + 1) * HD]) + bias[...]
            top = jnp.max(scores, axis=0, keepdims=True)
            weights = jnp.exp(scores - top)
            total = jnp.sum(weights, axis=0, keepdims=True)
            totals.append(top + jnp.log(total))
            mixed.append(dot(values, weights.astype(jnp.bfloat16)) * (1.0 / total))
        mixed_ref[...] = jnp.concatenate(mixed, axis=0).T.astype(jnp.bfloat16)
        total_ref[0] = jnp.concatenate(totals, axis=0)

    tile = pl.BlockSpec((block, 2 * HD), lambda i, j: (i, j))
    table = pl.BlockSpec((block, 2 * HD), lambda i, j: (i, 0))
    return pl.pallas_call(
        kernel,
        grid=(rows // block, couples),
        in_specs=[
            tile,
            table,
            table,
            table,
            pl.BlockSpec(pairs.shape, lambda i, j: (0, 0)),
            pl.BlockSpec(pairs_across.shape, lambda i, j: (0, 0)),
            pl.BlockSpec((1, block), lambda i, j: (0, i)),
            pl.BlockSpec(doc_key.shape, lambda i, j: (0, 0)),
        ],
        out_specs=[tile, tile, pl.BlockSpec((1, 2, block), lambda i, j: (j, 0, i))],
        out_shape=[
            jax.ShapeDtypeStruct((rows, width), jnp.bfloat16),
            jax.ShapeDtypeStruct((rows, width), jnp.bfloat16),
            jax.ShapeDtypeStruct((couples, 2, rows), jnp.float32),
        ],
        scratch_shapes=[pltpu.VMEM((keys, block), jnp.float32)],
        compiler_params=pltpu.CompilerParams(vmem_limit_bytes=48 * 2**20),
        cost_estimate=pl.CostEstimate(flops=10**8, bytes_accessed=10**5, transcendentals=0),
    )(query_lin, *tables, pairs, pairs_across, doc_query, doc_key)


def attend_back(queries, d_mixed, totals, tables, pairs, pairs_across, doc_query, doc_key):
    rows, width = queries.shape
    block = 256
    keys = WINDOW + block
    couples = width // (2 * HD)
    last = (rows // block - 1, couples - 1)

    def kernel(q_ref, do_ref, total_ref, t0, t1, t2, pairs_ref, across_ref, dq_ref, dk_ref, d_lin_ref, d_pairs_ref, bias, d_keys, d_values, values):
        start = pl.multiple_of(pl.program_id(0) * block, block)
        window = pl.ds(start, keys)

        @pl.when((pl.program_id(0) == 0) & (pl.program_id(1) == 0))
        def clear():
            d_keys[...] = jnp.zeros_like(d_keys)
            d_values[...] = jnp.zeros_like(d_values)
            values[...] = pairs_ref[...][:, HD:]

        @pl.when(pl.program_id(1) == 0)
        def fill():
            bias[...] = no_entry(dq_ref[...], dk_ref[window, :], block, keys)

        own_keys = pairs_ref[window, :][:, :HD]
        own_values = values[window, :]
        keys_across = across_ref[pl.ds(0, HD), window]
        d_turned = []
        for head in range(2):
            part = slice(head * HD, (head + 1) * HD)
            q, do = q_ref[...][:, part], do_ref[...][:, part]
            scores = dot_last(own_keys, q) + bias[...]
            probs = jnp.exp(scores - total_ref[0][head : head + 1, :])
            d_probs = dot_last(own_values, do)
            product = probs * d_probs
            weighted = jnp.sum(product, axis=0, keepdims=True)
            d_scores = (product - probs * weighted).astype(jnp.bfloat16)
            d_turned.append(dot(keys_across, d_scores))
            d_keys[window, :] += dot(d_scores, q)
            d_values[window, :] += dot(probs.astype(jnp.bfloat16), do)
        d_turned = jnp.concatenate(d_turned, axis=0).T
        d_lin = turn(d_turned, (t0[...], t1[...], t2[...]), True) * HD ** (-0.5)
        d_lin_ref[...] = d_lin.astype(jnp.bfloat16)

        @pl.when((pl.program_id(0) == last[0]) & (pl.program_id(1) == last[1]))
        def finish():
            d_pairs_ref[...] = jnp.concatenate([d_keys[...], d_values[...]], axis=1)

    tile = pl.BlockSpec((block, 2 * HD), lambda i, j: (i, j))
    table = pl.BlockSpec((block, 2 * HD), lambda i, j: (i, 0))
    return pl.pallas_call(
        kernel,
        grid=(rows // block, couples),
        in_specs=[
            tile,
            tile,
            pl.BlockSpec((1, 2, block), lambda i, j: (j, 0, i)),
            table,
            table,
            table,
            pl.BlockSpec(pairs.shape, lambda i, j: (0, 0)),
            pl.BlockSpec(pairs_across.shape, lambda i, j: (0, 0)),
            pl.BlockSpec((1, block), lambda i, j: (0, i)),
            pl.BlockSpec(doc_key.shape, lambda i, j: (0, 0)),
        ],
        out_specs=[tile, pl.BlockSpec(pairs.shape, lambda i, j: (0, 0))],
        out_shape=[
            jax.ShapeDtypeStruct((rows, width), jnp.bfloat16),
            jax.ShapeDtypeStruct(pairs.shape, jnp.float32),
        ],
        scratch_shapes=[
            pltpu.VMEM((keys, block), jnp.float32),
            pltpu.VMEM((pairs.shape[0], HD), jnp.float32),
            pltpu.VMEM((pairs.shape[0], HD), jnp.float32),
            pltpu.VMEM((pairs.shape[0], HD), jnp.bfloat16),
        ],
        compiler_params=pltpu.CompilerParams(vmem_limit_bytes=48 * 2**20),
        cost_estimate=pl.CostEstimate(flops=10**8, bytes_accessed=10**5, transcendentals=0),
    )(queries, d_mixed, totals, *tables, pairs, pairs_across, doc_query, doc_key)


def put_pieces(pieces, positions, shards):
    count = len(pieces)
    others, rows, unused_width = pieces[0].shape
    depth = others + 1
    widths = [shard.shape[2] for shard in shards]

    def kernel(positions_ref, *refs):
        i, j = pl.program_id(0), pl.program_id(1)
        sources, locals_, targets = (
            refs[:count],
            refs[count : count + len(shards)],
            refs[count + len(shards) :],
        )
        for at in range(count):

            @pl.when((i == at) & (j < others))
            def take():
                start = 0
                for target, width in zip(targets, widths):
                    target[0, 0] = sources[at][j, :, pl.ds(start, width)]
                    start += width

        @pl.when(j == others)
        def keep():
            for target, source in zip(targets, locals_):
                target[0, 0] = source[0]

    return pl.pallas_call(
        kernel,
        out_shape=[
            jax.ShapeDtypeStruct((depth, count, rows, width), pieces[0].dtype) for width in widths
        ],
        grid_spec=pltpu.PrefetchScalarGridSpec(
            num_scalar_prefetch=1,
            grid=(count, depth),
            in_specs=[pl.BlockSpec(p.shape, lambda i, j, at: (0, 0, 0)) for p in pieces]
            + [pl.BlockSpec((1, rows, width), lambda i, j, at: (at[i], 0, 0)) for width in widths],
            out_specs=[
                pl.BlockSpec(
                    (1, 1, rows, width),
                    lambda i, j, at: (at[count + j], at[i], 0, 0),
                )
                for width in widths
            ],
        ),
        compiler_params=pltpu.CompilerParams(vmem_limit_bytes=40 * 2**20),
    )(positions, *pieces, *shards)


def rest(x, level):
    depth = x.shape[0]
    block = (1,) + x.shape[1:]
    zeros = (0,) * (x.ndim - 1)

    def kernel(level_ref, source, target):
        target[...] = source[...]

    return pl.pallas_call(
        kernel,
        out_shape=jax.ShapeDtypeStruct((depth - 1,) + x.shape[1:], x.dtype),
        grid_spec=pltpu.PrefetchScalarGridSpec(
            num_scalar_prefetch=1,
            grid=(depth - 1,),
            in_specs=[
                pl.BlockSpec(block, lambda i, at: (lax.rem(at[0] + i + 1, depth), *zeros))
            ],
            out_specs=pl.BlockSpec(block, lambda i, at: (i, *zeros)),
        ),
    )(level[None], x)


def spread(pieces, positions, shape, place):
    count = len(pieces)
    rows, width = pieces[0].shape

    def kernel(positions_ref, *refs):
        for at in range(count):

            @pl.when(pl.program_id(0) == at)
            def take():
                refs[-1][...] = refs[at][...].astype(jnp.float32)

    return pl.pallas_call(
        kernel,
        out_shape=jax.ShapeDtypeStruct(shape, jnp.float32),
        grid_spec=pltpu.PrefetchScalarGridSpec(
            num_scalar_prefetch=1,
            grid=(count,),
            in_specs=[pl.BlockSpec((rows, width), lambda i, at: (0, 0))] * count,
            out_specs=pl.BlockSpec((rows, width), lambda i, at: place(at[i])),
        ),
        compiler_params=pltpu.CompilerParams(vmem_limit_bytes=40 * 2**20),
    )(positions, *pieces)


GELU_SCALE = 0.7978845608028654
GELU_CUBE = 0.044715


def dot_first(a, b):
    return lax.dot_general(a, b, (((0,), (0,)), ((), ())), preferred_element_type=jnp.float32)


def feed(facts, x, grad, first_w, second_w, shard, down_pieces, down_shard, block_sum, back_sum, terms):
    rows, width = x.shape
    hidden = first_w.shape[1]
    half = hidden // 2
    column = width // 4
    depth = down_pieces[0].shape[0] + 1
    level_rows = width // depth
    full = depth * hidden
    started = back_sum is not None
    pieces = 8
    f32, bf16 = jnp.float32, jnp.bfloat16

    def kernel(facts_ref, x_ref, g_ref, *refs):
        wa_in, wb_in, shard_in, down_in, block_in = refs[:5]
        down_pieces_in = refs[5 : 5 + pieces]
        refs = refs[5 + pieces :]
        if started:
            back_in = refs[0]
            refs = refs[1 + pieces :]
        block_out, back_out, ga_out, gb_out = refs[:4]
        term_out = refs[4 : 4 + pieces]
        wa, wb, wd, a, b, d, act, da, db, block, back, ga, gb, gd, sems = refs[4 + pieces :]
        chip = facts_ref[1]
        core, level = facts_ref[2], facts_ref[7]

        def rows_of(source, target, side, sem):
            copies = []
            for i in range(1, depth):
                place = pl.multiple_of(lax.rem(level + i, depth) * level_rows, 16)
                copies.append(
                    pltpu.make_async_copy(
                        source.at[pl.ds((i - 1) * level_rows, level_rows)],
                        target.at[pl.ds(place, level_rows)],
                        sem,
                    )
                )
            place = pl.multiple_of(level * level_rows, 16)
            start = pl.multiple_of(side * full + chip * hidden, 128)
            copies.append(
                pltpu.make_async_copy(
                    shard_in.at[:, pl.ds(start, hidden)],
                    target.at[pl.ds(place, level_rows)],
                    sem,
                )
            )
            return copies

        for copy in rows_of(wa_in, wa, core, sems.at[0]):
            copy.start()
        for copy in rows_of(wb_in, wb, 1 - core, sems.at[1]):
            copy.start()

        @pl.when(chip == level)
        def here():
            pltpu.make_async_copy(down_in, wd, sems.at[2]).start()

        @pl.when(chip != level)
        def elsewhere():
            step = lax.rem(chip - level + depth - 1, depth)
            for i in range(pieces):
                side = jnp.where(i < 4, core, 1 - core)
                pltpu.make_async_copy(
                    down_pieces_in[i].at[step],
                    wd.at[
                        pl.ds(pl.multiple_of(side * half, 16), half),
                        pl.ds(pl.multiple_of(facts_ref[3 + i % 4] * column, 128), column),
                    ],
                    sems.at[2],
                ).start()

        load_block = pltpu.make_async_copy(block_in, block, sems.at[3])
        load_block.start()
        if started:
            load_back = pltpu.make_async_copy(back_in, back, sems.at[4])
            load_back.start()
        pltpu.make_async_copy(wa, wa, sems.at[0]).wait()
        a[...] = dot(x_ref[...], wa[...])
        pltpu.make_async_copy(wb, wb, sems.at[1]).wait()
        b[...] = dot(x_ref[...], wb[...])
        pltpu.make_async_copy(wd, wd, sems.at[2]).wait()
        d[...] = dot_last(g_ref[...], wd[...])
        swapped = facts_ref[0] == 1

        @pl.loop(0, rows // 16)
        def glu(i):
            part = pl.ds(pl.multiple_of(i * 16, 16), 16)
            for j in range(hidden // 384):
                lanes = slice(j * 384, (j + 1) * 384)
                one, two, slope = a[part, lanes], b[part, lanes], d[part, lanes]
                gate = jnp.where(swapped, two, one)
                up = jnp.where(swapped, one, two)
                square = gate * gate
                inner = gate * (square * (GELU_SCALE * GELU_CUBE) + GELU_SCALE)
                share = 0.5 * jnp.tanh(inner) + 0.5
                gelu = gate * share
                bend = square * (6.0 * GELU_SCALE * GELU_CUBE) + 2.0 * GELU_SCALE
                rise = share + gelu * (1.0 - share) * bend
                d_gate = (slope * up) * rise
                d_up = slope * gelu
                act[part, lanes] = (gelu * up).astype(bf16)
                da[part, lanes] = jnp.where(swapped, d_up, d_gate).astype(bf16)
                db[part, lanes] = jnp.where(swapped, d_gate, d_up).astype(bf16)

        for i in range(width // 384):
            part = pl.ds(i * 384, 384)
            gb[part, :] = dot_first(x_ref[:, i * 384 : (i + 1) * 384], db[...]).astype(bf16)
            pltpu.make_async_copy(gb.at[part], gb_out.at[part], sems.at[5]).start()
        for i in range(width // 384):
            part = pl.ds(i * 384, 384)
            ga[part, :] = dot_first(x_ref[:, i * 384 : (i + 1) * 384], da[...]).astype(bf16)
            pltpu.make_async_copy(ga.at[part], ga_out.at[part], sems.at[6]).start()
        for i in range(hidden // 384):
            part = pl.ds(i * 384, 384)
            gd[part, :] = dot_first(act[:, i * 384 : (i + 1) * 384], g_ref[...]).astype(bf16)
        stores = []
        for i in range(pieces):
            side = jnp.where(i < 4, core, 1 - core)
            stores.append(
                pltpu.make_async_copy(
                    gd.at[
                        pl.ds(pl.multiple_of(side * half, 16), half),
                        pl.ds(pl.multiple_of(facts_ref[3 + i % 4] * column, 128), column),
                    ],
                    term_out[i].at[chip],
                    sems.at[7 + i],
                )
            )
        for store in stores:
            store.start()
        if started:
            load_back.wait()

            back[...] += dot_last(da[...], wa[...])
            back[...] += dot_last(db[...], wb[...])
        else:
            back[...] = dot_last(da[...], wa[...])
            back[...] += dot_last(db[...], wb[...])
        store_back = pltpu.make_async_copy(back, back_out, sems.at[15])
        store_back.start()
        load_block.wait()
        for i in range(2):
            part = pl.ds(i * (rows // 2), rows // 2)
            block[part, :] += dot(act[part, :], wd[...])
            pltpu.make_async_copy(block.at[part], block_out.at[part], sems.at[16]).start()
        for store in stores:
            store.wait()
        pltpu.make_async_copy(gb, gb_out, sems.at[5]).wait()
        pltpu.make_async_copy(ga, ga_out, sems.at[6]).wait()
        store_back.wait()
        pltpu.make_async_copy(block, block_out, sems.at[16]).wait()

    anywhere = pl.BlockSpec(memory_space=pl.ANY)
    inside = pl.BlockSpec(memory_space=pltpu.VMEM)
    operands = [facts, x, grad, first_w, second_w, shard, down_shard, block_sum, *down_pieces]
    aliases = {}
    if started:
        aliases[7] = 0
        aliases[len(operands)] = 1
        operands.append(back_sum)
        for i, term in enumerate(terms):
            aliases[len(operands)] = 4 + i
            operands.append(term)
    sums = jax.ShapeDtypeStruct((rows, width), f32)
    grads = jax.ShapeDtypeStruct((width, hidden), bf16)
    results = pl.pallas_call(
        kernel,
        in_specs=[pl.BlockSpec(memory_space=pltpu.SMEM), inside, inside]
        + [anywhere] * (len(operands) - 3),
        out_specs=[anywhere] * (4 + pieces),
        out_shape=[sums, sums, grads, grads]
        + [jax.ShapeDtypeStruct((depth, half, column), bf16)] * pieces,
        input_output_aliases=aliases,
        scratch_shapes=[
            pltpu.VMEM((width, hidden), bf16),
            pltpu.VMEM((width, hidden), bf16),
            pltpu.VMEM((hidden, width), bf16),
            pltpu.VMEM((rows, hidden), f32),
            pltpu.VMEM((rows, hidden), f32),
            pltpu.VMEM((rows, hidden), f32),
            pltpu.VMEM((rows, hidden), bf16),
            pltpu.VMEM((rows, hidden), bf16),
            pltpu.VMEM((rows, hidden), bf16),
            pltpu.VMEM((rows, width), f32),
            pltpu.VMEM((rows, width), f32),
            pltpu.VMEM((width, hidden), bf16),
            pltpu.VMEM((width, hidden), bf16),
            pltpu.VMEM((hidden, width), bf16),
            pltpu.SemaphoreType.DMA((17,)),
        ],
        compiler_params=pltpu.CompilerParams(vmem_limit_bytes=56 * 2**20),
        cost_estimate=pl.CostEstimate(flops=10**8, bytes_accessed=10**5, transcendentals=0),
    )(*operands)
    return results[0], results[1], results[2], results[3], results[4:]


class Plane:
    def __init__(self):
        self.me = lax.axis_index("seq")
        self.core = self.me % 2
        self.chip = self.me // 2
        first = jnp.where(self.core == 0, 1, 2)
        self.chips = [self.chip, self.chip ^ first, self.chip ^ (3 - first), self.chip ^ 3]
        self.first_pairs = [(i, i ^ (2 if i % 2 == 0 else 4)) for i in range(8)]
        self.second_pairs = [(i, i ^ (4 if i % 2 == 0 else 2)) for i in range(8)]
        self.core_pairs = [(i, i ^ 1) for i in range(8)]
        self.sources = jnp.stack(
            [chip * 2 + self.core for chip in self.chips]
            + [chip * 2 + 1 - self.core for chip in self.chips]
        )

    def first(self, x):
        return lax.ppermute(x, "seq", self.first_pairs)

    def second(self, x):
        return lax.ppermute(x, "seq", self.second_pairs)

    def along(self, x):
        depth = lax.axis_size("fsdp")
        return [
            lax.ppermute(x, "fsdp", [((i + k) % depth, i) for i in range(depth)])
            for k in range(1, depth)
        ]

    def swap(self, x):
        return lax.ppermute(x, "seq", self.core_pairs)

    def down_columns(self, x):
        return lax.psum_scatter(x, "fsdp", scatter_dimension=0, tiled=True)


def places_of(arrival_order, ranks):
    row_count = arrival_order.shape[1]
    capacity = 2 * row_count // ranks
    arrived_at = arrival_order[0]
    owner = arrived_at // row_count
    owner_hits = (owner[:, None] == jnp.arange(ranks, dtype=jnp.int32)[None, :]).astype(jnp.int32)
    within = jnp.sum(jnp.cumsum(owner_hits, axis=0) * owner_hits, axis=1) - 1
    return owner * capacity + within, arrived_at % row_count


def to_slots(rows, slots, ranks, empty=0):
    capacity = 2 * rows.shape[0] // ranks
    out = jnp.full((ranks * capacity,) + rows.shape[1:], empty, rows.dtype)
    return out.at[slots].set(rows).reshape((ranks, capacity) + rows.shape[1:])


def from_slots(slots, landing):
    flat = slots.reshape((-1, slots.shape[-1]))
    out = jnp.zeros((flat.shape[0] // 2, flat.shape[1]), flat.dtype)
    return out.at[landing].set(flat, mode="drop")


def back_to_slots(rows, is_live, safe_place, ranks):
    chosen = jnp.where(is_live[:, None], rows[safe_place], jnp.zeros((), rows.dtype))
    return chosen.reshape(ranks, -1, rows.shape[1])


def exchange(x):
    return lax.all_to_all(x, "seq", split_axis=0, concat_axis=0, tiled=True)


def positions_of(lengths, row_count):
    position = lax.axis_index("seq")
    places = position * row_count + jnp.arange(row_count, dtype=jnp.int32)
    doc_query, offset_query = layout(lengths[0], places)
    key_places = (
        position * row_count - WINDOW + jnp.arange(WINDOW + row_count, dtype=jnp.int32)
    )
    doc_key, unused_offset = layout(lengths[0], key_places)
    cosine, sine = angles(offset_query.astype(jnp.float32), HD)
    return (doc_query[None, :], doc_key[:, None]), cosine, sine


def pair_of(kv_lin, cosine, sine):
    own_keys = rounded(rotate(kv_lin[:, :HD], cosine, sine))
    return jnp.concatenate([own_keys, rounded(kv_lin[:, HD:])], axis=1)


def with_earlier(pair, reach):
    return jnp.concatenate(
        [passed_along(pair, "seq", distance) for distance in range(reach, 0, -1)] + [pair], axis=0
    )


def owners_sum(d_pairs, row_count, reach):
    parts = [
        passed_along(
            rounded(d_pairs[(reach - distance) * row_count :][:row_count]), "seq", -distance
        )
        for distance in range(reach, 0, -1)
    ]
    own = d_pairs[reach * row_count :]
    for part in parts:
        own = own + widened(part)
    return own


def body(*operands):
    return square_body(*operands) if lax.axis_size("seq") == 8 else plain_body(*operands)


def plain_body(
    tokens,
    cotangent,
    arrival_order,
    lengths,
    norm_gain,
    w_query,
    w_kv,
    w_out,
    ffn_gain,
    w_gate_up,
    w_down,
):
    row_count = tokens.shape[1]
    ranks = lax.axis_size("seq")
    reach = WINDOW // row_count
    position = lax.axis_index("seq")

    def whole(shard):
        part = shard.shape[0] // ranks
        mine = lax.dynamic_slice_in_dim(shard, position * part, part, axis=0)
        return lax.all_gather(mine, ("fsdp", "seq"), axis=0, tiled=True)

    def summed(grad):
        mine = lax.psum_scatter(rounded(grad), ("fsdp", "seq"), scatter_dimension=0, tiled=True)
        return widened(lax.all_gather(mine, "seq", axis=0, tiled=True))

    send_slot, send_place = places_of(arrival_order, ranks)
    got_tokens = exchange(to_slots(tokens[0], send_slot, ranks))
    got_cotangent = exchange(to_slots(cotangent[0], send_slot, ranks))
    recv_place = exchange(to_slots(send_place, send_slot, ranks, -1)).reshape(-1)
    is_live = recv_place >= 0
    landing = jnp.where(is_live, recv_place, row_count)
    safe_place = jnp.where(is_live, recv_place, 0)
    packed_f = widened(from_slots(got_tokens, landing))
    packed_grad = from_slots(got_cotangent, landing)
    query_w, kv_w, out_w, down_w, gate_up_w = (
        whole(w_query),
        whole(w_kv),
        whole(w_out),
        whole(w_down),
        whole(w_gate_up),
    )
    gain_attn, gain_ffn = (
        widened(lax.all_gather(gain, "fsdp", axis=0, tiled=True)) for gain in (norm_gain, ffn_gain)
    )
    docs, cosine, sine = positions_of(lengths, row_count)
    tables = tables_of(cosine, sine, 2, 0)

    normed = rounded(rms_scale(packed_f, gain_attn))
    pair_rows = with_earlier(pair_of(dot(normed, kv_w), cosine, sine), reach)
    queries, mixed, totals = attend(dot(normed, query_w), tables, pair_rows, pair_rows.T, *docs)
    hidden_state = packed_f + dot(mixed, out_w)
    ffn_in = rounded(rms_scale(hidden_state, gain_ffn))
    gate, up = dot(ffn_in, gate_up_w[:, :FF]), dot(ffn_in, gate_up_w[:, FF:])
    activated, pull = jax.vjp(lambda g, u: jax.nn.gelu(g, approximate=True) * u, gate, up)
    activated = rounded(activated)
    block_rows = rounded(hidden_state + dot(activated, down_w))

    d_gate, d_up = pull(dot_across(packed_grad, down_w))
    d_gate_up = jnp.concatenate([rounded(d_gate), rounded(d_up)], axis=1)
    unused_scaled, ffn_norm_pull = jax.vjp(rms_scale, hidden_state, gain_ffn)
    d_hidden_norm, grad_gain_ffn = ffn_norm_pull(dot_across(d_gate_up, gate_up_w))
    d_hidden = widened(packed_grad) + d_hidden_norm
    d_branch = rounded(d_hidden)
    d_mixed = rounded(dot_across(d_branch, out_w))
    d_query_lin, d_pairs = attend_back(
        queries, d_mixed, totals, tables, pair_rows, pair_rows.T, *docs
    )
    d_own = owners_sum(d_pairs, row_count, reach)
    d_kv_lin = rounded(
        jnp.concatenate([unrotate(d_own[:, :HD], cosine, sine), d_own[:, HD:]], axis=1)
    )
    d_normed = dot_across(d_query_lin, query_w) + dot_across(d_kv_lin, kv_w)
    unused_normed, attn_norm_pull = jax.vjp(rms_scale, packed_f, gain_attn)
    d_packed_norm, grad_gain_attn = attn_norm_pull(d_normed)
    grad_rows = rounded(d_hidden + d_packed_norm)
    block_arrived, grad_arrived = (
        exchange(back_to_slots(rows, is_live, safe_place, ranks)).reshape(-1, rows.shape[1])[
            send_slot
        ]
        for rows in (block_rows, grad_rows)
    )
    total_gain_attn, total_gain_ffn = (
        lax.psum(lax.psum_scatter(gain, "fsdp", scatter_dimension=0, tiled=True), "seq")
        for gain in (grad_gain_attn, grad_gain_ffn)
    )
    return (
        block_arrived[None],
        grad_arrived[None],
        total_gain_attn,
        summed(dot_rows(normed, d_query_lin)),
        summed(dot_rows(normed, d_kv_lin)),
        summed(dot_rows(mixed, d_branch)),
        total_gain_ffn,
        summed(dot_rows(ffn_in, d_gate_up)),
        summed(dot_rows(activated, packed_grad)),
    )


def square_body(
    tokens,
    cotangent,
    arrival_order,
    lengths,
    norm_gain,
    w_query,
    w_kv,
    w_out,
    ffn_gain,
    w_gate_up,
    w_down,
):
    row_count = tokens.shape[1]
    model_width = tokens.shape[2]
    ranks = lax.axis_size("seq")
    depth = lax.axis_size("fsdp")
    reach = WINDOW // row_count
    shard_rows = w_query.shape[0]
    part_rows = shard_rows // ranks
    quarter = FF // 4
    column = model_width // 4
    half_rows = w_down.shape[0] // 2
    split = model_width + 2 * HD
    plane = Plane()
    level = lax.axis_index("fsdp").astype(jnp.int32)
    levels = (level + 1 + jnp.arange(depth, dtype=jnp.int32)) % depth
    at = jnp.concatenate([plane.sources, levels]).astype(jnp.int32)

    def my_rows(shard):
        return lax.dynamic_slice_in_dim(shard, plane.me * part_rows, part_rows, axis=0)

    def by_parts(shard):
        return shard.reshape(ranks, part_rows, shard.shape[1])

    def second_halves(slots):
        return [plane.swap(slots[i]) for i in (0, 2, 1, 3)]


    gains = jnp.concatenate([norm_gain, ffn_gain]).reshape(part_rows, -1)
    gain_width = gains.shape[1]
    early = plane.along(
        jnp.concatenate(
            [my_rows(w_query), my_rows(w_kv), jnp.pad(gains, ((0, 0), (0, 128 - gain_width)))],
            axis=1,
        )
    )
    send_slot, send_place = places_of(arrival_order, ranks)
    labels = jnp.stack([send_place // 2, send_place % 2, jnp.ones_like(send_place)], axis=1)
    labels = jnp.pad(labels.astype(jnp.bfloat16), ((0, 0), (0, 125)))
    token_slots = to_slots(jnp.concatenate([tokens[0], labels], axis=1), send_slot, ranks)
    *early, token_slots, cotangent_rows, out_mine, down_mine, gate_up_mine = fence(
        *early, token_slots, cotangent[0], my_rows(w_out), w_down, w_gate_up
    )
    got_tokens = exchange(token_slots)
    early = jnp.stack(early)
    gain_rows = early[:, :, split : split + gain_width].reshape(depth - 1, 2, shard_rows)
    early = early[:, :, :split]

    def down_of(shard, chip):
        piece = lax.dynamic_slice(
            shard, (plane.core * half_rows, chip * column), (half_rows, column)
        )
        return lax.all_gather(piece, "fsdp", axis=0, tiled=False)

    down_piece = down_of(down_mine, plane.chip)
    gate_up_piece = lax.dynamic_slice(
        gate_up_mine, (0, plane.core * FF + plane.chip * quarter), (shard_rows, quarter)
    )
    gate_up_piece = lax.all_gather(gate_up_piece, "fsdp", axis=0, tiled=False)

    early_u, early_v, early_0 = plane.first(early), plane.second(early), plane.swap(early)
    out = plane.along(out_mine)
    docs, cosine, sine = positions_of(lengths, row_count)
    tables = rows_first(tables_of(cosine, sine, 2, 0))
    cotangent_slots = to_slots(cotangent_rows, send_slot, ranks)
    early_u, early_v, early_0, got_tokens, out, cotangent_slots, tables = fence(
        early_u, early_v, early_0, got_tokens, out, cotangent_slots, tables
    )
    got_cotangent = exchange(cotangent_slots)

    out = jnp.stack(out)
    early_d, early_2, early_1 = plane.second(early_u), plane.swap(early_u), plane.swap(early_v)
    out_u, out_v, out_0 = plane.first(out), plane.second(out), plane.swap(out)
    labels = got_tokens.reshape(-1, model_width + 128)[:, model_width:].astype(jnp.int32)
    safe_place = labels[:, 0] * 2 + labels[:, 1]
    is_live = labels[:, 2] == 1
    landing = jnp.where(is_live, safe_place, row_count)
    packed_f = widened(from_slots(got_tokens, landing)[:, :model_width])
    gain_rows = jnp.concatenate([gain_rows, gains.reshape(1, 2, shard_rows)], axis=0)
    gain_rows = gain_rows[(jnp.arange(depth, dtype=jnp.int32) + depth - 1 - level) % depth]
    gain_attn = widened(gain_rows[:, 0].reshape(model_width))
    gain_ffn = widened(gain_rows[:, 1].reshape(model_width))
    normed = rounded(rms_scale(packed_f, gain_attn))
    early_d, early_2, early_1, out_u, out_v, out_0, normed = fence(
        early_d, early_2, early_1, out_u, out_v, out_0, normed
    )

    early_3, out_d, out_2, out_1 = (
        plane.swap(early_d),
        plane.second(out_u),
        plane.swap(out_u),
        plane.swap(out_v),
    )
    down_piece = rest(after(down_piece, normed), level)
    early_3, out_d, out_2, out_1, down_piece = fence(early_3, out_d, out_2, out_1, down_piece)

    down_u, down_v, down_0 = (
        plane.first(down_piece),
        plane.second(down_piece),
        plane.swap(down_piece),
    )
    out_3 = plane.swap(out_d)
    query_w, kv_w = put_pieces(
        [early, early_u, early_v, early_d, early_0, early_1, early_2, early_3],
        after(at, down_piece),
        [by_parts(w_query), by_parts(w_kv)],
    )
    query_w = query_w.reshape(model_width, model_width)
    kv_w = kv_w.reshape(model_width, 2 * HD)
    query_lin = dot(normed, query_w)
    pair = pair_of(dot(normed, kv_w), cosine, sine)
    down_u, down_v, down_0, out_3, query_lin, pair = fence(
        down_u, down_v, down_0, out_3, query_lin, pair
    )

    pair_rows = with_earlier(pair, reach)
    down_2, down_1 = plane.swap(down_u), plane.swap(down_v)
    (out_w,) = put_pieces(
        [out, out_u, out_v, out_d, out_0, out_1, out_2, out_3],
        after(at, pair),
        [by_parts(w_out)],
    )
    out_w = out_w.reshape(model_width, model_width)
    down_d = down_of(after(w_down, gate_up_piece), plane.chips[3])
    gate_up_piece = rest(gate_up_piece, level)
    gate_up_piece = gate_up_piece.reshape((depth - 1) * shard_rows, quarter)
    packed_grad = from_slots(after(got_cotangent, gate_up_piece), landing)
    pair_rows, down_2, down_1, out_w, gate_up_piece, packed_grad = fence(
        pair_rows, down_2, down_1, out_w, gate_up_piece, packed_grad
    )

    gate_up_u, gate_up_v, gate_up_0 = (
        plane.first(gate_up_piece),
        plane.second(gate_up_piece),
        plane.swap(gate_up_piece),
    )
    pairs_across = pair_rows.T
    queries, mixed, totals = attend(query_lin, tables, pair_rows, pairs_across, *docs)
    hidden_state = packed_f + dot(mixed, out_w)
    ffn_in = rounded(rms_scale(hidden_state, gain_ffn))
    down_d = rest(after(down_d, ffn_in), level)
    down_3 = plane.swap(down_d)

    def chunk(slot, first_w, second_w, chunk_in, block_sum, back_sum, terms):
        facts = [plane.core, plane.chips[slot], plane.core, *plane.chips, level]
        return feed(
            jnp.stack(facts).astype(jnp.int32),
            chunk_in,
            packed_grad,
            first_w,
            second_w,
            w_gate_up,
            [down_piece, down_u, down_v, down_d, down_0, down_1, down_2, down_3],
            w_down,
            block_sum,
            back_sum,
            terms,
        )

    block_sum, back_sum, own_0, other_0, terms = chunk(
        0, gate_up_piece, gate_up_0, ffn_in, hidden_state, None, None
    )
    gate_up_u, gate_up_v, block_sum, back_sum, own_0, other_0 = fence(
        gate_up_u, gate_up_v, block_sum, back_sum, own_0, other_0
    )

    gate_up_2, gate_up_1 = plane.swap(gate_up_u), plane.swap(gate_up_v)
    gate_up_2, gate_up_1, gate_up_u, back_sum = fence(gate_up_2, gate_up_1, gate_up_u, back_sum)
    gate_up_d, swap_0 = plane.second(gate_up_u), plane.swap(other_0)
    block_sum, back_sum, own_u, other_u, terms = chunk(
        1, gate_up_u, gate_up_1, ffn_in, block_sum, back_sum, terms
    )
    gate_up_d, swap_0, block_sum, back_sum, own_u, other_u = fence(
        gate_up_d, swap_0, block_sum, back_sum, own_u, other_u
    )
    gate_up_3, swap_u = plane.swap(gate_up_d), plane.swap(other_u)
    block_sum, back_sum, own_v, other_v, terms = chunk(
        2, gate_up_v, gate_up_2, ffn_in, block_sum, back_sum, terms
    )
    gate_up_3, swap_u, block_sum, back_sum, own_v, other_v = fence(
        gate_up_3, swap_u, block_sum, back_sum, own_v, other_v
    )
    sum_v, other_v, back_sum = fence(added(own_v, swap_u), other_v, back_sum)
    from_v, swap_v = plane.second(sum_v), plane.swap(other_v)
    block_sum, back_sum, own_d, other_d, terms = chunk(
        3, gate_up_d, gate_up_3, ffn_in, block_sum, back_sum, terms
    )
    sum_u = added(own_u, swap_v)
    from_v, sum_u, block_sum, back_sum, own_d, other_d, terms = fence(
        from_v, sum_u, block_sum, back_sum, own_d, other_d, terms
    )

    from_u, swap_d = plane.first(sum_u), plane.swap(other_d)
    terms = [term.reshape(depth * half_rows, column) for term in terms]
    down_swaps = [plane.swap(term) for term in terms[4:]]
    unused_scaled, ffn_norm_pull = jax.vjp(rms_scale, hidden_state, gain_ffn)
    d_hidden_norm, grad_gain_ffn = ffn_norm_pull(back_sum)
    d_hidden = widened(packed_grad) + d_hidden_norm
    d_branch = rounded(d_hidden)
    d_mixed = rounded(dot_across(d_branch, out_w))
    sum_d = added(after(own_d, d_mixed), swap_d)
    part_d = plane.down_columns(sum_d)
    down_sums = [
        added(after(term, sum_d), down_swaps[match])
        for term, match in zip(terms[:4], (0, 2, 1, 3))
    ]
    from_u, d_branch, d_mixed, down_sums = fence(from_u, d_branch, d_mixed, down_sums)
    from_down_d, from_down_v = plane.second(down_sums[3]), plane.second(down_sums[2])
    total = added(own_0, swap_0, from_v, from_u)
    part_0 = plane.down_columns(total)
    d_query_lin, d_pairs = attend_back(
        queries, after(d_mixed, total), totals, tables, pair_rows, pairs_across, *docs
    )
    from_down_d, from_down_v, d_query_lin, d_pairs, block_sum = fence(
        from_down_d, from_down_v, d_query_lin, d_pairs, block_sum
    )

    def by_rows(grad):
        pieces = rounded(grad).reshape(depth, ranks, part_rows, grad.shape[1])
        return [
            lax.dynamic_index_in_dim(pieces, plane.sources[i], axis=1, keepdims=False)
            for i in range(8)
        ]

    d_own = owners_sum(d_pairs, row_count, reach)
    down_u = added(down_sums[1], from_down_d)
    block_slots = back_to_slots(rounded(block_sum), is_live, safe_place, ranks)
    d_own, down_u, block_slots, part_d = fence(d_own, down_u, block_slots, part_d)
    home_out = exchange(block_slots)
    from_down_u, part_d_u = plane.first(down_u), plane.first(part_d)
    grad_out = dot_rows(mixed, after(d_branch, block_slots))
    out_terms = [p.reshape(depth * part_rows, model_width) for p in by_rows(grad_out)]
    out_swaps = [plane.swap(term) for term in out_terms[4:]]
    d_kv_lin = rounded(
        jnp.concatenate([unrotate(d_own[:, :HD], cosine, sine), d_own[:, HD:]], axis=1)
    )
    grad_query = dot_rows(normed, after(d_query_lin, *out_terms))
    grad_kv = dot_rows(normed, d_kv_lin)
    d_normed = dot_across(d_query_lin, query_w) + dot_across(d_kv_lin, kv_w)
    unused_normed, attn_norm_pull = jax.vjp(rms_scale, packed_f, gain_attn)
    d_packed_norm, grad_gain_attn = attn_norm_pull(d_normed)
    grad_rows = rounded(d_hidden + d_packed_norm)
    gain_rows = jnp.concatenate(
        [
            rounded(grad_gain_attn).reshape(depth, 1, shard_rows),
            rounded(grad_gain_ffn).reshape(depth, 1, shard_rows),
        ],
        axis=2,
    )
    gain_rows = jnp.pad(gain_rows, ((0, 0), (0, 15), (0, split - 2 * shard_rows)))
    early_terms = [
        jnp.concatenate([jnp.concatenate([q, k], axis=2), gain_rows], axis=1).reshape(
            depth * (part_rows + 16), split
        )
        for q, k in zip(by_rows(grad_query), by_rows(grad_kv))
    ]
    grad_slots = back_to_slots(after(grad_rows, *early_terms), is_live, safe_place, ranks)
    from_down_u, part_d_u, early_terms, out_swaps, grad_slots, home_out = fence(
        from_down_u, part_d_u, early_terms, out_swaps, grad_slots, home_out
    )

    home_grad = exchange(grad_slots)
    part_d = plane.second(part_d_u)
    early_swaps = [plane.swap(term) for term in early_terms[4:]]
    out_d, out_v = added(out_terms[3], out_swaps[3]), added(out_terms[2], out_swaps[1])
    out_from_d, out_from_v = plane.second(out_d), plane.second(out_v)
    total = added(after(down_sums[0], out_d, out_v), from_down_v, from_down_u)
    mine_down = plane.down_columns(total)
    early_d = added(early_terms[3], early_swaps[3])
    early_v = added(early_terms[2], early_swaps[1])
    block_arrived = home_out.reshape(-1, model_width)[send_slot]
    part_d, out_from_d, out_from_v, early_d, early_v, early_swaps, part_0, block_arrived = fence(
        part_d, out_from_d, out_from_v, early_d, early_v, early_swaps, part_0, block_arrived
    )

    mine_gate_up = added(part_0, part_d)
    early_from_d, early_from_v = plane.second(early_d), plane.second(early_v)
    out_from_u = plane.first(added(out_terms[1], out_swaps[2], out_from_d))
    gate_up_u, gate_up_v, gate_up_0 = (
        plane.first(mine_gate_up),
        plane.second(mine_gate_up),
        plane.swap(mine_gate_up),
    )
    early_from_d, early_from_v, out_from_u, gate_up_u, gate_up_v, gate_up_0, home_grad = fence(
        early_from_d, early_from_v, out_from_u, gate_up_u, gate_up_v, gate_up_0, home_grad
    )

    early_from_u = plane.first(added(early_terms[1], early_swaps[2], early_from_d))
    total = added(out_terms[0], out_swaps[0], out_from_v, out_from_u)
    mine_out = plane.down_columns(total)
    gate_up_d, gate_up_2, gate_up_1 = (
        plane.second(gate_up_u),
        plane.swap(gate_up_u),
        plane.swap(gate_up_v),
    )
    grad_arrived = home_grad.reshape(-1, model_width)[send_slot]
    early_from_u, gate_up_d, gate_up_2, gate_up_1, mine_down, total, grad_arrived = fence(
        early_from_u, gate_up_d, gate_up_2, gate_up_1, mine_down, total, grad_arrived
    )

    total = added(early_terms[0], early_swaps[0], early_from_v, early_from_u)
    mine_early = plane.down_columns(total)
    gate_up_3 = plane.swap(gate_up_d)
    down_own = [mine_down, plane.first(mine_down), plane.second(mine_down)]
    total_gate_up = spread(
        [mine_gate_up, gate_up_u, gate_up_v, gate_up_d]
        + [gate_up_0, gate_up_1, gate_up_2, gate_up_3],
        after(plane.sources, total),
        (shard_rows, 2 * FF),
        lambda p: (0, (p % 2) * 4 + p // 2),
    )
    down_own, total_gate_up, mine_out = fence(down_own, total_gate_up, mine_out)

    down_own.append(plane.second(down_own[1]))
    down_swaps = [plane.swap(piece) for piece in down_own[:3]]
    out_own = [mine_out, plane.first(mine_out), plane.second(mine_out)]
    down_own, down_swaps, out_own, mine_early = fence(down_own, down_swaps, out_own, mine_early)

    down_swaps.append(plane.swap(down_own[3]))
    out_own.append(plane.second(out_own[1]))
    piece = mine_early[:part_rows]
    early_own = [piece, plane.first(piece), plane.second(piece)]
    total_down = spread(
        down_own + [down_swaps[i] for i in (0, 2, 1, 3)],
        plane.sources,
        (2 * half_rows, model_width),
        lambda p: (p % 2, p // 2),
    )
    early_own, out_own, total_down = fence(early_own, out_own, total_down)
    early_own.append(plane.second(early_own[1]))
    total_out = spread(
        out_own + second_halves(out_own),
        plane.sources,
        (shard_rows, model_width),
        lambda p: (p, 0),
    )
    early_own, total_out = fence(early_own, total_out)
    total_early = spread(
        early_own + second_halves(early_own),
        plane.sources,
        (shard_rows, split),
        lambda p: (p, 0),
    )
    return (
        block_arrived[None],
        grad_arrived[None],
        widened(mine_early[part_rows, :shard_rows]),
        total_early[:, :model_width],
        total_early[:, model_width:],
        total_out,
        widened(mine_early[part_rows, shard_rows : 2 * shard_rows]),
        total_gate_up,
        total_down,
    )


def solution(mesh):
    placed = (
        P("fsdp", "seq", None),
        P("fsdp", "seq", None),
        P("fsdp", "seq"),
        P("fsdp", None),
        P("fsdp"),
        P("fsdp", None),
        P("fsdp", None),
        P("fsdp", None),
        P("fsdp"),
        P("fsdp", None),
        P("fsdp", None),
    )
    return jax.shard_map(
        body,
        mesh=mesh,
        in_specs=placed,
        out_specs=(
            P("fsdp", "seq", None),
            P("fsdp", "seq", None),
            P("fsdp"),
            P("fsdp", None),
            P("fsdp", None),
            P("fsdp", None),
            P("fsdp"),
            P("fsdp", None),
            P("fsdp", None),
        ),
        check_vma=False,
    )
```

```python
import jax
import jax.numpy as jnp
from jax import lax
from jax.experimental import pallas as pl
from jax.experimental.pallas import tpu as pltpu
from jax.sharding import PartitionSpec as P

HD = 192
FF = 4608
WINDOW = 1024


EPSILON = 1e-06
ROPE_BASE = 10000.0
MASKED = -1e30


def passed_along(x, axis, by):
    length = lax.axis_size(axis)
    pairs = [(i, i + by) for i in range(length) if 0 <= i + by < length]
    return lax.ppermute(x, axis, pairs)


def rms_scale(values, gain):
    return values * lax.rsqrt(jnp.mean(values * values, axis=-1, keepdims=True) + EPSILON) * gain


def rotate(heads, cosine, sine):
    half = heads.shape[-1] // 2
    first_half = heads[..., :half]
    second_half = heads[..., half:]
    return jnp.concatenate(
        [first_half * cosine - second_half * sine, second_half * cosine + first_half * sine],
        axis=-1,
    )


def unrotate(heads, cosine, sine):
    half = heads.shape[-1] // 2
    first_half = heads[..., :half]
    second_half = heads[..., half:]
    return jnp.concatenate(
        [first_half * cosine + second_half * sine, second_half * cosine - first_half * sine],
        axis=-1,
    )


def angles(places, head_width):
    steps_half = jnp.arange(head_width // 2, dtype=jnp.float32)
    inverse = ROPE_BASE ** (-2.0 * steps_half / head_width)
    theta = places[:, None] * inverse[None, :]
    return (jnp.cos(theta), jnp.sin(theta))


def layout(lengths, places):
    ends = jnp.cumsum(lengths)
    starts = ends - lengths
    inside = (places[:, None] >= starts[None, :]) & (places[:, None] < ends[None, :])
    numbers = jnp.arange(1, lengths.shape[0] + 1, dtype=jnp.int32)
    document = jnp.sum(jnp.where(inside, numbers[None, :], 0), axis=1) - 1
    offset = places - jnp.sum(jnp.where(inside, starts[None, :], 0), axis=1)
    return (document, offset)


def after(x, *done):
    return lax.optimization_barrier((x, *done))[0]


def fence(*xs):
    return lax.optimization_barrier(xs)


def rounded(x):
    return x.astype(jnp.bfloat16)


def widened(x):
    return x.astype(jnp.float32)


def added(*terms):
    return rounded(sum(widened(term) for term in terms))


def dot(a, b):
    return jnp.dot(a, b, preferred_element_type=jnp.float32)


def dot_rows(a, b):
    return jnp.einsum("td,tf->df", a, b, preferred_element_type=jnp.float32)


def dot_across(a, b):
    return jnp.einsum("tf,df->td", a, b, preferred_element_type=jnp.float32)


def turn(x, tables, back):
    width = x.shape[-1]
    half = HD // 2
    later = pltpu.roll(x, width - half, axis=1)
    sooner = pltpu.roll(x, half, axis=1)
    turned = later * tables[1] + sooner * tables[2]
    return x * tables[0] - turned if back else x * tables[0] + turned


def tables_of(cosine, sine, heads, still):
    none = jnp.zeros_like(sine)
    ones = jnp.ones_like(sine)
    return (
        jnp.concatenate([cosine, cosine] * heads + [ones, ones] * still, axis=1),
        jnp.concatenate([-sine, none] * heads + [none, none] * still, axis=1),
        jnp.concatenate([none, sine] * heads + [none, none] * still, axis=1),
    )


def rows_first(arrays):
    def kernel(*refs):
        for source, target in zip(refs, refs[len(arrays) :]):
            target[...] = source[...]

    return pl.pallas_call(
        kernel, out_shape=[jax.ShapeDtypeStruct(x.shape, x.dtype) for x in arrays]
    )(*arrays)


def no_entry(doc_query, doc_key, rows, keys):
    key = lax.broadcasted_iota(jnp.int32, (keys, rows), 0)
    row = lax.broadcasted_iota(jnp.int32, (keys, rows), 1)
    gap = WINDOW + row - key
    seen = (doc_key == doc_query) & (doc_key >= 0) & (gap >= 0) & (gap < WINDOW)
    return jnp.where(seen, 0.0, MASKED)


def dot_last(a, b):
    return lax.dot_general(a, b, (((1,), (1,)), ((), ())), preferred_element_type=jnp.float32)


def attend(query_lin, tables, pairs, pairs_across, doc_query, doc_key):
    rows, width = query_lin.shape
    block = 256
    keys = WINDOW + block
    couples = width // (2 * HD)

    def kernel(q_ref, t0, t1, t2, pairs_ref, across_ref, dq_ref, dk_ref, turned_ref, mixed_ref, total_ref, bias):
        start = pl.multiple_of(pl.program_id(0) * block, block)
        window = pl.ds(start, keys)

        @pl.when(pl.program_id(1) == 0)
        def fill():
            bias[...] = no_entry(dq_ref[...], dk_ref[window, :], block, keys)

        queries = turn(q_ref[...], (t0[...], t1[...], t2[...]), False) * HD ** (-0.5)
        queries = queries.astype(jnp.bfloat16)
        turned_ref[...] = queries
        own_keys = pairs_ref[window, :][:, :HD]
        values = across_ref[pl.ds(HD, HD), window]
        mixed, totals = [], []
        for head in range(2):
            scores = dot_last(own_keys, queries[:, head * HD : (head + 1) * HD]) + bias[...]
            top = jnp.max(scores, axis=0, keepdims=True)
            weights = jnp.exp(scores - top)
            total = jnp.sum(weights, axis=0, keepdims=True)
            totals.append(top + jnp.log(total))
            mixed.append(dot(values, weights.astype(jnp.bfloat16)) * (1.0 / total))
        mixed_ref[...] = jnp.concatenate(mixed, axis=0).T.astype(jnp.bfloat16)
        total_ref[0] = jnp.concatenate(totals, axis=0)

    tile = pl.BlockSpec((block, 2 * HD), lambda i, j: (i, j))
    table = pl.BlockSpec((block, 2 * HD), lambda i, j: (i, 0))
    return pl.pallas_call(
        kernel,
        grid=(rows // block, couples),
        in_specs=[
            tile,
            table,
            table,
            table,
            pl.BlockSpec(pairs.shape, lambda i, j: (0, 0)),
            pl.BlockSpec(pairs_across.shape, lambda i, j: (0, 0)),
            pl.BlockSpec((1, block), lambda i, j: (0, i)),
            pl.BlockSpec(doc_key.shape, lambda i, j: (0, 0)),
        ],
        out_specs=[tile, tile, pl.BlockSpec((1, 2, block), lambda i, j: (j, 0, i))],
        out_shape=[
            jax.ShapeDtypeStruct((rows, width), jnp.bfloat16),
            jax.ShapeDtypeStruct((rows, width), jnp.bfloat16),
            jax.ShapeDtypeStruct((couples, 2, rows), jnp.float32),
        ],
        scratch_shapes=[pltpu.VMEM((keys, block), jnp.float32)],
        compiler_params=pltpu.CompilerParams(vmem_limit_bytes=48 * 2**20),
        cost_estimate=pl.CostEstimate(flops=10**8, bytes_accessed=10**5, transcendentals=0),
    )(query_lin, *tables, pairs, pairs_across, doc_query, doc_key)


def attend_back(queries, d_mixed, totals, tables, pairs, pairs_across, doc_query, doc_key):
    rows, width = queries.shape
    block = 256
    keys = WINDOW + block
    couples = width // (2 * HD)
    last = (rows // block - 1, couples - 1)

    def kernel(q_ref, do_ref, total_ref, t0, t1, t2, pairs_ref, across_ref, dq_ref, dk_ref, d_lin_ref, d_pairs_ref, bias, d_keys, d_values, values):
        start = pl.multiple_of(pl.program_id(0) * block, block)
        window = pl.ds(start, keys)

        @pl.when((pl.program_id(0) == 0) & (pl.program_id(1) == 0))
        def clear():
            d_keys[...] = jnp.zeros_like(d_keys)
            d_values[...] = jnp.zeros_like(d_values)
            values[...] = pairs_ref[...][:, HD:]

        @pl.when(pl.program_id(1) == 0)
        def fill():
            bias[...] = no_entry(dq_ref[...], dk_ref[window, :], block, keys)

        own_keys = pairs_ref[window, :][:, :HD]
        own_values = values[window, :]
        keys_across = across_ref[pl.ds(0, HD), window]
        d_turned = []
        for head in range(2):
            part = slice(head * HD, (head + 1) * HD)
            q, do = q_ref[...][:, part], do_ref[...][:, part]
            scores = dot_last(own_keys, q) + bias[...]
            probs = jnp.exp(scores - total_ref[0][head : head + 1, :])
            d_probs = dot_last(own_values, do)
            product = probs * d_probs
            weighted = jnp.sum(product, axis=0, keepdims=True)
            d_scores = (product - probs * weighted).astype(jnp.bfloat16)
            d_turned.append(dot(keys_across, d_scores))
            d_keys[window, :] += dot(d_scores, q)
            d_values[window, :] += dot(probs.astype(jnp.bfloat16), do)
        d_turned = jnp.concatenate(d_turned, axis=0).T
        d_lin = turn(d_turned, (t0[...], t1[...], t2[...]), True) * HD ** (-0.5)
        d_lin_ref[...] = d_lin.astype(jnp.bfloat16)

        @pl.when((pl.program_id(0) == last[0]) & (pl.program_id(1) == last[1]))
        def finish():
            d_pairs_ref[...] = jnp.concatenate([d_keys[...], d_values[...]], axis=1)

    tile = pl.BlockSpec((block, 2 * HD), lambda i, j: (i, j))
    table = pl.BlockSpec((block, 2 * HD), lambda i, j: (i, 0))
    return pl.pallas_call(
        kernel,
        grid=(rows // block, couples),
        in_specs=[
            tile,
            tile,
            pl.BlockSpec((1, 2, block), lambda i, j: (j, 0, i)),
            table,
            table,
            table,
            pl.BlockSpec(pairs.shape, lambda i, j: (0, 0)),
            pl.BlockSpec(pairs_across.shape, lambda i, j: (0, 0)),
            pl.BlockSpec((1, block), lambda i, j: (0, i)),
            pl.BlockSpec(doc_key.shape, lambda i, j: (0, 0)),
        ],
        out_specs=[tile, pl.BlockSpec(pairs.shape, lambda i, j: (0, 0))],
        out_shape=[
            jax.ShapeDtypeStruct((rows, width), jnp.bfloat16),
            jax.ShapeDtypeStruct(pairs.shape, jnp.float32),
        ],
        scratch_shapes=[
            pltpu.VMEM((keys, block), jnp.float32),
            pltpu.VMEM((pairs.shape[0], HD), jnp.float32),
            pltpu.VMEM((pairs.shape[0], HD), jnp.float32),
            pltpu.VMEM((pairs.shape[0], HD), jnp.bfloat16),
        ],
        compiler_params=pltpu.CompilerParams(vmem_limit_bytes=48 * 2**20),
        cost_estimate=pl.CostEstimate(flops=10**8, bytes_accessed=10**5, transcendentals=0),
    )(queries, d_mixed, totals, *tables, pairs, pairs_across, doc_query, doc_key)


def put_pieces(pieces, positions, shards):
    count = len(pieces)
    others, rows, unused_width = pieces[0].shape
    depth = others + 1
    widths = [shard.shape[2] for shard in shards]

    def kernel(positions_ref, *refs):
        i, j = pl.program_id(0), pl.program_id(1)
        sources, locals_, targets = (
            refs[:count],
            refs[count : count + len(shards)],
            refs[count + len(shards) :],
        )
        for at in range(count):

            @pl.when((i == at) & (j < others))
            def take():
                start = 0
                for target, width in zip(targets, widths):
                    target[0, 0] = sources[at][j, :, pl.ds(start, width)]
                    start += width

        @pl.when(j == others)
        def keep():
            for target, source in zip(targets, locals_):
                target[0, 0] = source[0]

    return pl.pallas_call(
        kernel,
        out_shape=[
            jax.ShapeDtypeStruct((depth, count, rows, width), pieces[0].dtype) for width in widths
        ],
        grid_spec=pltpu.PrefetchScalarGridSpec(
            num_scalar_prefetch=1,
            grid=(count, depth),
            in_specs=[pl.BlockSpec(p.shape, lambda i, j, at: (0, 0, 0)) for p in pieces]
            + [pl.BlockSpec((1, rows, width), lambda i, j, at: (at[i], 0, 0)) for width in widths],
            out_specs=[
                pl.BlockSpec(
                    (1, 1, rows, width),
                    lambda i, j, at: (at[count + j], at[i], 0, 0),
                )
                for width in widths
            ],
        ),
        compiler_params=pltpu.CompilerParams(vmem_limit_bytes=40 * 2**20),
    )(positions, *pieces, *shards)


def rest(x, level):
    depth = x.shape[0]
    block = (1,) + x.shape[1:]
    zeros = (0,) * (x.ndim - 1)

    def kernel(level_ref, source, target):
        target[...] = source[...]

    return pl.pallas_call(
        kernel,
        out_shape=jax.ShapeDtypeStruct((depth - 1,) + x.shape[1:], x.dtype),
        grid_spec=pltpu.PrefetchScalarGridSpec(
            num_scalar_prefetch=1,
            grid=(depth - 1,),
            in_specs=[
                pl.BlockSpec(block, lambda i, at: (lax.rem(at[0] + i + 1, depth), *zeros))
            ],
            out_specs=pl.BlockSpec(block, lambda i, at: (i, *zeros)),
        ),
    )(level[None], x)


def spread(pieces, positions, shape, place):
    count = len(pieces)
    rows, width = pieces[0].shape

    def kernel(positions_ref, *refs):
        for at in range(count):

            @pl.when(pl.program_id(0) == at)
            def take():
                refs[-1][...] = refs[at][...].astype(jnp.float32)

    return pl.pallas_call(
        kernel,
        out_shape=jax.ShapeDtypeStruct(shape, jnp.float32),
        grid_spec=pltpu.PrefetchScalarGridSpec(
            num_scalar_prefetch=1,
            grid=(count,),
            in_specs=[pl.BlockSpec((rows, width), lambda i, at: (0, 0))] * count,
            out_specs=pl.BlockSpec((rows, width), lambda i, at: place(at[i])),
        ),
        compiler_params=pltpu.CompilerParams(vmem_limit_bytes=40 * 2**20),
    )(positions, *pieces)


GELU_SCALE = 0.7978845608028654
GELU_CUBE = 0.044715


def dot_first(a, b):
    return lax.dot_general(a, b, (((0,), (0,)), ((), ())), preferred_element_type=jnp.float32)


def feed(facts, x, grad, first_w, second_w, shard, down_pieces, down_shard, block_sum, back_sum, terms):
    rows, width = x.shape
    hidden = first_w.shape[1]
    half = hidden // 2
    column = width // 4
    depth = down_pieces[0].shape[0] + 1
    level_rows = width // depth
    full = depth * hidden
    started = back_sum is not None
    pieces = 8
    f32, bf16 = jnp.float32, jnp.bfloat16

    def kernel(facts_ref, x_ref, g_ref, *refs):
        wa_in, wb_in, shard_in, down_in, block_in = refs[:5]
        down_pieces_in = refs[5 : 5 + pieces]
        refs = refs[5 + pieces :]
        if started:
            back_in = refs[0]
            refs = refs[1 + pieces :]
        block_out, back_out, ga_out, gb_out = refs[:4]
        term_out = refs[4 : 4 + pieces]
        wa, wb, wd, a, b, d, act, da, db, block, back, ga, gb, gd, sems = refs[4 + pieces :]
        chip = facts_ref[1]
        core, level = facts_ref[2], facts_ref[7]

        def rows_of(source, target, side, sem):
            copies = []
            for i in range(1, depth):
                place = pl.multiple_of(lax.rem(level + i, depth) * level_rows, 16)
                copies.append(
                    pltpu.make_async_copy(
                        source.at[pl.ds((i - 1) * level_rows, level_rows)],
                        target.at[pl.ds(place, level_rows)],
                        sem,
                    )
                )
            place = pl.multiple_of(level * level_rows, 16)
            start = pl.multiple_of(side * full + chip * hidden, 128)
            copies.append(
                pltpu.make_async_copy(
                    shard_in.at[:, pl.ds(start, hidden)],
                    target.at[pl.ds(place, level_rows)],
                    sem,
                )
            )
            return copies

        for copy in rows_of(wa_in, wa, core, sems.at[0]):
            copy.start()
        for copy in rows_of(wb_in, wb, 1 - core, sems.at[1]):
            copy.start()

        @pl.when(chip == level)
        def here():
            pltpu.make_async_copy(down_in, wd, sems.at[2]).start()

        @pl.when(chip != level)
        def elsewhere():
            step = lax.rem(chip - level + depth - 1, depth)
            for i in range(pieces):
                side = jnp.where(i < 4, core, 1 - core)
                pltpu.make_async_copy(
                    down_pieces_in[i].at[step],
                    wd.at[
                        pl.ds(pl.multiple_of(side * half, 16), half),
                        pl.ds(pl.multiple_of(facts_ref[3 + i % 4] * column, 128), column),
                    ],
                    sems.at[2],
                ).start()

        load_block = pltpu.make_async_copy(block_in, block, sems.at[3])
        load_block.start()
        if started:
            load_back = pltpu.make_async_copy(back_in, back, sems.at[4])
            load_back.start()
        pltpu.make_async_copy(wa, wa, sems.at[0]).wait()
        a[...] = dot(x_ref[...], wa[...])
        pltpu.make_async_copy(wb, wb, sems.at[1]).wait()
        b[...] = dot(x_ref[...], wb[...])
        pltpu.make_async_copy(wd, wd, sems.at[2]).wait()
        d[...] = dot_last(g_ref[...], wd[...])
        swapped = facts_ref[0] == 1

        @pl.loop(0, rows // 16)
        def glu(i):
            part = pl.ds(pl.multiple_of(i * 16, 16), 16)
            for j in range(hidden // 384):
                lanes = slice(j * 384, (j + 1) * 384)
                one, two, slope = a[part, lanes], b[part, lanes], d[part, lanes]
                gate = jnp.where(swapped, two, one)
                up = jnp.where(swapped, one, two)
                square = gate * gate
                inner = gate * (square * (GELU_SCALE * GELU_CUBE) + GELU_SCALE)
                share = 0.5 * jnp.tanh(inner) + 0.5
                gelu = gate * share
                bend = square * (6.0 * GELU_SCALE * GELU_CUBE) + 2.0 * GELU_SCALE
                rise = share + gelu * (1.0 - share) * bend
                d_gate = (slope * up) * rise
                d_up = slope * gelu
                act[part, lanes] = (gelu * up).astype(bf16)
                da[part, lanes] = jnp.where(swapped, d_up, d_gate).astype(bf16)
                db[part, lanes] = jnp.where(swapped, d_gate, d_up).astype(bf16)

        for i in range(width // 384):
            part = pl.ds(i * 384, 384)
            gb[part, :] = dot_first(x_ref[:, i * 384 : (i + 1) * 384], db[...]).astype(bf16)
            pltpu.make_async_copy(gb.at[part], gb_out.at[part], sems.at[5]).start()
        for i in range(width // 384):
            part = pl.ds(i * 384, 384)
            ga[part, :] = dot_first(x_ref[:, i * 384 : (i + 1) * 384], da[...]).astype(bf16)
            pltpu.make_async_copy(ga.at[part], ga_out.at[part], sems.at[6]).start()
        for i in range(hidden // 384):
            part = pl.ds(i * 384, 384)
            gd[part, :] = dot_first(act[:, i * 384 : (i + 1) * 384], g_ref[...]).astype(bf16)
        stores = []
        for i in range(pieces):
            side = jnp.where(i < 4, core, 1 - core)
            stores.append(
                pltpu.make_async_copy(
                    gd.at[
                        pl.ds(pl.multiple_of(side * half, 16), half),
                        pl.ds(pl.multiple_of(facts_ref[3 + i % 4] * column, 128), column),
                    ],
                    term_out[i].at[chip],
                    sems.at[7 + i],
                )
            )
        for store in stores:
            store.start()
        if started:
            load_back.wait()

            back[...] += dot_last(da[...], wa[...])
            back[...] += dot_last(db[...], wb[...])
        else:
            back[...] = dot_last(da[...], wa[...])
            back[...] += dot_last(db[...], wb[...])
        store_back = pltpu.make_async_copy(back, back_out, sems.at[15])
        store_back.start()
        load_block.wait()
        for i in range(2):
            part = pl.ds(i * (rows // 2), rows // 2)
            block[part, :] += dot(act[part, :], wd[...])
            pltpu.make_async_copy(block.at[part], block_out.at[part], sems.at[16]).start()
        for store in stores:
            store.wait()
        pltpu.make_async_copy(gb, gb_out, sems.at[5]).wait()
        pltpu.make_async_copy(ga, ga_out, sems.at[6]).wait()
        store_back.wait()
        pltpu.make_async_copy(block, block_out, sems.at[16]).wait()

    anywhere = pl.BlockSpec(memory_space=pl.ANY)
    inside = pl.BlockSpec(memory_space=pltpu.VMEM)
    operands = [facts, x, grad, first_w, second_w, shard, down_shard, block_sum, *down_pieces]
    aliases = {}
    if started:
        aliases[7] = 0
        aliases[len(operands)] = 1
        operands.append(back_sum)
        for i, term in enumerate(terms):
            aliases[len(operands)] = 4 + i
            operands.append(term)
    sums = jax.ShapeDtypeStruct((rows, width), f32)
    grads = jax.ShapeDtypeStruct((width, hidden), bf16)
    results = pl.pallas_call(
        kernel,
        in_specs=[pl.BlockSpec(memory_space=pltpu.SMEM), inside, inside]
        + [anywhere] * (len(operands) - 3),
        out_specs=[anywhere] * (4 + pieces),
        out_shape=[sums, sums, grads, grads]
        + [jax.ShapeDtypeStruct((depth, half, column), bf16)] * pieces,
        input_output_aliases=aliases,
        scratch_shapes=[
            pltpu.VMEM((width, hidden), bf16),
            pltpu.VMEM((width, hidden), bf16),
            pltpu.VMEM((hidden, width), bf16),
            pltpu.VMEM((rows, hidden), f32),
            pltpu.VMEM((rows, hidden), f32),
            pltpu.VMEM((rows, hidden), f32),
            pltpu.VMEM((rows, hidden), bf16),
            pltpu.VMEM((rows, hidden), bf16),
            pltpu.VMEM((rows, hidden), bf16),
            pltpu.VMEM((rows, width), f32),
            pltpu.VMEM((rows, width), f32),
            pltpu.VMEM((width, hidden), bf16),
            pltpu.VMEM((width, hidden), bf16),
            pltpu.VMEM((hidden, width), bf16),
            pltpu.SemaphoreType.DMA((17,)),
        ],
        compiler_params=pltpu.CompilerParams(vmem_limit_bytes=56 * 2**20),
        cost_estimate=pl.CostEstimate(flops=10**8, bytes_accessed=10**5, transcendentals=0),
    )(*operands)
    return results[0], results[1], results[2], results[3], results[4:]


class Plane:
    def __init__(self):
        self.me = lax.axis_index("seq")
        self.core = self.me % 2
        self.chip = self.me // 2
        first = jnp.where(self.core == 0, 1, 2)
        self.chips = [self.chip, self.chip ^ first, self.chip ^ (3 - first), self.chip ^ 3]
        self.first_pairs = [(i, i ^ (2 if i % 2 == 0 else 4)) for i in range(8)]
        self.second_pairs = [(i, i ^ (4 if i % 2 == 0 else 2)) for i in range(8)]
        self.core_pairs = [(i, i ^ 1) for i in range(8)]
        self.sources = jnp.stack(
            [chip * 2 + self.core for chip in self.chips]
            + [chip * 2 + 1 - self.core for chip in self.chips]
        )

    def first(self, x):
        return lax.ppermute(x, "seq", self.first_pairs)

    def second(self, x):
        return lax.ppermute(x, "seq", self.second_pairs)

    def along(self, x):
        depth = lax.axis_size("fsdp")
        return [
            lax.ppermute(x, "fsdp", [((i + k) % depth, i) for i in range(depth)])
            for k in range(1, depth)
        ]

    def swap(self, x):
        return lax.ppermute(x, "seq", self.core_pairs)

    def down_columns(self, x):
        return lax.psum_scatter(x, "fsdp", scatter_dimension=0, tiled=True)


def places_of(arrival_order, ranks):
    row_count = arrival_order.shape[1]
    capacity = 2 * row_count // ranks
    arrived_at = arrival_order[0]
    owner = arrived_at // row_count
    owner_hits = (owner[:, None] == jnp.arange(ranks, dtype=jnp.int32)[None, :]).astype(jnp.int32)
    within = jnp.sum(jnp.cumsum(owner_hits, axis=0) * owner_hits, axis=1) - 1
    return owner * capacity + within, arrived_at % row_count


def to_slots(rows, slots, ranks, empty=0):
    capacity = 2 * rows.shape[0] // ranks
    out = jnp.full((ranks * capacity,) + rows.shape[1:], empty, rows.dtype)
    return out.at[slots].set(rows).reshape((ranks, capacity) + rows.shape[1:])


def from_slots(slots, landing):
    flat = slots.reshape((-1, slots.shape[-1]))
    out = jnp.zeros((flat.shape[0] // 2, flat.shape[1]), flat.dtype)
    return out.at[landing].set(flat, mode="drop")


def back_to_slots(rows, safe_place, ranks):
    return rows[safe_place].reshape(ranks, -1, rows.shape[1])


def exchange(x):
    return lax.all_to_all(x, "seq", split_axis=0, concat_axis=0, tiled=True)


def positions_of(lengths, row_count):
    position = lax.axis_index("seq")
    places = position * row_count + jnp.arange(row_count, dtype=jnp.int32)
    doc_query, offset_query = layout(lengths[0], places)
    key_places = (
        position * row_count - WINDOW + jnp.arange(WINDOW + row_count, dtype=jnp.int32)
    )
    doc_key, unused_offset = layout(lengths[0], key_places)
    cosine, sine = angles(offset_query.astype(jnp.float32), HD)
    return (doc_query[None, :], doc_key[:, None]), cosine, sine


def pair_of(kv_lin, cosine, sine):
    own_keys = rounded(rotate(kv_lin[:, :HD], cosine, sine))
    return jnp.concatenate([own_keys, rounded(kv_lin[:, HD:])], axis=1)


def with_earlier(pair, reach):
    return jnp.concatenate(
        [passed_along(pair, "seq", distance) for distance in range(reach, 0, -1)] + [pair], axis=0
    )


def owners_sum(d_pairs, row_count, reach):
    parts = [
        passed_along(
            rounded(d_pairs[(reach - distance) * row_count :][:row_count]), "seq", -distance
        )
        for distance in range(reach, 0, -1)
    ]
    own = d_pairs[reach * row_count :]
    for part in parts:
        own = own + widened(part)
    return own


def body(*operands):
    return square_body(*operands) if lax.axis_size("seq") == 8 else plain_body(*operands)


def plain_body(
    tokens,
    cotangent,
    arrival_order,
    lengths,
    norm_gain,
    w_query,
    w_kv,
    w_out,
    ffn_gain,
    w_gate_up,
    w_down,
):
    row_count = tokens.shape[1]
    ranks = lax.axis_size("seq")
    reach = WINDOW // row_count
    position = lax.axis_index("seq")

    def whole(shard):
        part = shard.shape[0] // ranks
        mine = lax.dynamic_slice_in_dim(shard, position * part, part, axis=0)
        return lax.all_gather(mine, ("fsdp", "seq"), axis=0, tiled=True)

    def summed(grad):
        mine = lax.psum_scatter(rounded(grad), ("fsdp", "seq"), scatter_dimension=0, tiled=True)
        return widened(lax.all_gather(mine, "seq", axis=0, tiled=True))

    send_slot, send_place = places_of(arrival_order, ranks)
    got_tokens = exchange(to_slots(tokens[0], send_slot, ranks))
    got_cotangent = exchange(to_slots(cotangent[0], send_slot, ranks))
    recv_place = exchange(to_slots(send_place, send_slot, ranks, -1)).reshape(-1)
    is_live = recv_place >= 0
    landing = jnp.where(is_live, recv_place, row_count)
    safe_place = jnp.where(is_live, recv_place, 0)
    packed_f = widened(from_slots(got_tokens, landing))
    packed_grad = from_slots(got_cotangent, landing)
    query_w, kv_w, out_w, down_w, gate_up_w = (
        whole(w_query),
        whole(w_kv),
        whole(w_out),
        whole(w_down),
        whole(w_gate_up),
    )
    gain_attn, gain_ffn = (
        widened(lax.all_gather(gain, "fsdp", axis=0, tiled=True)) for gain in (norm_gain, ffn_gain)
    )
    docs, cosine, sine = positions_of(lengths, row_count)
    tables = tables_of(cosine, sine, 2, 0)

    normed = rounded(rms_scale(packed_f, gain_attn))
    pair_rows = with_earlier(pair_of(dot(normed, kv_w), cosine, sine), reach)
    queries, mixed, totals = attend(dot(normed, query_w), tables, pair_rows, pair_rows.T, *docs)
    hidden_state = packed_f + dot(mixed, out_w)
    ffn_in = rounded(rms_scale(hidden_state, gain_ffn))
    gate, up = dot(ffn_in, gate_up_w[:, :FF]), dot(ffn_in, gate_up_w[:, FF:])
    activated, pull = jax.vjp(lambda g, u: jax.nn.gelu(g, approximate=True) * u, gate, up)
    activated = rounded(activated)
    block_rows = rounded(hidden_state + dot(activated, down_w))

    d_gate, d_up = pull(dot_across(packed_grad, down_w))
    d_gate_up = jnp.concatenate([rounded(d_gate), rounded(d_up)], axis=1)
    unused_scaled, ffn_norm_pull = jax.vjp(rms_scale, hidden_state, gain_ffn)
    d_hidden_norm, grad_gain_ffn = ffn_norm_pull(dot_across(d_gate_up, gate_up_w))
    d_hidden = widened(packed_grad) + d_hidden_norm
    d_branch = rounded(d_hidden)
    d_mixed = rounded(dot_across(d_branch, out_w))
    d_query_lin, d_pairs = attend_back(
        queries, d_mixed, totals, tables, pair_rows, pair_rows.T, *docs
    )
    d_own = owners_sum(d_pairs, row_count, reach)
    d_kv_lin = rounded(
        jnp.concatenate([unrotate(d_own[:, :HD], cosine, sine), d_own[:, HD:]], axis=1)
    )
    d_normed = dot_across(d_query_lin, query_w) + dot_across(d_kv_lin, kv_w)
    unused_normed, attn_norm_pull = jax.vjp(rms_scale, packed_f, gain_attn)
    d_packed_norm, grad_gain_attn = attn_norm_pull(d_normed)
    grad_rows = rounded(d_hidden + d_packed_norm)
    block_arrived, grad_arrived = (
        exchange(back_to_slots(rows, safe_place, ranks)).reshape(-1, rows.shape[1])[
            send_slot
        ]
        for rows in (block_rows, grad_rows)
    )
    total_gain_attn, total_gain_ffn = (
        lax.psum(lax.psum_scatter(gain, "fsdp", scatter_dimension=0, tiled=True), "seq")
        for gain in (grad_gain_attn, grad_gain_ffn)
    )
    return (
        block_arrived[None],
        grad_arrived[None],
        total_gain_attn,
        summed(dot_rows(normed, d_query_lin)),
        summed(dot_rows(normed, d_kv_lin)),
        summed(dot_rows(mixed, d_branch)),
        total_gain_ffn,
        summed(dot_rows(ffn_in, d_gate_up)),
        summed(dot_rows(activated, packed_grad)),
    )


def square_body(
    tokens,
    cotangent,
    arrival_order,
    lengths,
    norm_gain,
    w_query,
    w_kv,
    w_out,
    ffn_gain,
    w_gate_up,
    w_down,
):
    row_count = tokens.shape[1]
    model_width = tokens.shape[2]
    ranks = lax.axis_size("seq")
    depth = lax.axis_size("fsdp")
    reach = WINDOW // row_count
    shard_rows = w_query.shape[0]
    part_rows = shard_rows // ranks
    quarter = FF // 4
    column = model_width // 4
    half_rows = w_down.shape[0] // 2
    split = model_width + 2 * HD
    plane = Plane()
    level = lax.axis_index("fsdp").astype(jnp.int32)
    levels = (level + 1 + jnp.arange(depth, dtype=jnp.int32)) % depth
    at = jnp.concatenate([plane.sources, levels]).astype(jnp.int32)

    def my_rows(shard):
        return lax.dynamic_slice_in_dim(shard, plane.me * part_rows, part_rows, axis=0)

    def by_parts(shard):
        return shard.reshape(ranks, part_rows, shard.shape[1])

    def second_halves(slots):
        return [plane.swap(slots[i]) for i in (0, 2, 1, 3)]


    gains = jnp.concatenate([norm_gain, ffn_gain]).reshape(part_rows, -1)
    gain_width = gains.shape[1]
    early = plane.along(
        jnp.concatenate(
            [my_rows(w_query), my_rows(w_kv), jnp.pad(gains, ((0, 0), (0, 128 - gain_width)))],
            axis=1,
        )
    )
    send_slot, send_place = places_of(arrival_order, ranks)
    labels = jnp.stack([send_place // 2, send_place % 2, jnp.ones_like(send_place)], axis=1)
    labels = jnp.pad(labels.astype(jnp.bfloat16), ((0, 0), (0, 125)))
    token_slots = to_slots(jnp.concatenate([tokens[0], labels], axis=1), send_slot, ranks)
    got_tokens = exchange(token_slots)
    *early, cotangent_rows, out_mine, down_mine, gate_up_mine = fence(
        *early, after(cotangent[0], token_slots), my_rows(w_out), w_down, w_gate_up
    )
    early = jnp.stack(early)
    gain_rows = early[:, :, split : split + gain_width].reshape(depth - 1, 2, shard_rows)
    early = early[:, :, :split]

    def down_of(shard, chip):
        piece = lax.dynamic_slice(
            shard, (plane.core * half_rows, chip * column), (half_rows, column)
        )
        return lax.all_gather(piece, "fsdp", axis=0, tiled=False)

    down_piece = down_of(down_mine, plane.chip)
    gate_up_piece = lax.dynamic_slice(
        gate_up_mine, (0, plane.core * FF + plane.chip * quarter), (shard_rows, quarter)
    )
    gate_up_piece = lax.all_gather(gate_up_piece, "fsdp", axis=0, tiled=False)

    early_u, early_v, early_0 = plane.first(early), plane.second(early), plane.swap(early)
    out = plane.along(out_mine)
    docs, cosine, sine = positions_of(lengths, row_count)
    tables = rows_first(tables_of(cosine, sine, 2, 0))
    cotangent_slots = to_slots(cotangent_rows, send_slot, ranks)
    early_u, early_v, early_0, got_tokens, out, cotangent_slots, tables = fence(
        early_u, early_v, early_0, got_tokens, out, cotangent_slots, tables
    )
    got_cotangent = exchange(cotangent_slots)

    out = jnp.stack(out)
    early_d, early_2, early_1 = plane.second(early_u), plane.swap(early_u), plane.swap(early_v)
    out_u, out_v, out_0 = plane.first(out), plane.second(out), plane.swap(out)
    labels = got_tokens.reshape(-1, model_width + 128)[:, model_width:].astype(jnp.int32)
    safe_place = labels[:, 0] * 2 + labels[:, 1]
    is_live = labels[:, 2] == 1
    landing = jnp.where(is_live, safe_place, row_count)
    packed_f = widened(from_slots(got_tokens, landing)[:, :model_width])
    gain_rows = jnp.concatenate([gain_rows, gains.reshape(1, 2, shard_rows)], axis=0)
    gain_rows = gain_rows[(jnp.arange(depth, dtype=jnp.int32) + depth - 1 - level) % depth]
    gain_attn = widened(gain_rows[:, 0].reshape(model_width))
    gain_ffn = widened(gain_rows[:, 1].reshape(model_width))
    normed = rounded(rms_scale(packed_f, gain_attn))
    early_d, early_2, early_1, out_u, out_v, out_0, normed = fence(
        early_d, early_2, early_1, out_u, out_v, out_0, normed
    )

    early_3, out_d, out_2, out_1 = (
        plane.swap(early_d),
        plane.second(out_u),
        plane.swap(out_u),
        plane.swap(out_v),
    )
    down_piece = rest(after(down_piece, normed), level)
    early_3, out_d, out_2, out_1, down_piece = fence(early_3, out_d, out_2, out_1, down_piece)

    down_u, down_v, down_0 = (
        plane.first(down_piece),
        plane.second(down_piece),
        plane.swap(down_piece),
    )
    out_3 = plane.swap(out_d)
    query_w, kv_w = put_pieces(
        [early, early_u, early_v, early_d, early_0, early_1, early_2, early_3],
        after(at, down_piece),
        [by_parts(w_query), by_parts(w_kv)],
    )
    query_w = query_w.reshape(model_width, model_width)
    kv_w = kv_w.reshape(model_width, 2 * HD)
    query_lin = dot(normed, query_w)
    pair = pair_of(dot(normed, kv_w), cosine, sine)
    (out_w,) = put_pieces(
        [out, out_u, out_v, out_d, out_0, out_1, out_2, out_3],
        after(at, pair),
        [by_parts(w_out)],
    )
    out_w = out_w.reshape(model_width, model_width)
    down_u, down_v, down_0, out_w, query_lin, pair = fence(
        down_u, down_v, down_0, out_w, query_lin, pair
    )

    pair_rows = with_earlier(pair, reach)
    down_2, down_1 = plane.swap(down_u), plane.swap(down_v)
    down_d = down_of(after(w_down, gate_up_piece), plane.chips[3])
    gate_up_piece = rest(gate_up_piece, level)
    gate_up_piece = gate_up_piece.reshape((depth - 1) * shard_rows, quarter)
    packed_grad = from_slots(after(got_cotangent, gate_up_piece), landing)
    pair_rows, down_2, down_1, gate_up_piece, packed_grad = fence(
        pair_rows, down_2, down_1, gate_up_piece, packed_grad
    )

    gate_up_u, gate_up_v, gate_up_0 = (
        plane.first(gate_up_piece),
        plane.second(gate_up_piece),
        plane.swap(gate_up_piece),
    )
    pairs_across = pair_rows.T
    queries, mixed, totals = attend(query_lin, tables, pair_rows, pairs_across, *docs)
    hidden_state = packed_f + dot(mixed, out_w)
    ffn_in = rounded(rms_scale(hidden_state, gain_ffn))
    down_d = rest(after(down_d, ffn_in), level)
    down_3 = plane.swap(down_d)

    def chunk(slot, first_w, second_w, chunk_in, block_sum, back_sum, terms):
        facts = [plane.core, plane.chips[slot], plane.core, *plane.chips, level]
        return feed(
            jnp.stack(facts).astype(jnp.int32),
            chunk_in,
            packed_grad,
            first_w,
            second_w,
            w_gate_up,
            [down_piece, down_u, down_v, down_d, down_0, down_1, down_2, down_3],
            w_down,
            block_sum,
            back_sum,
            terms,
        )

    block_sum, back_sum, own_0, other_0, terms = chunk(
        0, gate_up_piece, gate_up_0, ffn_in, hidden_state, None, None
    )
    gate_up_u, gate_up_v, block_sum, back_sum, own_0, other_0 = fence(
        gate_up_u, gate_up_v, block_sum, back_sum, own_0, other_0
    )

    gate_up_2, gate_up_1 = plane.swap(gate_up_u), plane.swap(gate_up_v)
    gate_up_2, gate_up_1, gate_up_u, back_sum = fence(gate_up_2, gate_up_1, gate_up_u, back_sum)
    gate_up_d, swap_0 = plane.second(gate_up_u), plane.swap(other_0)
    block_sum, back_sum, own_u, other_u, terms = chunk(
        1, gate_up_u, gate_up_1, ffn_in, block_sum, back_sum, terms
    )
    gate_up_d, swap_0, block_sum, back_sum, own_u, other_u = fence(
        gate_up_d, swap_0, block_sum, back_sum, own_u, other_u
    )
    gate_up_3, swap_u = plane.swap(gate_up_d), plane.swap(other_u)
    block_sum, back_sum, own_v, other_v, terms = chunk(
        2, gate_up_v, gate_up_2, ffn_in, block_sum, back_sum, terms
    )
    gate_up_3, swap_u, block_sum, back_sum, own_v, other_v = fence(
        gate_up_3, swap_u, block_sum, back_sum, own_v, other_v
    )
    sum_v, other_v, back_sum = fence(added(own_v, swap_u), other_v, back_sum)
    from_v, swap_v = plane.second(sum_v), plane.swap(other_v)
    block_sum, back_sum, own_d, other_d, terms = chunk(
        3, gate_up_d, gate_up_3, ffn_in, block_sum, back_sum, terms
    )
    sum_u = added(own_u, swap_v)
    from_v, sum_u, block_sum, back_sum, own_d, other_d, terms = fence(
        from_v, sum_u, block_sum, back_sum, own_d, other_d, terms
    )

    from_u, swap_d = plane.first(sum_u), plane.swap(other_d)
    terms = [term.reshape(depth * half_rows, column) for term in terms]
    down_swaps = [plane.swap(term) for term in terms[4:]]
    unused_scaled, ffn_norm_pull = jax.vjp(rms_scale, hidden_state, gain_ffn)
    d_hidden_norm, grad_gain_ffn = ffn_norm_pull(back_sum)
    d_hidden = widened(packed_grad) + d_hidden_norm
    d_branch = rounded(d_hidden)
    d_mixed = rounded(dot_across(d_branch, out_w))
    sum_d = added(after(own_d, d_mixed), swap_d)
    part_d = plane.down_columns(sum_d)
    down_sums = [
        added(after(term, sum_d), down_swaps[match])
        for term, match in zip(terms[:4], (0, 2, 1, 3))
    ]
    from_u, d_branch, d_mixed, down_sums = fence(from_u, d_branch, d_mixed, down_sums)
    from_down_d, from_down_v = plane.second(down_sums[3]), plane.second(down_sums[2])
    total = added(own_0, swap_0, from_v, from_u)
    part_0 = plane.down_columns(total)
    d_query_lin, d_pairs = attend_back(
        queries, after(d_mixed, total), totals, tables, pair_rows, pairs_across, *docs
    )
    from_down_d, from_down_v, d_query_lin, d_pairs, block_sum, part_d = fence(
        from_down_d, from_down_v, d_query_lin, d_pairs, block_sum, part_d
    )
    part_d_u = plane.first(part_d)

    def by_rows(grad):
        pieces = rounded(grad).reshape(depth, ranks, part_rows, grad.shape[1])
        return [
            lax.dynamic_index_in_dim(pieces, plane.sources[i], axis=1, keepdims=False)
            for i in range(8)
        ]

    d_own = owners_sum(d_pairs, row_count, reach)
    down_u = added(down_sums[1], from_down_d)
    block_slots = back_to_slots(rounded(block_sum), safe_place, ranks)
    d_own, down_u, block_slots, part_d_u = fence(d_own, down_u, block_slots, part_d_u)
    home_out = exchange(block_slots)
    from_down_u, part_d = plane.first(down_u), plane.second(part_d_u)
    grad_out = dot_rows(mixed, after(d_branch, block_slots))
    out_terms = [p.reshape(depth * part_rows, model_width) for p in by_rows(grad_out)]
    out_swaps = [plane.swap(term) for term in out_terms[4:]]
    d_kv_lin = rounded(
        jnp.concatenate([unrotate(d_own[:, :HD], cosine, sine), d_own[:, HD:]], axis=1)
    )
    grad_query = dot_rows(normed, after(d_query_lin, *out_terms))
    grad_kv = dot_rows(normed, d_kv_lin)
    d_normed = dot_across(d_query_lin, query_w) + dot_across(d_kv_lin, kv_w)
    unused_normed, attn_norm_pull = jax.vjp(rms_scale, packed_f, gain_attn)
    d_packed_norm, grad_gain_attn = attn_norm_pull(d_normed)
    grad_rows = rounded(d_hidden + d_packed_norm)
    gain_rows = jnp.concatenate(
        [
            rounded(grad_gain_attn).reshape(depth, 1, shard_rows),
            rounded(grad_gain_ffn).reshape(depth, 1, shard_rows),
        ],
        axis=2,
    )
    gain_rows = jnp.pad(gain_rows, ((0, 0), (0, 15), (0, split - 2 * shard_rows)))
    early_terms = [
        jnp.concatenate([jnp.concatenate([q, k], axis=2), gain_rows], axis=1).reshape(
            depth * (part_rows + 16), split
        )
        for q, k in zip(by_rows(grad_query), by_rows(grad_kv))
    ]
    grad_slots = back_to_slots(after(grad_rows, *early_terms), safe_place, ranks)
    from_down_u, part_d, early_terms, out_swaps, grad_slots, home_out = fence(
        from_down_u, part_d, early_terms, out_swaps, grad_slots, home_out
    )

    home_grad = exchange(grad_slots)
    early_swaps = [plane.swap(term) for term in early_terms[4:]]
    out_d, out_v = added(out_terms[3], out_swaps[3]), added(out_terms[2], out_swaps[1])
    out_from_d, out_from_v = plane.second(out_d), plane.second(out_v)
    total = added(after(down_sums[0], out_d, out_v), from_down_v, from_down_u)
    mine_down = plane.down_columns(total)
    early_d = added(early_terms[3], early_swaps[3])
    early_v = added(early_terms[2], early_swaps[1])
    block_arrived = home_out.reshape(-1, model_width)[send_slot]
    out_from_d, out_from_v, early_d, early_v, early_swaps, part_0, block_arrived = fence(
        out_from_d, out_from_v, early_d, early_v, early_swaps, part_0, block_arrived
    )

    mine_gate_up = added(part_0, part_d)
    early_from_d, early_from_v = plane.second(early_d), plane.second(early_v)
    out_from_u = plane.first(added(out_terms[1], out_swaps[2], out_from_d))
    gate_up_u, gate_up_v, gate_up_0 = (
        plane.first(mine_gate_up),
        plane.second(mine_gate_up),
        plane.swap(mine_gate_up),
    )
    early_from_d, early_from_v, out_from_u, gate_up_u, gate_up_v, gate_up_0, home_grad = fence(
        early_from_d, early_from_v, out_from_u, gate_up_u, gate_up_v, gate_up_0, home_grad
    )

    early_from_u = plane.first(added(early_terms[1], early_swaps[2], early_from_d))
    total = added(out_terms[0], out_swaps[0], out_from_v, out_from_u)
    mine_out = plane.down_columns(total)
    gate_up_d, gate_up_2, gate_up_1 = (
        plane.second(gate_up_u),
        plane.swap(gate_up_u),
        plane.swap(gate_up_v),
    )
    grad_arrived = home_grad.reshape(-1, model_width)[send_slot]
    early_from_u, gate_up_d, gate_up_2, gate_up_1, mine_down, total, grad_arrived = fence(
        early_from_u, gate_up_d, gate_up_2, gate_up_1, mine_down, total, grad_arrived
    )

    total = added(early_terms[0], early_swaps[0], early_from_v, early_from_u)
    mine_early = plane.down_columns(total)
    gate_up_3 = plane.swap(gate_up_d)
    down_own = [mine_down, plane.first(mine_down), plane.second(mine_down)]
    total_gate_up = spread(
        [mine_gate_up, gate_up_u, gate_up_v, gate_up_d]
        + [gate_up_0, gate_up_1, gate_up_2, gate_up_3],
        after(plane.sources, total),
        (shard_rows, 2 * FF),
        lambda p: (0, (p % 2) * 4 + p // 2),
    )
    down_own, total_gate_up, mine_out = fence(down_own, total_gate_up, mine_out)

    down_own.append(plane.second(down_own[1]))
    down_swaps = [plane.swap(piece) for piece in down_own[:3]]
    out_own = [mine_out, plane.first(mine_out), plane.second(mine_out)]
    down_own, down_swaps, out_own, mine_early = fence(down_own, down_swaps, out_own, mine_early)

    down_swaps.append(plane.swap(down_own[3]))
    out_own.append(plane.second(out_own[1]))
    piece = mine_early[:part_rows]
    early_own = [piece, plane.first(piece), plane.second(piece)]
    total_down = spread(
        down_own + [down_swaps[i] for i in (0, 2, 1, 3)],
        plane.sources,
        (2 * half_rows, model_width),
        lambda p: (p % 2, p // 2),
    )
    early_own, out_own, total_down = fence(early_own, out_own, total_down)
    early_own.append(plane.second(early_own[1]))
    total_out = spread(
        out_own + second_halves(out_own),
        plane.sources,
        (shard_rows, model_width),
        lambda p: (p, 0),
    )
    early_own, total_out = fence(early_own, total_out)
    total_early = spread(
        early_own + second_halves(early_own),
        plane.sources,
        (shard_rows, split),
        lambda p: (p, 0),
    )
    return (
        block_arrived[None],
        grad_arrived[None],
        widened(mine_early[part_rows, :shard_rows]),
        total_early[:, :model_width],
        total_early[:, model_width:],
        total_out,
        widened(mine_early[part_rows, shard_rows : 2 * shard_rows]),
        total_gate_up,
        total_down,
    )


def solution(mesh):
    placed = (
        P("fsdp", "seq", None),
        P("fsdp", "seq", None),
        P("fsdp", "seq"),
        P("fsdp", None),
        P("fsdp"),
        P("fsdp", None),
        P("fsdp", None),
        P("fsdp", None),
        P("fsdp"),
        P("fsdp", None),
        P("fsdp", None),
    )
    return jax.shard_map(
        body,
        mesh=mesh,
        in_specs=placed,
        out_specs=(
            P("fsdp", "seq", None),
            P("fsdp", "seq", None),
            P("fsdp"),
            P("fsdp", None),
            P("fsdp", None),
            P("fsdp", None),
            P("fsdp"),
            P("fsdp", None),
            P("fsdp", None),
        ),
        check_vma=False,
    )
```

```python
import jax
import jax.numpy as jnp
from jax import lax
from jax.experimental import pallas as pl
from jax.experimental.pallas import tpu as pltpu
from jax.sharding import PartitionSpec as P

HD = 192
FF = 4608
WINDOW = 1024


EPSILON = 1e-06
ROPE_BASE = 10000.0
MASKED = -1e30


def passed_along(x, axis, by):
    length = lax.axis_size(axis)
    pairs = [(i, i + by) for i in range(length) if 0 <= i + by < length]
    return lax.ppermute(x, axis, pairs)


def rms_scale(values, gain):
    return values * lax.rsqrt(jnp.mean(values * values, axis=-1, keepdims=True) + EPSILON) * gain


def rotate(heads, cosine, sine):
    half = heads.shape[-1] // 2
    first_half = heads[..., :half]
    second_half = heads[..., half:]
    return jnp.concatenate(
        [first_half * cosine - second_half * sine, second_half * cosine + first_half * sine],
        axis=-1,
    )


def unrotate(heads, cosine, sine):
    half = heads.shape[-1] // 2
    first_half = heads[..., :half]
    second_half = heads[..., half:]
    return jnp.concatenate(
        [first_half * cosine + second_half * sine, second_half * cosine - first_half * sine],
        axis=-1,
    )


def angles(places, head_width):
    steps_half = jnp.arange(head_width // 2, dtype=jnp.float32)
    inverse = ROPE_BASE ** (-2.0 * steps_half / head_width)
    theta = places[:, None] * inverse[None, :]
    return (jnp.cos(theta), jnp.sin(theta))


def layout(lengths, places):
    ends = jnp.cumsum(lengths)
    starts = ends - lengths
    inside = (places[:, None] >= starts[None, :]) & (places[:, None] < ends[None, :])
    numbers = jnp.arange(1, lengths.shape[0] + 1, dtype=jnp.int32)
    document = jnp.sum(jnp.where(inside, numbers[None, :], 0), axis=1) - 1
    offset = places - jnp.sum(jnp.where(inside, starts[None, :], 0), axis=1)
    return (document, offset)


def after(x, *done):
    return lax.optimization_barrier((x, *done))[0]


def fence(*xs):
    return lax.optimization_barrier(xs)


def rounded(x):
    return x.astype(jnp.bfloat16)


def widened(x):
    return x.astype(jnp.float32)


def added(*terms):
    return rounded(sum(widened(term) for term in terms))


def added_apart(*terms):
    rows, width = terms[0].shape
    steps = 4

    def kernel(*refs):
        refs[-1][...] = rounded(sum(widened(ref[...]) for ref in refs[:-1]))

    block = pl.BlockSpec((rows // steps, width), lambda i: (i, 0))
    return pl.pallas_call(
        kernel,
        grid=(steps,),
        in_specs=[block] * len(terms),
        out_specs=block,
        out_shape=jax.ShapeDtypeStruct((rows, width), jnp.bfloat16),
        compiler_params=pltpu.CompilerParams(vmem_limit_bytes=32 * 2**20),
        cost_estimate=pl.CostEstimate(flops=10**6, bytes_accessed=10**5, transcendentals=0),
    )(*terms)


def dot(a, b):
    return jnp.dot(a, b, preferred_element_type=jnp.float32)


def dot_rows(a, b):
    return jnp.einsum("td,tf->df", a, b, preferred_element_type=jnp.float32)


def dot_across(a, b):
    return jnp.einsum("tf,df->td", a, b, preferred_element_type=jnp.float32)


def turn(x, tables, back):
    width = x.shape[-1]
    half = HD // 2
    later = pltpu.roll(x, width - half, axis=1)
    sooner = pltpu.roll(x, half, axis=1)
    turned = later * tables[1] + sooner * tables[2]
    return x * tables[0] - turned if back else x * tables[0] + turned


def tables_of(cosine, sine, heads, still):
    none = jnp.zeros_like(sine)
    ones = jnp.ones_like(sine)
    return (
        jnp.concatenate([cosine, cosine] * heads + [ones, ones] * still, axis=1),
        jnp.concatenate([-sine, none] * heads + [none, none] * still, axis=1),
        jnp.concatenate([none, sine] * heads + [none, none] * still, axis=1),
    )


def rows_first(arrays):
    def kernel(*refs):
        for source, target in zip(refs, refs[len(arrays) :]):
            target[...] = source[...]

    return pl.pallas_call(
        kernel, out_shape=[jax.ShapeDtypeStruct(x.shape, x.dtype) for x in arrays]
    )(*arrays)


def no_entry(doc_query, doc_key, rows, keys):
    key = lax.broadcasted_iota(jnp.int32, (keys, rows), 0)
    row = lax.broadcasted_iota(jnp.int32, (keys, rows), 1)
    gap = WINDOW + row - key
    seen = (doc_key == doc_query) & (doc_key >= 0) & (gap >= 0) & (gap < WINDOW)
    return jnp.where(seen, 0.0, MASKED)


def dot_last(a, b):
    return lax.dot_general(a, b, (((1,), (1,)), ((), ())), preferred_element_type=jnp.float32)


def attend(query_lin, tables, pairs, pairs_across, doc_query, doc_key):
    rows, width = query_lin.shape
    block = 256
    keys = WINDOW + block
    couples = width // (2 * HD)

    def kernel(q_ref, t0, t1, t2, pairs_ref, across_ref, dq_ref, dk_ref, turned_ref, mixed_ref, total_ref, bias):
        start = pl.multiple_of(pl.program_id(0) * block, block)
        window = pl.ds(start, keys)

        @pl.when(pl.program_id(1) == 0)
        def fill():
            bias[...] = no_entry(dq_ref[...], dk_ref[window, :], block, keys)

        queries = turn(q_ref[...], (t0[...], t1[...], t2[...]), False) * HD ** (-0.5)
        queries = queries.astype(jnp.bfloat16)
        turned_ref[...] = queries
        own_keys = pairs_ref[window, :][:, :HD]
        values = across_ref[pl.ds(HD, HD), window]
        mixed, totals = [], []
        for head in range(2):
            scores = dot_last(own_keys, queries[:, head * HD : (head + 1) * HD]) + bias[...]
            top = jnp.max(scores, axis=0, keepdims=True)
            weights = jnp.exp(scores - top)
            total = jnp.sum(weights, axis=0, keepdims=True)
            totals.append(top + jnp.log(total))
            mixed.append(dot(values, weights.astype(jnp.bfloat16)) * (1.0 / total))
        mixed_ref[...] = jnp.concatenate(mixed, axis=0).T.astype(jnp.bfloat16)
        total_ref[0] = jnp.concatenate(totals, axis=0)

    tile = pl.BlockSpec((block, 2 * HD), lambda i, j: (i, j))
    table = pl.BlockSpec((block, 2 * HD), lambda i, j: (i, 0))
    return pl.pallas_call(
        kernel,
        grid=(rows // block, couples),
        in_specs=[
            tile,
            table,
            table,
            table,
            pl.BlockSpec(pairs.shape, lambda i, j: (0, 0)),
            pl.BlockSpec(pairs_across.shape, lambda i, j: (0, 0)),
            pl.BlockSpec((1, block), lambda i, j: (0, i)),
            pl.BlockSpec(doc_key.shape, lambda i, j: (0, 0)),
        ],
        out_specs=[tile, tile, pl.BlockSpec((1, 2, block), lambda i, j: (j, 0, i))],
        out_shape=[
            jax.ShapeDtypeStruct((rows, width), jnp.bfloat16),
            jax.ShapeDtypeStruct((rows, width), jnp.bfloat16),
            jax.ShapeDtypeStruct((couples, 2, rows), jnp.float32),
        ],
        scratch_shapes=[pltpu.VMEM((keys, block), jnp.float32)],
        compiler_params=pltpu.CompilerParams(vmem_limit_bytes=48 * 2**20),
        cost_estimate=pl.CostEstimate(flops=10**8, bytes_accessed=10**5, transcendentals=0),
    )(query_lin, *tables, pairs, pairs_across, doc_query, doc_key)


def attend_back(queries, d_mixed, totals, tables, pairs, pairs_across, doc_query, doc_key):
    rows, width = queries.shape
    block = 256
    keys = WINDOW + block
    couples = width // (2 * HD)
    last = (rows // block - 1, couples - 1)

    def kernel(q_ref, do_ref, total_ref, t0, t1, t2, pairs_ref, across_ref, dq_ref, dk_ref, d_lin_ref, d_pairs_ref, bias, d_keys, d_values, values):
        start = pl.multiple_of(pl.program_id(0) * block, block)
        window = pl.ds(start, keys)

        @pl.when((pl.program_id(0) == 0) & (pl.program_id(1) == 0))
        def clear():
            d_keys[...] = jnp.zeros_like(d_keys)
            d_values[...] = jnp.zeros_like(d_values)
            values[...] = pairs_ref[...][:, HD:]

        @pl.when(pl.program_id(1) == 0)
        def fill():
            bias[...] = no_entry(dq_ref[...], dk_ref[window, :], block, keys)

        own_keys = pairs_ref[window, :][:, :HD]
        own_values = values[window, :]
        keys_across = across_ref[pl.ds(0, HD), window]
        d_turned = []
        for head in range(2):
            part = slice(head * HD, (head + 1) * HD)
            q, do = q_ref[...][:, part], do_ref[...][:, part]
            scores = dot_last(own_keys, q) + bias[...]
            probs = jnp.exp(scores - total_ref[0][head : head + 1, :])
            d_probs = dot_last(own_values, do)
            product = probs * d_probs
            weighted = jnp.sum(product, axis=0, keepdims=True)
            d_scores = (product - probs * weighted).astype(jnp.bfloat16)
            d_turned.append(dot(keys_across, d_scores))
            d_keys[window, :] += dot(d_scores, q)
            d_values[window, :] += dot(probs.astype(jnp.bfloat16), do)
        d_turned = jnp.concatenate(d_turned, axis=0).T
        d_lin = turn(d_turned, (t0[...], t1[...], t2[...]), True) * HD ** (-0.5)
        d_lin_ref[...] = d_lin.astype(jnp.bfloat16)

        @pl.when((pl.program_id(0) == last[0]) & (pl.program_id(1) == last[1]))
        def finish():
            d_pairs_ref[...] = jnp.concatenate([d_keys[...], d_values[...]], axis=1)

    tile = pl.BlockSpec((block, 2 * HD), lambda i, j: (i, j))
    table = pl.BlockSpec((block, 2 * HD), lambda i, j: (i, 0))
    return pl.pallas_call(
        kernel,
        grid=(rows // block, couples),
        in_specs=[
            tile,
            tile,
            pl.BlockSpec((1, 2, block), lambda i, j: (j, 0, i)),
            table,
            table,
            table,
            pl.BlockSpec(pairs.shape, lambda i, j: (0, 0)),
            pl.BlockSpec(pairs_across.shape, lambda i, j: (0, 0)),
            pl.BlockSpec((1, block), lambda i, j: (0, i)),
            pl.BlockSpec(doc_key.shape, lambda i, j: (0, 0)),
        ],
        out_specs=[tile, pl.BlockSpec(pairs.shape, lambda i, j: (0, 0))],
        out_shape=[
            jax.ShapeDtypeStruct((rows, width), jnp.bfloat16),
            jax.ShapeDtypeStruct(pairs.shape, jnp.float32),
        ],
        scratch_shapes=[
            pltpu.VMEM((keys, block), jnp.float32),
            pltpu.VMEM((pairs.shape[0], HD), jnp.float32),
            pltpu.VMEM((pairs.shape[0], HD), jnp.float32),
            pltpu.VMEM((pairs.shape[0], HD), jnp.bfloat16),
        ],
        compiler_params=pltpu.CompilerParams(vmem_limit_bytes=48 * 2**20),
        cost_estimate=pl.CostEstimate(flops=10**8, bytes_accessed=10**5, transcendentals=0),
    )(queries, d_mixed, totals, *tables, pairs, pairs_across, doc_query, doc_key)


def put_pieces(pieces, positions, shards):
    count = len(pieces)
    others, rows, unused_width = pieces[0].shape
    depth = others + 1
    widths = [shard.shape[2] for shard in shards]

    def kernel(positions_ref, *refs):
        i, j = pl.program_id(0), pl.program_id(1)
        sources, locals_, targets = (
            refs[:count],
            refs[count : count + len(shards)],
            refs[count + len(shards) :],
        )
        for at in range(count):

            @pl.when((i == at) & (j < others))
            def take():
                start = 0
                for target, width in zip(targets, widths):
                    target[0, 0] = sources[at][j, :, pl.ds(start, width)]
                    start += width

        @pl.when(j == others)
        def keep():
            for target, source in zip(targets, locals_):
                target[0, 0] = source[0]

    return pl.pallas_call(
        kernel,
        out_shape=[
            jax.ShapeDtypeStruct((depth, count, rows, width), pieces[0].dtype) for width in widths
        ],
        grid_spec=pltpu.PrefetchScalarGridSpec(
            num_scalar_prefetch=1,
            grid=(count, depth),
            in_specs=[pl.BlockSpec(p.shape, lambda i, j, at: (0, 0, 0)) for p in pieces]
            + [pl.BlockSpec((1, rows, width), lambda i, j, at: (at[i], 0, 0)) for width in widths],
            out_specs=[
                pl.BlockSpec(
                    (1, 1, rows, width),
                    lambda i, j, at: (at[count + j], at[i], 0, 0),
                )
                for width in widths
            ],
        ),
        compiler_params=pltpu.CompilerParams(vmem_limit_bytes=40 * 2**20),
    )(positions, *pieces, *shards)


def rest(x, level):
    depth = x.shape[0]
    block = (1,) + x.shape[1:]
    zeros = (0,) * (x.ndim - 1)

    def kernel(level_ref, source, target):
        target[...] = source[...]

    return pl.pallas_call(
        kernel,
        out_shape=jax.ShapeDtypeStruct((depth - 1,) + x.shape[1:], x.dtype),
        grid_spec=pltpu.PrefetchScalarGridSpec(
            num_scalar_prefetch=1,
            grid=(depth - 1,),
            in_specs=[
                pl.BlockSpec(block, lambda i, at: (lax.rem(at[0] + i + 1, depth), *zeros))
            ],
            out_specs=pl.BlockSpec(block, lambda i, at: (i, *zeros)),
        ),
    )(level[None], x)


def spread(pieces, positions, shape, place):
    count = len(pieces)
    rows, width = pieces[0].shape

    def kernel(positions_ref, *refs):
        for at in range(count):

            @pl.when(pl.program_id(0) == at)
            def take():
                refs[-1][...] = refs[at][...].astype(jnp.float32)

    return pl.pallas_call(
        kernel,
        out_shape=jax.ShapeDtypeStruct(shape, jnp.float32),
        grid_spec=pltpu.PrefetchScalarGridSpec(
            num_scalar_prefetch=1,
            grid=(count,),
            in_specs=[pl.BlockSpec((rows, width), lambda i, at: (0, 0))] * count,
            out_specs=pl.BlockSpec((rows, width), lambda i, at: place(at[i])),
        ),
        compiler_params=pltpu.CompilerParams(vmem_limit_bytes=40 * 2**20),
    )(positions, *pieces)


GELU_SCALE = 0.7978845608028654
GELU_CUBE = 0.044715


def dot_first(a, b):
    return lax.dot_general(a, b, (((0,), (0,)), ((), ())), preferred_element_type=jnp.float32)


def feed(facts, x, grad, first_w, second_w, shard, down_pieces, down_shard, block_sum, back_sum, terms):
    rows, width = x.shape
    hidden = first_w.shape[1]
    half = hidden // 2
    column = width // 4
    depth = down_pieces[0].shape[0] + 1
    level_rows = width // depth
    full = depth * hidden
    started = back_sum is not None
    pieces = 8
    f32, bf16 = jnp.float32, jnp.bfloat16

    def kernel(facts_ref, x_ref, g_ref, *refs):
        wa_in, wb_in, shard_in, down_in, block_in = refs[:5]
        down_pieces_in = refs[5 : 5 + pieces]
        refs = refs[5 + pieces :]
        if started:
            back_in = refs[0]
            refs = refs[1 + pieces :]
        block_out, back_out, ga_out, gb_out = refs[:4]
        term_out = refs[4 : 4 + pieces]
        wa, wb, wd, a, b, d, act, da, db, block, back, ga, gb, gd, sems = refs[4 + pieces :]
        chip = facts_ref[1]
        core, level = facts_ref[2], facts_ref[7]

        def rows_of(source, target, side, sem):
            copies = []
            for i in range(1, depth):
                place = pl.multiple_of(lax.rem(level + i, depth) * level_rows, 16)
                copies.append(
                    pltpu.make_async_copy(
                        source.at[pl.ds((i - 1) * level_rows, level_rows)],
                        target.at[pl.ds(place, level_rows)],
                        sem,
                    )
                )
            place = pl.multiple_of(level * level_rows, 16)
            start = pl.multiple_of(side * full + chip * hidden, 128)
            copies.append(
                pltpu.make_async_copy(
                    shard_in.at[:, pl.ds(start, hidden)],
                    target.at[pl.ds(place, level_rows)],
                    sem,
                )
            )
            return copies

        for copy in rows_of(wa_in, wa, core, sems.at[0]):
            copy.start()
        for copy in rows_of(wb_in, wb, 1 - core, sems.at[1]):
            copy.start()

        @pl.when(chip == level)
        def here():
            pltpu.make_async_copy(down_in, wd, sems.at[2]).start()

        @pl.when(chip != level)
        def elsewhere():
            step = lax.rem(chip - level + depth - 1, depth)
            for i in range(pieces):
                side = jnp.where(i < 4, core, 1 - core)
                pltpu.make_async_copy(
                    down_pieces_in[i].at[step],
                    wd.at[
                        pl.ds(pl.multiple_of(side * half, 16), half),
                        pl.ds(pl.multiple_of(facts_ref[3 + i % 4] * column, 128), column),
                    ],
                    sems.at[2],
                ).start()

        load_block = pltpu.make_async_copy(block_in, block, sems.at[3])
        load_block.start()
        if started:
            load_back = pltpu.make_async_copy(back_in, back, sems.at[4])
            load_back.start()
        pltpu.make_async_copy(wa, wa, sems.at[0]).wait()
        a[...] = dot(x_ref[...], wa[...])
        pltpu.make_async_copy(wb, wb, sems.at[1]).wait()
        b[...] = dot(x_ref[...], wb[...])
        pltpu.make_async_copy(wd, wd, sems.at[2]).wait()
        d[...] = dot_last(g_ref[...], wd[...])
        swapped = facts_ref[0] == 1

        @pl.loop(0, rows // 16)
        def glu(i):
            part = pl.ds(pl.multiple_of(i * 16, 16), 16)
            for j in range(hidden // 384):
                lanes = slice(j * 384, (j + 1) * 384)
                one, two, slope = a[part, lanes], b[part, lanes], d[part, lanes]
                gate = jnp.where(swapped, two, one)
                up = jnp.where(swapped, one, two)
                square = gate * gate
                inner = gate * (square * (GELU_SCALE * GELU_CUBE) + GELU_SCALE)
                share = 0.5 * jnp.tanh(inner) + 0.5
                gelu = gate * share
                bend = square * (6.0 * GELU_SCALE * GELU_CUBE) + 2.0 * GELU_SCALE
                rise = share + gelu * (1.0 - share) * bend
                d_gate = (slope * up) * rise
                d_up = slope * gelu
                act[part, lanes] = (gelu * up).astype(bf16)
                da[part, lanes] = jnp.where(swapped, d_up, d_gate).astype(bf16)
                db[part, lanes] = jnp.where(swapped, d_gate, d_up).astype(bf16)

        for i in range(width // 384):
            part = pl.ds(i * 384, 384)
            gb[part, :] = dot_first(x_ref[:, i * 384 : (i + 1) * 384], db[...]).astype(bf16)
            pltpu.make_async_copy(gb.at[part], gb_out.at[part], sems.at[5]).start()
        for i in range(width // 384):
            part = pl.ds(i * 384, 384)
            ga[part, :] = dot_first(x_ref[:, i * 384 : (i + 1) * 384], da[...]).astype(bf16)
            pltpu.make_async_copy(ga.at[part], ga_out.at[part], sems.at[6]).start()
        for i in range(hidden // 384):
            part = pl.ds(i * 384, 384)
            gd[part, :] = dot_first(act[:, i * 384 : (i + 1) * 384], g_ref[...]).astype(bf16)
        stores = []
        for i in range(pieces):
            side = jnp.where(i < 4, core, 1 - core)
            stores.append(
                pltpu.make_async_copy(
                    gd.at[
                        pl.ds(pl.multiple_of(side * half, 16), half),
                        pl.ds(pl.multiple_of(facts_ref[3 + i % 4] * column, 128), column),
                    ],
                    term_out[i].at[chip],
                    sems.at[7 + i],
                )
            )
        for store in stores:
            store.start()
        if started:
            load_back.wait()

            back[...] += dot_last(da[...], wa[...])
            back[...] += dot_last(db[...], wb[...])
        else:
            back[...] = dot_last(da[...], wa[...])
            back[...] += dot_last(db[...], wb[...])
        store_back = pltpu.make_async_copy(back, back_out, sems.at[15])
        store_back.start()
        load_block.wait()
        for i in range(2):
            part = pl.ds(i * (rows // 2), rows // 2)
            block[part, :] += dot(act[part, :], wd[...])
            pltpu.make_async_copy(block.at[part], block_out.at[part], sems.at[16]).start()
        for store in stores:
            store.wait()
        pltpu.make_async_copy(gb, gb_out, sems.at[5]).wait()
        pltpu.make_async_copy(ga, ga_out, sems.at[6]).wait()
        store_back.wait()
        pltpu.make_async_copy(block, block_out, sems.at[16]).wait()

    anywhere = pl.BlockSpec(memory_space=pl.ANY)
    inside = pl.BlockSpec(memory_space=pltpu.VMEM)
    operands = [facts, x, grad, first_w, second_w, shard, down_shard, block_sum, *down_pieces]
    aliases = {}
    if started:
        aliases[7] = 0
        aliases[len(operands)] = 1
        operands.append(back_sum)
        for i, term in enumerate(terms):
            aliases[len(operands)] = 4 + i
            operands.append(term)
    sums = jax.ShapeDtypeStruct((rows, width), f32)
    grads = jax.ShapeDtypeStruct((width, hidden), bf16)
    results = pl.pallas_call(
        kernel,
        in_specs=[pl.BlockSpec(memory_space=pltpu.SMEM), inside, inside]
        + [anywhere] * (len(operands) - 3),
        out_specs=[anywhere] * (4 + pieces),
        out_shape=[sums, sums, grads, grads]
        + [jax.ShapeDtypeStruct((depth, half, column), bf16)] * pieces,
        input_output_aliases=aliases,
        scratch_shapes=[
            pltpu.VMEM((width, hidden), bf16),
            pltpu.VMEM((width, hidden), bf16),
            pltpu.VMEM((hidden, width), bf16),
            pltpu.VMEM((rows, hidden), f32),
            pltpu.VMEM((rows, hidden), f32),
            pltpu.VMEM((rows, hidden), f32),
            pltpu.VMEM((rows, hidden), bf16),
            pltpu.VMEM((rows, hidden), bf16),
            pltpu.VMEM((rows, hidden), bf16),
            pltpu.VMEM((rows, width), f32),
            pltpu.VMEM((rows, width), f32),
            pltpu.VMEM((width, hidden), bf16),
            pltpu.VMEM((width, hidden), bf16),
            pltpu.VMEM((hidden, width), bf16),
            pltpu.SemaphoreType.DMA((17,)),
        ],
        compiler_params=pltpu.CompilerParams(vmem_limit_bytes=56 * 2**20),
        cost_estimate=pl.CostEstimate(flops=10**8, bytes_accessed=10**5, transcendentals=0),
    )(*operands)
    return results[0], results[1], results[2], results[3], results[4:]


class Plane:
    def __init__(self):
        self.me = lax.axis_index("seq")
        self.core = self.me % 2
        self.chip = self.me // 2
        first = jnp.where(self.core == 0, 1, 2)
        self.chips = [self.chip, self.chip ^ first, self.chip ^ (3 - first), self.chip ^ 3]
        self.first_pairs = [(i, i ^ (2 if i % 2 == 0 else 4)) for i in range(8)]
        self.second_pairs = [(i, i ^ (4 if i % 2 == 0 else 2)) for i in range(8)]
        self.core_pairs = [(i, i ^ 1) for i in range(8)]
        self.sources = jnp.stack(
            [chip * 2 + self.core for chip in self.chips]
            + [chip * 2 + 1 - self.core for chip in self.chips]
        )

    def first(self, x):
        return lax.ppermute(x, "seq", self.first_pairs)

    def second(self, x):
        return lax.ppermute(x, "seq", self.second_pairs)

    def along(self, x):
        depth = lax.axis_size("fsdp")
        return [
            lax.ppermute(x, "fsdp", [((i + k) % depth, i) for i in range(depth)])
            for k in range(1, depth)
        ]

    def swap(self, x):
        return lax.ppermute(x, "seq", self.core_pairs)

    def down_columns(self, x):
        return lax.psum_scatter(x, "fsdp", scatter_dimension=0, tiled=True)


def places_of(arrival_order, ranks):
    row_count = arrival_order.shape[1]
    capacity = 2 * row_count // ranks
    arrived_at = arrival_order[0]
    owner = arrived_at // row_count
    owner_hits = (owner[:, None] == jnp.arange(ranks, dtype=jnp.int32)[None, :]).astype(jnp.int32)
    within = jnp.sum(jnp.cumsum(owner_hits, axis=0) * owner_hits, axis=1) - 1
    return owner * capacity + within, arrived_at % row_count


def to_slots(rows, slots, ranks, empty=0):
    capacity = 2 * rows.shape[0] // ranks
    out = jnp.full((ranks * capacity,) + rows.shape[1:], empty, rows.dtype)
    return out.at[slots].set(rows).reshape((ranks, capacity) + rows.shape[1:])


def from_slots(slots, landing):
    flat = slots.reshape((-1, slots.shape[-1]))
    out = jnp.zeros((flat.shape[0] // 2, flat.shape[1]), flat.dtype)
    return out.at[landing].set(flat, mode="drop")


def back_to_slots(rows, safe_place, ranks):
    return rows[safe_place].reshape(ranks, -1, rows.shape[1])


def exchange(x):
    return lax.all_to_all(x, "seq", split_axis=0, concat_axis=0, tiled=True)


def positions_of(lengths, row_count):
    position = lax.axis_index("seq")
    places = position * row_count + jnp.arange(row_count, dtype=jnp.int32)
    doc_query, offset_query = layout(lengths[0], places)
    key_places = (
        position * row_count - WINDOW + jnp.arange(WINDOW + row_count, dtype=jnp.int32)
    )
    doc_key, unused_offset = layout(lengths[0], key_places)
    cosine, sine = angles(offset_query.astype(jnp.float32), HD)
    return (doc_query[None, :], doc_key[:, None]), cosine, sine


def pair_of(kv_lin, cosine, sine):
    own_keys = rounded(rotate(kv_lin[:, :HD], cosine, sine))
    return jnp.concatenate([own_keys, rounded(kv_lin[:, HD:])], axis=1)


def with_earlier(pair, reach):
    return jnp.concatenate(
        [passed_along(pair, "seq", distance) for distance in range(reach, 0, -1)] + [pair], axis=0
    )


def owners_sum(d_pairs, row_count, reach):
    parts = [
        passed_along(
            rounded(d_pairs[(reach - distance) * row_count :][:row_count]), "seq", -distance
        )
        for distance in range(reach, 0, -1)
    ]
    own = d_pairs[reach * row_count :]
    for part in parts:
        own = own + widened(part)
    return own


def body(*operands):
    return square_body(*operands) if lax.axis_size("seq") == 8 else plain_body(*operands)


def plain_body(
    tokens,
    cotangent,
    arrival_order,
    lengths,
    norm_gain,
    w_query,
    w_kv,
    w_out,
    ffn_gain,
    w_gate_up,
    w_down,
):
    row_count = tokens.shape[1]
    ranks = lax.axis_size("seq")
    reach = WINDOW // row_count
    position = lax.axis_index("seq")

    def whole(shard):
        part = shard.shape[0] // ranks
        mine = lax.dynamic_slice_in_dim(shard, position * part, part, axis=0)
        return lax.all_gather(mine, ("fsdp", "seq"), axis=0, tiled=True)

    def summed(grad):
        mine = lax.psum_scatter(rounded(grad), ("fsdp", "seq"), scatter_dimension=0, tiled=True)
        return widened(lax.all_gather(mine, "seq", axis=0, tiled=True))

    send_slot, send_place = places_of(arrival_order, ranks)
    got_tokens = exchange(to_slots(tokens[0], send_slot, ranks))
    got_cotangent = exchange(to_slots(cotangent[0], send_slot, ranks))
    recv_place = exchange(to_slots(send_place, send_slot, ranks, -1)).reshape(-1)
    is_live = recv_place >= 0
    landing = jnp.where(is_live, recv_place, row_count)
    safe_place = jnp.where(is_live, recv_place, 0)
    packed_f = widened(from_slots(got_tokens, landing))
    packed_grad = from_slots(got_cotangent, landing)
    query_w, kv_w, out_w, down_w, gate_up_w = (
        whole(w_query),
        whole(w_kv),
        whole(w_out),
        whole(w_down),
        whole(w_gate_up),
    )
    gain_attn, gain_ffn = (
        widened(lax.all_gather(gain, "fsdp", axis=0, tiled=True)) for gain in (norm_gain, ffn_gain)
    )
    docs, cosine, sine = positions_of(lengths, row_count)
    tables = tables_of(cosine, sine, 2, 0)

    normed = rounded(rms_scale(packed_f, gain_attn))
    pair_rows = with_earlier(pair_of(dot(normed, kv_w), cosine, sine), reach)
    queries, mixed, totals = attend(dot(normed, query_w), tables, pair_rows, pair_rows.T, *docs)
    hidden_state = packed_f + dot(mixed, out_w)
    ffn_in = rounded(rms_scale(hidden_state, gain_ffn))
    gate, up = dot(ffn_in, gate_up_w[:, :FF]), dot(ffn_in, gate_up_w[:, FF:])
    activated, pull = jax.vjp(lambda g, u: jax.nn.gelu(g, approximate=True) * u, gate, up)
    activated = rounded(activated)
    block_rows = rounded(hidden_state + dot(activated, down_w))

    d_gate, d_up = pull(dot_across(packed_grad, down_w))
    d_gate_up = jnp.concatenate([rounded(d_gate), rounded(d_up)], axis=1)
    unused_scaled, ffn_norm_pull = jax.vjp(rms_scale, hidden_state, gain_ffn)
    d_hidden_norm, grad_gain_ffn = ffn_norm_pull(dot_across(d_gate_up, gate_up_w))
    d_hidden = widened(packed_grad) + d_hidden_norm
    d_branch = rounded(d_hidden)
    d_mixed = rounded(dot_across(d_branch, out_w))
    d_query_lin, d_pairs = attend_back(
        queries, d_mixed, totals, tables, pair_rows, pair_rows.T, *docs
    )
    d_own = owners_sum(d_pairs, row_count, reach)
    d_kv_lin = rounded(
        jnp.concatenate([unrotate(d_own[:, :HD], cosine, sine), d_own[:, HD:]], axis=1)
    )
    d_normed = dot_across(d_query_lin, query_w) + dot_across(d_kv_lin, kv_w)
    unused_normed, attn_norm_pull = jax.vjp(rms_scale, packed_f, gain_attn)
    d_packed_norm, grad_gain_attn = attn_norm_pull(d_normed)
    grad_rows = rounded(d_hidden + d_packed_norm)
    block_arrived, grad_arrived = (
        exchange(back_to_slots(rows, safe_place, ranks)).reshape(-1, rows.shape[1])[
            send_slot
        ]
        for rows in (block_rows, grad_rows)
    )
    total_gain_attn, total_gain_ffn = (
        lax.psum(lax.psum_scatter(gain, "fsdp", scatter_dimension=0, tiled=True), "seq")
        for gain in (grad_gain_attn, grad_gain_ffn)
    )
    return (
        block_arrived[None],
        grad_arrived[None],
        total_gain_attn,
        summed(dot_rows(normed, d_query_lin)),
        summed(dot_rows(normed, d_kv_lin)),
        summed(dot_rows(mixed, d_branch)),
        total_gain_ffn,
        summed(dot_rows(ffn_in, d_gate_up)),
        summed(dot_rows(activated, packed_grad)),
    )


def square_body(
    tokens,
    cotangent,
    arrival_order,
    lengths,
    norm_gain,
    w_query,
    w_kv,
    w_out,
    ffn_gain,
    w_gate_up,
    w_down,
):
    row_count = tokens.shape[1]
    model_width = tokens.shape[2]
    ranks = lax.axis_size("seq")
    depth = lax.axis_size("fsdp")
    reach = WINDOW // row_count
    shard_rows = w_query.shape[0]
    part_rows = shard_rows // ranks
    quarter = FF // 4
    column = model_width // 4
    half_rows = w_down.shape[0] // 2
    split = model_width + 2 * HD
    plane = Plane()
    level = lax.axis_index("fsdp").astype(jnp.int32)
    levels = (level + 1 + jnp.arange(depth, dtype=jnp.int32)) % depth
    at = jnp.concatenate([plane.sources, levels]).astype(jnp.int32)

    def my_rows(shard):
        return lax.dynamic_slice_in_dim(shard, plane.me * part_rows, part_rows, axis=0)

    def by_parts(shard):
        return shard.reshape(ranks, part_rows, shard.shape[1])

    def second_halves(slots):
        return [plane.swap(slots[i]) for i in (0, 2, 1, 3)]


    gains = jnp.concatenate([norm_gain, ffn_gain]).reshape(part_rows, -1)
    gain_width = gains.shape[1]
    early = plane.along(
        jnp.concatenate(
            [my_rows(w_query), my_rows(w_kv), jnp.pad(gains, ((0, 0), (0, 128 - gain_width)))],
            axis=1,
        )
    )
    send_slot, send_place = places_of(arrival_order, ranks)
    labels = jnp.stack([send_place // 2, send_place % 2, jnp.ones_like(send_place)], axis=1)
    labels = jnp.pad(labels.astype(jnp.bfloat16), ((0, 0), (0, 125)))
    token_slots = to_slots(jnp.concatenate([tokens[0], labels], axis=1), send_slot, ranks)
    got_tokens = exchange(token_slots)
    *early, cotangent_rows, out_mine, down_mine, gate_up_mine = fence(
        *early, after(cotangent[0], token_slots), my_rows(w_out), w_down, w_gate_up
    )
    early = jnp.stack(early)
    gain_rows = early[:, :, split : split + gain_width].reshape(depth - 1, 2, shard_rows)
    early = early[:, :, :split]

    def down_of(shard, chip):
        piece = lax.dynamic_slice(
            shard, (plane.core * half_rows, chip * column), (half_rows, column)
        )
        return lax.all_gather(piece, "fsdp", axis=0, tiled=False)

    down_piece = down_of(down_mine, plane.chip)
    gate_up_piece = lax.dynamic_slice(
        gate_up_mine, (0, plane.core * FF + plane.chip * quarter), (shard_rows, quarter)
    )
    gate_up_piece = lax.all_gather(gate_up_piece, "fsdp", axis=0, tiled=False)

    early_u, early_v, early_0 = plane.first(early), plane.second(early), plane.swap(early)
    out = plane.along(out_mine)
    docs, cosine, sine = positions_of(lengths, row_count)
    tables = rows_first(tables_of(cosine, sine, 2, 0))
    cotangent_slots = to_slots(cotangent_rows, send_slot, ranks)
    early_u, early_v, early_0, got_tokens, out, cotangent_slots, tables = fence(
        early_u, early_v, early_0, got_tokens, out, cotangent_slots, tables
    )
    got_cotangent = exchange(cotangent_slots)

    out = jnp.stack(out)
    early_d, early_2, early_1 = plane.second(early_u), plane.swap(early_u), plane.swap(early_v)
    out_u, out_v, out_0 = plane.first(out), plane.second(out), plane.swap(out)
    labels = got_tokens.reshape(-1, model_width + 128)[:, model_width:].astype(jnp.int32)
    safe_place = labels[:, 0] * 2 + labels[:, 1]
    is_live = labels[:, 2] == 1
    landing = jnp.where(is_live, safe_place, row_count)
    packed_f = widened(from_slots(got_tokens, landing)[:, :model_width])
    gain_rows = jnp.concatenate([gain_rows, gains.reshape(1, 2, shard_rows)], axis=0)
    gain_rows = gain_rows[(jnp.arange(depth, dtype=jnp.int32) + depth - 1 - level) % depth]
    gain_attn = widened(gain_rows[:, 0].reshape(model_width))
    gain_ffn = widened(gain_rows[:, 1].reshape(model_width))
    normed = rounded(rms_scale(packed_f, gain_attn))
    early_d, early_2, early_1, out_u, out_v, out_0, normed = fence(
        early_d, early_2, early_1, out_u, out_v, out_0, normed
    )

    early_3, out_d, out_2, out_1 = (
        plane.swap(early_d),
        plane.second(out_u),
        plane.swap(out_u),
        plane.swap(out_v),
    )
    down_piece = rest(after(down_piece, normed), level)
    early_3, out_d, out_2, out_1, down_piece = fence(early_3, out_d, out_2, out_1, down_piece)

    down_u, down_v, down_0 = (
        plane.first(down_piece),
        plane.second(down_piece),
        plane.swap(down_piece),
    )
    out_3 = plane.swap(out_d)
    query_w, kv_w = put_pieces(
        [early, early_u, early_v, early_d, early_0, early_1, early_2, early_3],
        after(at, down_piece),
        [by_parts(w_query), by_parts(w_kv)],
    )
    query_w = query_w.reshape(model_width, model_width)
    kv_w = kv_w.reshape(model_width, 2 * HD)
    query_lin = dot(normed, query_w)
    pair = pair_of(dot(normed, kv_w), cosine, sine)
    (out_w,) = put_pieces(
        [out, out_u, out_v, out_d, out_0, out_1, out_2, out_3],
        after(at, pair),
        [by_parts(w_out)],
    )
    out_w = out_w.reshape(model_width, model_width)
    down_u, down_v, down_0, out_w, query_lin, pair = fence(
        down_u, down_v, down_0, out_w, query_lin, pair
    )

    pair_rows = with_earlier(pair, reach)
    down_2, down_1 = plane.swap(down_u), plane.swap(down_v)
    down_d = down_of(after(w_down, gate_up_piece), plane.chips[3])
    gate_up_piece = rest(gate_up_piece, level)
    gate_up_piece = gate_up_piece.reshape((depth - 1) * shard_rows, quarter)
    packed_grad = from_slots(after(got_cotangent, gate_up_piece), landing)
    pair_rows, down_2, down_1, gate_up_piece, packed_grad = fence(
        pair_rows, down_2, down_1, gate_up_piece, packed_grad
    )

    gate_up_u, gate_up_v, gate_up_0 = (
        plane.first(gate_up_piece),
        plane.second(gate_up_piece),
        plane.swap(gate_up_piece),
    )
    pairs_across = pair_rows.T
    queries, mixed, totals = attend(query_lin, tables, pair_rows, pairs_across, *docs)
    down_d = rest(after(down_d, mixed), level)
    down_3 = plane.swap(down_d)
    hidden_state = packed_f + dot(after(mixed, down_d), out_w)
    ffn_in = rounded(rms_scale(hidden_state, gain_ffn))

    def chunk(slot, first_w, second_w, chunk_in, block_sum, back_sum, terms):
        facts = [plane.core, plane.chips[slot], plane.core, *plane.chips, level]
        return feed(
            jnp.stack(facts).astype(jnp.int32),
            chunk_in,
            packed_grad,
            first_w,
            second_w,
            w_gate_up,
            [down_piece, down_u, down_v, down_d, down_0, down_1, down_2, down_3],
            w_down,
            block_sum,
            back_sum,
            terms,
        )

    block_sum, back_sum, own_0, other_0, terms = chunk(
        0, gate_up_piece, gate_up_0, ffn_in, hidden_state, None, None
    )
    gate_up_u, gate_up_v, block_sum, back_sum, own_0, other_0 = fence(
        gate_up_u, gate_up_v, block_sum, back_sum, own_0, other_0
    )

    gate_up_2, gate_up_1 = plane.swap(gate_up_u), plane.swap(gate_up_v)
    gate_up_2, gate_up_1, gate_up_u, back_sum = fence(gate_up_2, gate_up_1, gate_up_u, back_sum)
    gate_up_d, swap_0 = plane.second(gate_up_u), plane.swap(other_0)
    block_sum, back_sum, own_u, other_u, terms = chunk(
        1, gate_up_u, gate_up_1, ffn_in, block_sum, back_sum, terms
    )
    gate_up_d, swap_0, block_sum, back_sum, own_u, other_u = fence(
        gate_up_d, swap_0, block_sum, back_sum, own_u, other_u
    )
    gate_up_3, swap_u = plane.swap(gate_up_d), plane.swap(other_u)
    block_sum, back_sum, own_v, other_v, terms = chunk(
        2, gate_up_v, gate_up_2, ffn_in, block_sum, back_sum, terms
    )
    gate_up_3, swap_u, block_sum, back_sum, own_v, other_v = fence(
        gate_up_3, swap_u, block_sum, back_sum, own_v, other_v
    )
    sum_v, other_v, back_sum = fence(added(own_v, swap_u), other_v, back_sum)
    from_v, swap_v = plane.second(sum_v), plane.swap(other_v)
    block_sum, back_sum, own_d, other_d, terms = chunk(
        3, gate_up_d, gate_up_3, ffn_in, block_sum, back_sum, terms
    )
    sum_u = added(own_u, swap_v)
    from_v, sum_u, block_sum, back_sum, own_d, other_d, terms = fence(
        from_v, sum_u, block_sum, back_sum, own_d, other_d, terms
    )

    from_u, swap_d = plane.first(sum_u), plane.swap(other_d)
    terms = [term.reshape(depth * half_rows, column) for term in terms]
    down_swaps = [plane.swap(term) for term in terms[4:]]
    unused_scaled, ffn_norm_pull = jax.vjp(rms_scale, hidden_state, gain_ffn)
    d_hidden_norm, grad_gain_ffn = ffn_norm_pull(back_sum)
    d_hidden = widened(packed_grad) + d_hidden_norm
    d_branch = rounded(d_hidden)
    d_mixed = rounded(dot_across(d_branch, out_w))
    sum_d = added_apart(after(own_d, d_mixed), swap_d)
    part_d = plane.down_columns(sum_d)
    down_sums = [
        added_apart(after(term, sum_d), down_swaps[match])
        for term, match in zip(terms[:4], (0, 2, 1, 3))
    ]
    from_u, d_branch, d_mixed, down_sums = fence(from_u, d_branch, d_mixed, down_sums)
    from_down_d, from_down_v = plane.second(down_sums[3]), plane.second(down_sums[2])
    total = added(own_0, swap_0, from_v, from_u)
    part_0 = plane.down_columns(total)
    d_query_lin, d_pairs = attend_back(
        queries, after(d_mixed, total), totals, tables, pair_rows, pairs_across, *docs
    )
    from_down_d, from_down_v, d_query_lin, d_pairs, block_sum, part_d = fence(
        from_down_d, from_down_v, d_query_lin, d_pairs, block_sum, part_d
    )
    part_d_u = plane.first(part_d)

    def by_rows(grad):
        pieces = rounded(grad).reshape(depth, ranks, part_rows, grad.shape[1])
        return [
            lax.dynamic_index_in_dim(pieces, plane.sources[i], axis=1, keepdims=False)
            for i in range(8)
        ]

    d_own = owners_sum(d_pairs, row_count, reach)
    down_u = added(down_sums[1], from_down_d)
    block_slots = back_to_slots(rounded(block_sum), safe_place, ranks)
    d_own, down_u, block_slots, part_d_u = fence(d_own, down_u, block_slots, part_d_u)
    home_out = exchange(block_slots)
    from_down_u, part_d = plane.first(down_u), plane.second(part_d_u)
    grad_out = dot_rows(mixed, after(d_branch, block_slots))
    out_terms = [p.reshape(depth * part_rows, model_width) for p in by_rows(grad_out)]
    out_swaps = [plane.swap(term) for term in out_terms[4:]]
    d_kv_lin = rounded(
        jnp.concatenate([unrotate(d_own[:, :HD], cosine, sine), d_own[:, HD:]], axis=1)
    )
    grad_query = dot_rows(normed, after(d_query_lin, *out_terms))
    grad_kv = dot_rows(normed, d_kv_lin)
    d_normed = dot_across(d_query_lin, query_w) + dot_across(d_kv_lin, kv_w)
    unused_normed, attn_norm_pull = jax.vjp(rms_scale, packed_f, gain_attn)
    d_packed_norm, grad_gain_attn = attn_norm_pull(d_normed)
    grad_rows = rounded(d_hidden + d_packed_norm)
    gain_rows = jnp.concatenate(
        [
            rounded(grad_gain_attn).reshape(depth, 1, shard_rows),
            rounded(grad_gain_ffn).reshape(depth, 1, shard_rows),
        ],
        axis=2,
    )
    gain_rows = jnp.pad(gain_rows, ((0, 0), (0, 15), (0, split - 2 * shard_rows)))
    early_terms = [
        jnp.concatenate([jnp.concatenate([q, k], axis=2), gain_rows], axis=1).reshape(
            depth * (part_rows + 16), split
        )
        for q, k in zip(by_rows(grad_query), by_rows(grad_kv))
    ]
    grad_slots = back_to_slots(after(grad_rows, *early_terms), safe_place, ranks)
    from_down_u, part_d, early_terms, out_swaps, grad_slots, home_out = fence(
        from_down_u, part_d, early_terms, out_swaps, grad_slots, home_out
    )

    home_grad = exchange(grad_slots)
    early_swaps = [plane.swap(term) for term in early_terms[4:]]
    out_d, out_v = added(out_terms[3], out_swaps[3]), added(out_terms[2], out_swaps[1])
    out_from_d, out_from_v = plane.second(out_d), plane.second(out_v)
    total = added(after(down_sums[0], out_d, out_v), from_down_v, from_down_u)
    mine_down = plane.down_columns(total)
    early_d = added(early_terms[3], early_swaps[3])
    early_v = added(early_terms[2], early_swaps[1])
    block_arrived = home_out.reshape(-1, model_width)[send_slot]
    out_from_d, out_from_v, early_d, early_v, early_swaps, part_0, block_arrived = fence(
        out_from_d, out_from_v, early_d, early_v, early_swaps, part_0, block_arrived
    )

    mine_gate_up = added(part_0, part_d)
    early_from_d, early_from_v = plane.second(early_d), plane.second(early_v)
    out_from_u = plane.first(added(out_terms[1], out_swaps[2], out_from_d))
    gate_up_u, gate_up_v, gate_up_0 = (
        plane.first(mine_gate_up),
        plane.second(mine_gate_up),
        plane.swap(mine_gate_up),
    )
    early_from_d, early_from_v, out_from_u, gate_up_u, gate_up_v, gate_up_0, home_grad = fence(
        early_from_d, early_from_v, out_from_u, gate_up_u, gate_up_v, gate_up_0, home_grad
    )

    early_from_u = plane.first(added(early_terms[1], early_swaps[2], early_from_d))
    total = added(out_terms[0], out_swaps[0], out_from_v, out_from_u)
    mine_out = plane.down_columns(total)
    gate_up_d, gate_up_2, gate_up_1 = (
        plane.second(gate_up_u),
        plane.swap(gate_up_u),
        plane.swap(gate_up_v),
    )
    grad_arrived = home_grad.reshape(-1, model_width)[send_slot]
    early_from_u, gate_up_d, gate_up_2, gate_up_1, mine_down, total, grad_arrived = fence(
        early_from_u, gate_up_d, gate_up_2, gate_up_1, mine_down, total, grad_arrived
    )

    total = added(early_terms[0], early_swaps[0], early_from_v, early_from_u)
    mine_early = plane.down_columns(total)
    gate_up_3 = plane.swap(gate_up_d)
    down_own = [mine_down, plane.first(mine_down), plane.second(mine_down)]
    total_gate_up = spread(
        [mine_gate_up, gate_up_u, gate_up_v, gate_up_d]
        + [gate_up_0, gate_up_1, gate_up_2, gate_up_3],
        after(plane.sources, total),
        (shard_rows, 2 * FF),
        lambda p: (0, (p % 2) * 4 + p // 2),
    )
    down_own, total_gate_up, mine_out = fence(down_own, total_gate_up, mine_out)

    down_own.append(plane.second(down_own[1]))
    down_swaps = [plane.swap(piece) for piece in down_own[:3]]
    out_own = [mine_out, plane.first(mine_out), plane.second(mine_out)]
    down_own, down_swaps, out_own, mine_early = fence(down_own, down_swaps, out_own, mine_early)

    down_swaps.append(plane.swap(down_own[3]))
    out_own.append(plane.second(out_own[1]))
    piece = mine_early[:part_rows]
    early_own = [piece, plane.first(piece), plane.second(piece)]
    total_down = spread(
        down_own + [down_swaps[i] for i in (0, 2, 1, 3)],
        plane.sources,
        (2 * half_rows, model_width),
        lambda p: (p % 2, p // 2),
    )
    early_own, out_own, total_down = fence(early_own, out_own, total_down)
    early_own.append(plane.second(early_own[1]))
    total_out = spread(
        out_own + second_halves(out_own),
        plane.sources,
        (shard_rows, model_width),
        lambda p: (p, 0),
    )
    early_own, total_out = fence(early_own, total_out)
    total_early = spread(
        early_own + second_halves(early_own),
        plane.sources,
        (shard_rows, split),
        lambda p: (p, 0),
    )
    return (
        block_arrived[None],
        grad_arrived[None],
        widened(mine_early[part_rows, :shard_rows]),
        total_early[:, :model_width],
        total_early[:, model_width:],
        total_out,
        widened(mine_early[part_rows, shard_rows : 2 * shard_rows]),
        total_gate_up,
        total_down,
    )


def solution(mesh):
    placed = (
        P("fsdp", "seq", None),
        P("fsdp", "seq", None),
        P("fsdp", "seq"),
        P("fsdp", None),
        P("fsdp"),
        P("fsdp", None),
        P("fsdp", None),
        P("fsdp", None),
        P("fsdp"),
        P("fsdp", None),
        P("fsdp", None),
    )
    return jax.shard_map(
        body,
        mesh=mesh,
        in_specs=placed,
        out_specs=(
            P("fsdp", "seq", None),
            P("fsdp", "seq", None),
            P("fsdp"),
            P("fsdp", None),
            P("fsdp", None),
            P("fsdp", None),
            P("fsdp"),
            P("fsdp", None),
            P("fsdp", None),
        ),
        check_vma=False,
    )
```

```python
import jax
import jax.numpy as jnp
from jax import lax
from jax.experimental import pallas as pl
from jax.experimental.pallas import tpu as pltpu
from jax.sharding import PartitionSpec as P

HD = 192
FF = 4608
WINDOW = 1024


EPSILON = 1e-06
ROPE_BASE = 10000.0
MASKED = -1e30


def passed_along(x, axis, by):
    length = lax.axis_size(axis)
    pairs = [(i, i + by) for i in range(length) if 0 <= i + by < length]
    return lax.ppermute(x, axis, pairs)


def rms_scale(values, gain):
    return values * lax.rsqrt(jnp.mean(values * values, axis=-1, keepdims=True) + EPSILON) * gain


def rotate(heads, cosine, sine):
    half = heads.shape[-1] // 2
    first_half = heads[..., :half]
    second_half = heads[..., half:]
    return jnp.concatenate(
        [first_half * cosine - second_half * sine, second_half * cosine + first_half * sine],
        axis=-1,
    )


def unrotate(heads, cosine, sine):
    half = heads.shape[-1] // 2
    first_half = heads[..., :half]
    second_half = heads[..., half:]
    return jnp.concatenate(
        [first_half * cosine + second_half * sine, second_half * cosine - first_half * sine],
        axis=-1,
    )


def angles(places, head_width):
    steps_half = jnp.arange(head_width // 2, dtype=jnp.float32)
    inverse = ROPE_BASE ** (-2.0 * steps_half / head_width)
    theta = places[:, None] * inverse[None, :]
    return (jnp.cos(theta), jnp.sin(theta))


def layout(lengths, places):
    ends = jnp.cumsum(lengths)
    starts = ends - lengths
    inside = (places[:, None] >= starts[None, :]) & (places[:, None] < ends[None, :])
    numbers = jnp.arange(1, lengths.shape[0] + 1, dtype=jnp.int32)
    document = jnp.sum(jnp.where(inside, numbers[None, :], 0), axis=1) - 1
    offset = places - jnp.sum(jnp.where(inside, starts[None, :], 0), axis=1)
    return (document, offset)


def after(x, *done):
    return lax.optimization_barrier((x, *done))[0]


def fence(*xs):
    return lax.optimization_barrier(xs)


def rounded(x):
    return x.astype(jnp.bfloat16)


def widened(x):
    return x.astype(jnp.float32)


def added(*terms):
    return rounded(sum(widened(term) for term in terms))


def added_apart(*terms):
    rows, width = terms[0].shape
    steps = 4

    def kernel(*refs):
        refs[-1][...] = rounded(sum(widened(ref[...]) for ref in refs[:-1]))

    block = pl.BlockSpec((rows // steps, width), lambda i: (i, 0))
    return pl.pallas_call(
        kernel,
        grid=(steps,),
        in_specs=[block] * len(terms),
        out_specs=block,
        out_shape=jax.ShapeDtypeStruct((rows, width), jnp.bfloat16),
        compiler_params=pltpu.CompilerParams(vmem_limit_bytes=32 * 2**20),
        cost_estimate=pl.CostEstimate(flops=10**6, bytes_accessed=10**5, transcendentals=0),
    )(*terms)


def dot(a, b):
    return jnp.dot(a, b, preferred_element_type=jnp.float32)


def dot_rows(a, b):
    return jnp.einsum("td,tf->df", a, b, preferred_element_type=jnp.float32)


def dot_across(a, b):
    return jnp.einsum("tf,df->td", a, b, preferred_element_type=jnp.float32)


def turn(x, tables, back):
    width = x.shape[-1]
    half = HD // 2
    later = pltpu.roll(x, width - half, axis=1)
    sooner = pltpu.roll(x, half, axis=1)
    turned = later * tables[1] + sooner * tables[2]
    return x * tables[0] - turned if back else x * tables[0] + turned


def tables_of(cosine, sine, heads, still):
    none = jnp.zeros_like(sine)
    ones = jnp.ones_like(sine)
    return (
        jnp.concatenate([cosine, cosine] * heads + [ones, ones] * still, axis=1),
        jnp.concatenate([-sine, none] * heads + [none, none] * still, axis=1),
        jnp.concatenate([none, sine] * heads + [none, none] * still, axis=1),
    )


def rows_first(arrays):
    def kernel(*refs):
        for source, target in zip(refs, refs[len(arrays) :]):
            target[...] = source[...]

    return pl.pallas_call(
        kernel, out_shape=[jax.ShapeDtypeStruct(x.shape, x.dtype) for x in arrays]
    )(*arrays)


def no_entry(doc_query, doc_key, rows, keys):
    key = lax.broadcasted_iota(jnp.int32, (keys, rows), 0)
    row = lax.broadcasted_iota(jnp.int32, (keys, rows), 1)
    gap = WINDOW + row - key
    seen = (doc_key == doc_query) & (doc_key >= 0) & (gap >= 0) & (gap < WINDOW)
    return jnp.where(seen, 0.0, MASKED)


def dot_last(a, b):
    return lax.dot_general(a, b, (((1,), (1,)), ((), ())), preferred_element_type=jnp.float32)


def attend(query_lin, tables, pairs, pairs_across, doc_query, doc_key):
    rows, width = query_lin.shape
    block = 256
    keys = WINDOW + block
    couples = width // (2 * HD)

    def kernel(q_ref, t0, t1, t2, pairs_ref, across_ref, dq_ref, dk_ref, turned_ref, mixed_ref, total_ref, bias):
        start = pl.multiple_of(pl.program_id(0) * block, block)
        window = pl.ds(start, keys)

        @pl.when(pl.program_id(1) == 0)
        def fill():
            bias[...] = no_entry(dq_ref[...], dk_ref[window, :], block, keys)

        queries = turn(q_ref[...], (t0[...], t1[...], t2[...]), False) * HD ** (-0.5)
        queries = queries.astype(jnp.bfloat16)
        turned_ref[...] = queries
        own_keys = pairs_ref[window, :][:, :HD]
        values = across_ref[pl.ds(HD, HD), window]
        mixed, totals = [], []
        for head in range(2):
            scores = dot_last(own_keys, queries[:, head * HD : (head + 1) * HD]) + bias[...]
            top = jnp.max(scores, axis=0, keepdims=True)
            weights = jnp.exp(scores - top)
            total = jnp.sum(weights, axis=0, keepdims=True)
            totals.append(top + jnp.log(total))
            mixed.append(dot(values, weights.astype(jnp.bfloat16)) * (1.0 / total))
        mixed_ref[...] = jnp.concatenate(mixed, axis=0).T.astype(jnp.bfloat16)
        total_ref[0] = jnp.concatenate(totals, axis=0)

    tile = pl.BlockSpec((block, 2 * HD), lambda i, j: (i, j))
    table = pl.BlockSpec((block, 2 * HD), lambda i, j: (i, 0))
    return pl.pallas_call(
        kernel,
        grid=(rows // block, couples),
        in_specs=[
            tile,
            table,
            table,
            table,
            pl.BlockSpec(pairs.shape, lambda i, j: (0, 0)),
            pl.BlockSpec(pairs_across.shape, lambda i, j: (0, 0)),
            pl.BlockSpec((1, block), lambda i, j: (0, i)),
            pl.BlockSpec(doc_key.shape, lambda i, j: (0, 0)),
        ],
        out_specs=[tile, tile, pl.BlockSpec((1, 2, block), lambda i, j: (j, 0, i))],
        out_shape=[
            jax.ShapeDtypeStruct((rows, width), jnp.bfloat16),
            jax.ShapeDtypeStruct((rows, width), jnp.bfloat16),
            jax.ShapeDtypeStruct((couples, 2, rows), jnp.float32),
        ],
        scratch_shapes=[pltpu.VMEM((keys, block), jnp.float32)],
        compiler_params=pltpu.CompilerParams(vmem_limit_bytes=48 * 2**20),
        cost_estimate=pl.CostEstimate(flops=10**8, bytes_accessed=10**5, transcendentals=0),
    )(query_lin, *tables, pairs, pairs_across, doc_query, doc_key)


def attend_back(queries, d_mixed, totals, tables, pairs, pairs_across, doc_query, doc_key):
    rows, width = queries.shape
    block = 256
    keys = WINDOW + block
    couples = width // (2 * HD)
    last = (rows // block - 1, couples - 1)

    def kernel(q_ref, do_ref, total_ref, t0, t1, t2, pairs_ref, across_ref, dq_ref, dk_ref, d_lin_ref, d_pairs_ref, bias, d_keys, d_values, values):
        start = pl.multiple_of(pl.program_id(0) * block, block)
        window = pl.ds(start, keys)

        @pl.when((pl.program_id(0) == 0) & (pl.program_id(1) == 0))
        def clear():
            d_keys[...] = jnp.zeros_like(d_keys)
            d_values[...] = jnp.zeros_like(d_values)
            values[...] = pairs_ref[...][:, HD:]

        @pl.when(pl.program_id(1) == 0)
        def fill():
            bias[...] = no_entry(dq_ref[...], dk_ref[window, :], block, keys)

        own_keys = pairs_ref[window, :][:, :HD]
        own_values = values[window, :]
        keys_across = across_ref[pl.ds(0, HD), window]
        d_turned = []
        for head in range(2):
            part = slice(head * HD, (head + 1) * HD)
            q, do = q_ref[...][:, part], do_ref[...][:, part]
            scores = dot_last(own_keys, q) + bias[...]
            probs = jnp.exp(scores - total_ref[0][head : head + 1, :])
            d_probs = dot_last(own_values, do)
            product = probs * d_probs
            weighted = jnp.sum(product, axis=0, keepdims=True)
            d_scores = (product - probs * weighted).astype(jnp.bfloat16)
            d_turned.append(dot(keys_across, d_scores))
            d_keys[window, :] += dot(d_scores, q)
            d_values[window, :] += dot(probs.astype(jnp.bfloat16), do)
        d_turned = jnp.concatenate(d_turned, axis=0).T
        d_lin = turn(d_turned, (t0[...], t1[...], t2[...]), True) * HD ** (-0.5)
        d_lin_ref[...] = d_lin.astype(jnp.bfloat16)

        @pl.when((pl.program_id(0) == last[0]) & (pl.program_id(1) == last[1]))
        def finish():
            d_pairs_ref[...] = jnp.concatenate([d_keys[...], d_values[...]], axis=1)

    tile = pl.BlockSpec((block, 2 * HD), lambda i, j: (i, j))
    table = pl.BlockSpec((block, 2 * HD), lambda i, j: (i, 0))
    return pl.pallas_call(
        kernel,
        grid=(rows // block, couples),
        in_specs=[
            tile,
            tile,
            pl.BlockSpec((1, 2, block), lambda i, j: (j, 0, i)),
            table,
            table,
            table,
            pl.BlockSpec(pairs.shape, lambda i, j: (0, 0)),
            pl.BlockSpec(pairs_across.shape, lambda i, j: (0, 0)),
            pl.BlockSpec((1, block), lambda i, j: (0, i)),
            pl.BlockSpec(doc_key.shape, lambda i, j: (0, 0)),
        ],
        out_specs=[tile, pl.BlockSpec(pairs.shape, lambda i, j: (0, 0))],
        out_shape=[
            jax.ShapeDtypeStruct((rows, width), jnp.bfloat16),
            jax.ShapeDtypeStruct(pairs.shape, jnp.float32),
        ],
        scratch_shapes=[
            pltpu.VMEM((keys, block), jnp.float32),
            pltpu.VMEM((pairs.shape[0], HD), jnp.float32),
            pltpu.VMEM((pairs.shape[0], HD), jnp.float32),
            pltpu.VMEM((pairs.shape[0], HD), jnp.bfloat16),
        ],
        compiler_params=pltpu.CompilerParams(vmem_limit_bytes=48 * 2**20),
        cost_estimate=pl.CostEstimate(flops=10**8, bytes_accessed=10**5, transcendentals=0),
    )(queries, d_mixed, totals, *tables, pairs, pairs_across, doc_query, doc_key)


def put_pieces(pieces, positions, shards):
    count = len(pieces)
    others, rows, unused_width = pieces[0].shape
    depth = others + 1
    widths = [shard.shape[2] for shard in shards]

    def kernel(positions_ref, *refs):
        i, j = pl.program_id(0), pl.program_id(1)
        sources, locals_, targets = (
            refs[:count],
            refs[count : count + len(shards)],
            refs[count + len(shards) :],
        )
        for at in range(count):

            @pl.when((i == at) & (j < others))
            def take():
                start = 0
                for target, width in zip(targets, widths):
                    target[0, 0] = sources[at][j, :, pl.ds(start, width)]
                    start += width

        @pl.when(j == others)
        def keep():
            for target, source in zip(targets, locals_):
                target[0, 0] = source[0]

    return pl.pallas_call(
        kernel,
        out_shape=[
            jax.ShapeDtypeStruct((depth, count, rows, width), pieces[0].dtype) for width in widths
        ],
        grid_spec=pltpu.PrefetchScalarGridSpec(
            num_scalar_prefetch=1,
            grid=(count, depth),
            in_specs=[pl.BlockSpec(p.shape, lambda i, j, at: (0, 0, 0)) for p in pieces]
            + [pl.BlockSpec((1, rows, width), lambda i, j, at: (at[i], 0, 0)) for width in widths],
            out_specs=[
                pl.BlockSpec(
                    (1, 1, rows, width),
                    lambda i, j, at: (at[count + j], at[i], 0, 0),
                )
                for width in widths
            ],
        ),
        compiler_params=pltpu.CompilerParams(vmem_limit_bytes=40 * 2**20),
    )(positions, *pieces, *shards)


def rest(x, level):
    depth = x.shape[0]
    block = (1,) + x.shape[1:]
    zeros = (0,) * (x.ndim - 1)

    def kernel(level_ref, source, target):
        target[...] = source[...]

    return pl.pallas_call(
        kernel,
        out_shape=jax.ShapeDtypeStruct((depth - 1,) + x.shape[1:], x.dtype),
        grid_spec=pltpu.PrefetchScalarGridSpec(
            num_scalar_prefetch=1,
            grid=(depth - 1,),
            in_specs=[
                pl.BlockSpec(block, lambda i, at: (lax.rem(at[0] + i + 1, depth), *zeros))
            ],
            out_specs=pl.BlockSpec(block, lambda i, at: (i, *zeros)),
        ),
    )(level[None], x)


def spread(pieces, positions, shape, place):
    count = len(pieces)
    rows, width = pieces[0].shape

    def kernel(positions_ref, *refs):
        for at in range(count):

            @pl.when(pl.program_id(0) == at)
            def take():
                refs[-1][...] = refs[at][...].astype(jnp.float32)

    return pl.pallas_call(
        kernel,
        out_shape=jax.ShapeDtypeStruct(shape, jnp.float32),
        grid_spec=pltpu.PrefetchScalarGridSpec(
            num_scalar_prefetch=1,
            grid=(count,),
            in_specs=[pl.BlockSpec((rows, width), lambda i, at: (0, 0))] * count,
            out_specs=pl.BlockSpec((rows, width), lambda i, at: place(at[i])),
        ),
        compiler_params=pltpu.CompilerParams(vmem_limit_bytes=40 * 2**20),
    )(positions, *pieces)


GELU_SCALE = 0.7978845608028654
GELU_CUBE = 0.044715


def dot_first(a, b):
    return lax.dot_general(a, b, (((0,), (0,)), ((), ())), preferred_element_type=jnp.float32)


def feed(facts, x, grad, first_w, second_w, shard, down_pieces, down_shard, block_sum, back_sum, terms):
    rows, width = x.shape
    hidden = first_w.shape[1]
    half = hidden // 2
    column = width // 4
    depth = down_pieces[0].shape[0] + 1
    level_rows = width // depth
    full = depth * hidden
    started = back_sum is not None
    pieces = 8
    f32, bf16 = jnp.float32, jnp.bfloat16

    def kernel(facts_ref, x_ref, g_ref, *refs):
        wa_in, wb_in, shard_in, down_in, block_in = refs[:5]
        down_pieces_in = refs[5 : 5 + pieces]
        refs = refs[5 + pieces :]
        if started:
            back_in = refs[0]
            refs = refs[1 + pieces :]
        block_out, back_out, ga_out, gb_out = refs[:4]
        term_out = refs[4 : 4 + pieces]
        wa, wb, wd, a, b, d, act, da, db, block, back, ga, gb, gd, sems = refs[4 + pieces :]
        chip = facts_ref[1]
        core, level = facts_ref[2], facts_ref[7]

        def rows_of(source, target, side, sem):
            copies = []
            for i in range(1, depth):
                place = pl.multiple_of(lax.rem(level + i, depth) * level_rows, 16)
                copies.append(
                    pltpu.make_async_copy(
                        source.at[pl.ds((i - 1) * level_rows, level_rows)],
                        target.at[pl.ds(place, level_rows)],
                        sem,
                    )
                )
            place = pl.multiple_of(level * level_rows, 16)
            start = pl.multiple_of(side * full + chip * hidden, 128)
            copies.append(
                pltpu.make_async_copy(
                    shard_in.at[:, pl.ds(start, hidden)],
                    target.at[pl.ds(place, level_rows)],
                    sem,
                )
            )
            return copies

        for copy in rows_of(wa_in, wa, core, sems.at[0]):
            copy.start()
        for copy in rows_of(wb_in, wb, 1 - core, sems.at[1]):
            copy.start()

        @pl.when(chip == level)
        def here():
            pltpu.make_async_copy(down_in, wd, sems.at[2]).start()

        @pl.when(chip != level)
        def elsewhere():
            step = lax.rem(chip - level + depth - 1, depth)
            for i in range(pieces):
                side = jnp.where(i < 4, core, 1 - core)
                pltpu.make_async_copy(
                    down_pieces_in[i].at[step],
                    wd.at[
                        pl.ds(pl.multiple_of(side * half, 16), half),
                        pl.ds(pl.multiple_of(facts_ref[3 + i % 4] * column, 128), column),
                    ],
                    sems.at[2],
                ).start()

        load_block = pltpu.make_async_copy(block_in, block, sems.at[3])
        load_block.start()
        if started:
            load_back = pltpu.make_async_copy(back_in, back, sems.at[4])
            load_back.start()
        pltpu.make_async_copy(wa, wa, sems.at[0]).wait()
        a[...] = dot(x_ref[...], wa[...])
        pltpu.make_async_copy(wb, wb, sems.at[1]).wait()
        b[...] = dot(x_ref[...], wb[...])
        pltpu.make_async_copy(wd, wd, sems.at[2]).wait()
        d[...] = dot_last(g_ref[...], wd[...])
        swapped = facts_ref[0] == 1

        @pl.loop(0, rows // 16)
        def glu(i):
            part = pl.ds(pl.multiple_of(i * 16, 16), 16)
            for j in range(hidden // 384):
                lanes = slice(j * 384, (j + 1) * 384)
                one, two, slope = a[part, lanes], b[part, lanes], d[part, lanes]
                gate = jnp.where(swapped, two, one)
                up = jnp.where(swapped, one, two)
                square = gate * gate
                inner = gate * (square * (GELU_SCALE * GELU_CUBE) + GELU_SCALE)
                share = 0.5 * jnp.tanh(inner) + 0.5
                gelu = gate * share
                bend = square * (6.0 * GELU_SCALE * GELU_CUBE) + 2.0 * GELU_SCALE
                rise = share + gelu * (1.0 - share) * bend
                d_gate = (slope * up) * rise
                d_up = slope * gelu
                act[part, lanes] = (gelu * up).astype(bf16)
                da[part, lanes] = jnp.where(swapped, d_up, d_gate).astype(bf16)
                db[part, lanes] = jnp.where(swapped, d_gate, d_up).astype(bf16)

        for i in range(width // 384):
            part = pl.ds(i * 384, 384)
            gb[part, :] = dot_first(x_ref[:, i * 384 : (i + 1) * 384], db[...]).astype(bf16)
            pltpu.make_async_copy(gb.at[part], gb_out.at[part], sems.at[5]).start()
        for i in range(width // 384):
            part = pl.ds(i * 384, 384)
            ga[part, :] = dot_first(x_ref[:, i * 384 : (i + 1) * 384], da[...]).astype(bf16)
            pltpu.make_async_copy(ga.at[part], ga_out.at[part], sems.at[6]).start()
        for i in range(hidden // 384):
            part = pl.ds(i * 384, 384)
            gd[part, :] = dot_first(act[:, i * 384 : (i + 1) * 384], g_ref[...]).astype(bf16)
        stores = []
        for i in range(pieces):
            side = jnp.where(i < 4, core, 1 - core)
            stores.append(
                pltpu.make_async_copy(
                    gd.at[
                        pl.ds(pl.multiple_of(side * half, 16), half),
                        pl.ds(pl.multiple_of(facts_ref[3 + i % 4] * column, 128), column),
                    ],
                    term_out[i].at[chip],
                    sems.at[7 + i],
                )
            )
        for store in stores:
            store.start()
        if started:
            load_back.wait()

            back[...] += dot_last(da[...], wa[...])
            back[...] += dot_last(db[...], wb[...])
        else:
            back[...] = dot_last(da[...], wa[...])
            back[...] += dot_last(db[...], wb[...])
        store_back = pltpu.make_async_copy(back, back_out, sems.at[15])
        store_back.start()
        load_block.wait()
        for i in range(2):
            part = pl.ds(i * (rows // 2), rows // 2)
            block[part, :] += dot(act[part, :], wd[...])
            pltpu.make_async_copy(block.at[part], block_out.at[part], sems.at[16]).start()
        for store in stores:
            store.wait()
        pltpu.make_async_copy(gb, gb_out, sems.at[5]).wait()
        pltpu.make_async_copy(ga, ga_out, sems.at[6]).wait()
        store_back.wait()
        pltpu.make_async_copy(block, block_out, sems.at[16]).wait()

    anywhere = pl.BlockSpec(memory_space=pl.ANY)
    inside = pl.BlockSpec(memory_space=pltpu.VMEM)
    operands = [facts, x, grad, first_w, second_w, shard, down_shard, block_sum, *down_pieces]
    aliases = {}
    if started:
        aliases[7] = 0
        aliases[len(operands)] = 1
        operands.append(back_sum)
        for i, term in enumerate(terms):
            aliases[len(operands)] = 4 + i
            operands.append(term)
    sums = jax.ShapeDtypeStruct((rows, width), f32)
    grads = jax.ShapeDtypeStruct((width, hidden), bf16)
    results = pl.pallas_call(
        kernel,
        in_specs=[pl.BlockSpec(memory_space=pltpu.SMEM), inside, inside]
        + [anywhere] * (len(operands) - 3),
        out_specs=[anywhere] * (4 + pieces),
        out_shape=[sums, sums, grads, grads]
        + [jax.ShapeDtypeStruct((depth, half, column), bf16)] * pieces,
        input_output_aliases=aliases,
        scratch_shapes=[
            pltpu.VMEM((width, hidden), bf16),
            pltpu.VMEM((width, hidden), bf16),
            pltpu.VMEM((hidden, width), bf16),
            pltpu.VMEM((rows, hidden), f32),
            pltpu.VMEM((rows, hidden), f32),
            pltpu.VMEM((rows, hidden), f32),
            pltpu.VMEM((rows, hidden), bf16),
            pltpu.VMEM((rows, hidden), bf16),
            pltpu.VMEM((rows, hidden), bf16),
            pltpu.VMEM((rows, width), f32),
            pltpu.VMEM((rows, width), f32),
            pltpu.VMEM((width, hidden), bf16),
            pltpu.VMEM((width, hidden), bf16),
            pltpu.VMEM((hidden, width), bf16),
            pltpu.SemaphoreType.DMA((17,)),
        ],
        compiler_params=pltpu.CompilerParams(vmem_limit_bytes=56 * 2**20),
        cost_estimate=pl.CostEstimate(flops=10**8, bytes_accessed=10**5, transcendentals=0),
    )(*operands)
    return results[0], results[1], results[2], results[3], results[4:]


class Plane:
    def __init__(self):
        self.me = lax.axis_index("seq")
        self.core = self.me % 2
        self.chip = self.me // 2
        first = jnp.where(self.core == 0, 1, 2)
        self.chips = [self.chip, self.chip ^ first, self.chip ^ (3 - first), self.chip ^ 3]
        self.first_pairs = [(i, i ^ (2 if i % 2 == 0 else 4)) for i in range(8)]
        self.second_pairs = [(i, i ^ (4 if i % 2 == 0 else 2)) for i in range(8)]
        self.core_pairs = [(i, i ^ 1) for i in range(8)]
        self.sources = jnp.stack(
            [chip * 2 + self.core for chip in self.chips]
            + [chip * 2 + 1 - self.core for chip in self.chips]
        )

    def first(self, x):
        return lax.ppermute(x, "seq", self.first_pairs)

    def second(self, x):
        return lax.ppermute(x, "seq", self.second_pairs)

    def along(self, x):
        depth = lax.axis_size("fsdp")
        return [
            lax.ppermute(x, "fsdp", [((i + k) % depth, i) for i in range(depth)])
            for k in range(1, depth)
        ]

    def swap(self, x):
        return lax.ppermute(x, "seq", self.core_pairs)

    def down_columns(self, x):
        return lax.psum_scatter(x, "fsdp", scatter_dimension=0, tiled=True)


def places_of(arrival_order, ranks):
    row_count = arrival_order.shape[1]
    capacity = 2 * row_count // ranks
    arrived_at = arrival_order[0]
    owner = arrived_at // row_count
    owner_hits = (owner[:, None] == jnp.arange(ranks, dtype=jnp.int32)[None, :]).astype(jnp.int32)
    within = jnp.sum(jnp.cumsum(owner_hits, axis=0) * owner_hits, axis=1) - 1
    return owner * capacity + within, arrived_at % row_count


def to_slots(rows, slots, ranks, empty=0):
    capacity = 2 * rows.shape[0] // ranks
    out = jnp.full((ranks * capacity,) + rows.shape[1:], empty, rows.dtype)
    return out.at[slots].set(rows).reshape((ranks, capacity) + rows.shape[1:])


def from_slots(slots, landing):
    flat = slots.reshape((-1, slots.shape[-1]))
    out = jnp.zeros((flat.shape[0] // 2, flat.shape[1]), flat.dtype)
    return out.at[landing].set(flat, mode="drop")


def back_to_slots(rows, safe_place, ranks):
    return rows[safe_place].reshape(ranks, -1, rows.shape[1])


def exchange(x):
    return lax.all_to_all(x, "seq", split_axis=0, concat_axis=0, tiled=True)


def positions_of(lengths, row_count):
    position = lax.axis_index("seq")
    places = position * row_count + jnp.arange(row_count, dtype=jnp.int32)
    doc_query, offset_query = layout(lengths[0], places)
    key_places = (
        position * row_count - WINDOW + jnp.arange(WINDOW + row_count, dtype=jnp.int32)
    )
    doc_key, unused_offset = layout(lengths[0], key_places)
    cosine, sine = angles(offset_query.astype(jnp.float32), HD)
    return (doc_query[None, :], doc_key[:, None]), cosine, sine


def pair_of(kv_lin, cosine, sine):
    own_keys = rounded(rotate(kv_lin[:, :HD], cosine, sine))
    return jnp.concatenate([own_keys, rounded(kv_lin[:, HD:])], axis=1)


def with_earlier(pair, reach):
    return jnp.concatenate(
        [passed_along(pair, "seq", distance) for distance in range(reach, 0, -1)] + [pair], axis=0
    )


def owners_sum(d_pairs, row_count, reach):
    parts = [
        passed_along(
            rounded(d_pairs[(reach - distance) * row_count :][:row_count]), "seq", -distance
        )
        for distance in range(reach, 0, -1)
    ]
    own = d_pairs[reach * row_count :]
    for part in parts:
        own = own + widened(part)
    return own


def body(*operands):
    return square_body(*operands) if lax.axis_size("seq") == 8 else plain_body(*operands)


def plain_body(
    tokens,
    cotangent,
    arrival_order,
    lengths,
    norm_gain,
    w_query,
    w_kv,
    w_out,
    ffn_gain,
    w_gate_up,
    w_down,
):
    row_count = tokens.shape[1]
    ranks = lax.axis_size("seq")
    reach = WINDOW // row_count
    position = lax.axis_index("seq")

    def whole(shard):
        part = shard.shape[0] // ranks
        mine = lax.dynamic_slice_in_dim(shard, position * part, part, axis=0)
        return lax.all_gather(mine, ("fsdp", "seq"), axis=0, tiled=True)

    def summed(grad):
        mine = lax.psum_scatter(rounded(grad), ("fsdp", "seq"), scatter_dimension=0, tiled=True)
        return widened(lax.all_gather(mine, "seq", axis=0, tiled=True))

    send_slot, send_place = places_of(arrival_order, ranks)
    got_tokens = exchange(to_slots(tokens[0], send_slot, ranks))
    got_cotangent = exchange(to_slots(cotangent[0], send_slot, ranks))
    recv_place = exchange(to_slots(send_place, send_slot, ranks, -1)).reshape(-1)
    is_live = recv_place >= 0
    landing = jnp.where(is_live, recv_place, row_count)
    safe_place = jnp.where(is_live, recv_place, 0)
    packed_f = widened(from_slots(got_tokens, landing))
    packed_grad = from_slots(got_cotangent, landing)
    query_w, kv_w, out_w, down_w, gate_up_w = (
        whole(w_query),
        whole(w_kv),
        whole(w_out),
        whole(w_down),
        whole(w_gate_up),
    )
    gain_attn, gain_ffn = (
        widened(lax.all_gather(gain, "fsdp", axis=0, tiled=True)) for gain in (norm_gain, ffn_gain)
    )
    docs, cosine, sine = positions_of(lengths, row_count)
    tables = tables_of(cosine, sine, 2, 0)

    normed = rounded(rms_scale(packed_f, gain_attn))
    pair_rows = with_earlier(pair_of(dot(normed, kv_w), cosine, sine), reach)
    queries, mixed, totals = attend(dot(normed, query_w), tables, pair_rows, pair_rows.T, *docs)
    hidden_state = packed_f + dot(mixed, out_w)
    ffn_in = rounded(rms_scale(hidden_state, gain_ffn))
    gate, up = dot(ffn_in, gate_up_w[:, :FF]), dot(ffn_in, gate_up_w[:, FF:])
    activated, pull = jax.vjp(lambda g, u: jax.nn.gelu(g, approximate=True) * u, gate, up)
    activated = rounded(activated)
    block_rows = rounded(hidden_state + dot(activated, down_w))

    d_gate, d_up = pull(dot_across(packed_grad, down_w))
    d_gate_up = jnp.concatenate([rounded(d_gate), rounded(d_up)], axis=1)
    unused_scaled, ffn_norm_pull = jax.vjp(rms_scale, hidden_state, gain_ffn)
    d_hidden_norm, grad_gain_ffn = ffn_norm_pull(dot_across(d_gate_up, gate_up_w))
    d_hidden = widened(packed_grad) + d_hidden_norm
    d_branch = rounded(d_hidden)
    d_mixed = rounded(dot_across(d_branch, out_w))
    d_query_lin, d_pairs = attend_back(
        queries, d_mixed, totals, tables, pair_rows, pair_rows.T, *docs
    )
    d_own = owners_sum(d_pairs, row_count, reach)
    d_kv_lin = rounded(
        jnp.concatenate([unrotate(d_own[:, :HD], cosine, sine), d_own[:, HD:]], axis=1)
    )
    d_normed = dot_across(d_query_lin, query_w) + dot_across(d_kv_lin, kv_w)
    unused_normed, attn_norm_pull = jax.vjp(rms_scale, packed_f, gain_attn)
    d_packed_norm, grad_gain_attn = attn_norm_pull(d_normed)
    grad_rows = rounded(d_hidden + d_packed_norm)
    block_arrived, grad_arrived = (
        exchange(back_to_slots(rows, safe_place, ranks)).reshape(-1, rows.shape[1])[
            send_slot
        ]
        for rows in (block_rows, grad_rows)
    )
    total_gain_attn, total_gain_ffn = (
        lax.psum(lax.psum_scatter(gain, "fsdp", scatter_dimension=0, tiled=True), "seq")
        for gain in (grad_gain_attn, grad_gain_ffn)
    )
    return (
        block_arrived[None],
        grad_arrived[None],
        total_gain_attn,
        summed(dot_rows(normed, d_query_lin)),
        summed(dot_rows(normed, d_kv_lin)),
        summed(dot_rows(mixed, d_branch)),
        total_gain_ffn,
        summed(dot_rows(ffn_in, d_gate_up)),
        summed(dot_rows(activated, packed_grad)),
    )


def square_body(
    tokens,
    cotangent,
    arrival_order,
    lengths,
    norm_gain,
    w_query,
    w_kv,
    w_out,
    ffn_gain,
    w_gate_up,
    w_down,
):
    row_count = tokens.shape[1]
    model_width = tokens.shape[2]
    ranks = lax.axis_size("seq")
    depth = lax.axis_size("fsdp")
    reach = WINDOW // row_count
    shard_rows = w_query.shape[0]
    part_rows = shard_rows // ranks
    quarter = FF // 4
    column = model_width // 4
    half_rows = w_down.shape[0] // 2
    split = model_width + 2 * HD
    plane = Plane()
    level = lax.axis_index("fsdp").astype(jnp.int32)
    levels = (level + 1 + jnp.arange(depth, dtype=jnp.int32)) % depth
    at = jnp.concatenate([plane.sources, levels]).astype(jnp.int32)

    def my_rows(shard):
        return lax.dynamic_slice_in_dim(shard, plane.me * part_rows, part_rows, axis=0)

    def by_parts(shard):
        return shard.reshape(ranks, part_rows, shard.shape[1])

    def second_halves(slots):
        return [plane.swap(slots[i]) for i in (0, 2, 1, 3)]


    gains = jnp.concatenate([norm_gain, ffn_gain]).reshape(part_rows, -1)
    gain_width = gains.shape[1]
    early = plane.along(
        jnp.concatenate(
            [my_rows(w_query), my_rows(w_kv), jnp.pad(gains, ((0, 0), (0, 128 - gain_width)))],
            axis=1,
        )
    )
    send_slot, send_place = places_of(arrival_order, ranks)
    labels = jnp.stack([send_place // 2, send_place % 2, jnp.ones_like(send_place)], axis=1)
    labels = jnp.pad(labels.astype(jnp.bfloat16), ((0, 0), (0, 125)))
    token_slots = to_slots(jnp.concatenate([tokens[0], labels], axis=1), send_slot, ranks)
    got_tokens = exchange(token_slots)
    *early, cotangent_rows, out_mine, down_mine, gate_up_mine = fence(
        *early, after(cotangent[0], token_slots), my_rows(w_out), w_down, w_gate_up
    )
    early = jnp.stack(early)
    gain_rows = early[:, :, split : split + gain_width].reshape(depth - 1, 2, shard_rows)
    early = early[:, :, :split]

    def down_of(shard, chip):
        piece = lax.dynamic_slice(
            shard, (plane.core * half_rows, chip * column), (half_rows, column)
        )
        return lax.all_gather(piece, "fsdp", axis=0, tiled=False)

    down_piece = down_of(down_mine, plane.chip)
    gate_up_piece = lax.dynamic_slice(
        gate_up_mine, (0, plane.core * FF + plane.chip * quarter), (shard_rows, quarter)
    )
    gate_up_piece = lax.all_gather(gate_up_piece, "fsdp", axis=0, tiled=False)

    early_u, early_v, early_0 = plane.first(early), plane.second(early), plane.swap(early)
    out = plane.along(out_mine)
    docs, cosine, sine = positions_of(lengths, row_count)
    tables = rows_first(tables_of(cosine, sine, 2, 0))
    cotangent_slots = to_slots(cotangent_rows, send_slot, ranks)
    early_u, early_v, early_0, got_tokens, out, cotangent_slots, tables = fence(
        early_u, early_v, early_0, got_tokens, out, cotangent_slots, tables
    )
    got_cotangent = exchange(cotangent_slots)

    out = jnp.stack(out)
    early_d, early_2, early_1 = plane.second(early_u), plane.swap(early_u), plane.swap(early_v)
    out_u, out_v, out_0 = plane.first(out), plane.second(out), plane.swap(out)
    labels = got_tokens.reshape(-1, model_width + 128)[:, model_width:].astype(jnp.int32)
    safe_place = labels[:, 0] * 2 + labels[:, 1]
    is_live = labels[:, 2] == 1
    landing = jnp.where(is_live, safe_place, row_count)
    packed_f = widened(from_slots(got_tokens, landing)[:, :model_width])
    gain_rows = jnp.concatenate([gain_rows, gains.reshape(1, 2, shard_rows)], axis=0)
    gain_rows = gain_rows[(jnp.arange(depth, dtype=jnp.int32) + depth - 1 - level) % depth]
    gain_attn = widened(gain_rows[:, 0].reshape(model_width))
    gain_ffn = widened(gain_rows[:, 1].reshape(model_width))
    normed = rounded(rms_scale(packed_f, gain_attn))
    early_d, early_2, early_1, out_u, out_v, out_0, normed = fence(
        early_d, early_2, early_1, out_u, out_v, out_0, normed
    )

    early_3, out_d, out_2, out_1 = (
        plane.swap(early_d),
        plane.second(out_u),
        plane.swap(out_u),
        plane.swap(out_v),
    )
    down_piece = rest(after(down_piece, normed), level)
    early_3, out_d, out_2, out_1, down_piece = fence(early_3, out_d, out_2, out_1, down_piece)

    down_u, down_v, down_0 = (
        plane.first(down_piece),
        plane.second(down_piece),
        plane.swap(down_piece),
    )
    out_3 = plane.swap(out_d)
    query_w, kv_w = put_pieces(
        [early, early_u, early_v, early_d, early_0, early_1, early_2, early_3],
        after(at, down_piece),
        [by_parts(w_query), by_parts(w_kv)],
    )
    query_w = query_w.reshape(model_width, model_width)
    kv_w = kv_w.reshape(model_width, 2 * HD)
    query_lin = dot(normed, query_w)
    pair = pair_of(dot(normed, kv_w), cosine, sine)
    (out_w,) = put_pieces(
        [out, out_u, out_v, out_d, out_0, out_1, out_2, out_3],
        after(at, pair),
        [by_parts(w_out)],
    )
    out_w = out_w.reshape(model_width, model_width)
    down_u, down_v, down_0, out_w, query_lin, pair = fence(
        down_u, down_v, down_0, out_w, query_lin, pair
    )

    pair_rows = with_earlier(pair, reach)
    down_2, down_1 = plane.swap(down_u), plane.swap(down_v)
    down_d = down_of(after(w_down, gate_up_piece), plane.chips[3])
    gate_up_piece = rest(gate_up_piece, level)
    gate_up_piece = gate_up_piece.reshape((depth - 1) * shard_rows, quarter)
    packed_grad = from_slots(after(got_cotangent, gate_up_piece), landing)
    pair_rows, down_2, down_1, gate_up_piece, packed_grad = fence(
        pair_rows, down_2, down_1, gate_up_piece, packed_grad
    )

    gate_up_u, gate_up_v, gate_up_0 = (
        plane.first(gate_up_piece),
        plane.second(gate_up_piece),
        plane.swap(gate_up_piece),
    )
    pairs_across = pair_rows.T
    queries, mixed, totals = attend(query_lin, tables, pair_rows, pairs_across, *docs)
    down_d = rest(after(down_d, mixed), level)
    down_3 = plane.swap(down_d)
    hidden_state = packed_f + dot(after(mixed, down_d), out_w)
    ffn_in = rounded(rms_scale(hidden_state, gain_ffn))

    def chunk(slot, first_w, second_w, chunk_in, block_sum, back_sum, terms):
        facts = [plane.core, plane.chips[slot], plane.core, *plane.chips, level]
        return feed(
            jnp.stack(facts).astype(jnp.int32),
            chunk_in,
            packed_grad,
            first_w,
            second_w,
            w_gate_up,
            [down_piece, down_u, down_v, down_d, down_0, down_1, down_2, down_3],
            w_down,
            block_sum,
            back_sum,
            terms,
        )

    block_sum, back_sum, own_0, other_0, terms = chunk(
        0, gate_up_piece, gate_up_0, ffn_in, hidden_state, None, None
    )
    gate_up_u, gate_up_v, block_sum, back_sum, own_0, other_0 = fence(
        gate_up_u, gate_up_v, block_sum, back_sum, own_0, other_0
    )

    gate_up_2, gate_up_1 = plane.swap(gate_up_u), plane.swap(gate_up_v)
    gate_up_2, gate_up_1, gate_up_u, back_sum = fence(gate_up_2, gate_up_1, gate_up_u, back_sum)
    gate_up_d, swap_0 = plane.second(gate_up_u), plane.swap(other_0)
    block_sum, back_sum, own_u, other_u, terms = chunk(
        1, gate_up_u, gate_up_1, ffn_in, block_sum, back_sum, terms
    )
    gate_up_d, swap_0, block_sum, back_sum, own_u, other_u = fence(
        gate_up_d, swap_0, block_sum, back_sum, own_u, other_u
    )
    gate_up_3, swap_u = plane.swap(gate_up_d), plane.swap(other_u)
    block_sum, back_sum, own_v, other_v, terms = chunk(
        2, gate_up_v, gate_up_2, ffn_in, block_sum, back_sum, terms
    )
    gate_up_3, swap_u, block_sum, back_sum, own_v, other_v = fence(
        gate_up_3, swap_u, block_sum, back_sum, own_v, other_v
    )
    sum_v, other_v, back_sum = fence(added(own_v, swap_u), other_v, back_sum)
    from_v, swap_v = plane.second(sum_v), plane.swap(other_v)
    block_sum, back_sum, own_d, other_d, terms = chunk(
        3, gate_up_d, gate_up_3, ffn_in, block_sum, back_sum, terms
    )
    sum_u = added(own_u, swap_v)
    from_v, sum_u, block_sum, back_sum, own_d, other_d, terms = fence(
        from_v, sum_u, block_sum, back_sum, own_d, other_d, terms
    )

    from_u, swap_d = plane.first(sum_u), plane.swap(other_d)
    terms = [term.reshape(depth * half_rows, column) for term in terms]
    down_swaps = [plane.swap(term) for term in terms[4:]]
    unused_scaled, ffn_norm_pull = jax.vjp(rms_scale, hidden_state, gain_ffn)
    d_hidden_norm, grad_gain_ffn = ffn_norm_pull(back_sum)
    d_hidden = widened(packed_grad) + d_hidden_norm
    d_branch = rounded(d_hidden)
    d_mixed = rounded(dot_across(d_branch, out_w))
    sum_d = added_apart(after(own_d, d_mixed), swap_d)
    part_d = plane.down_columns(sum_d)
    down_sums = [
        added_apart(after(term, sum_d), down_swaps[match])
        for term, match in zip(terms[:4], (0, 2, 1, 3))
    ]
    from_u, d_branch, d_mixed, down_sums = fence(from_u, d_branch, d_mixed, down_sums)
    from_down_d, from_down_v = plane.second(down_sums[3]), plane.second(down_sums[2])
    total = added(own_0, swap_0, from_v, from_u)
    part_0 = plane.down_columns(total)
    d_query_lin, d_pairs = attend_back(
        queries, after(d_mixed, total), totals, tables, pair_rows, pairs_across, *docs
    )
    from_down_d, from_down_v, d_query_lin, d_pairs, block_sum, part_d = fence(
        from_down_d, from_down_v, d_query_lin, d_pairs, block_sum, part_d
    )
    part_d_u = plane.first(part_d)

    def by_rows(grad):
        pieces = rounded(grad).reshape(depth, ranks, part_rows, grad.shape[1])
        return [
            lax.dynamic_index_in_dim(pieces, plane.sources[i], axis=1, keepdims=False)
            for i in range(8)
        ]

    d_own = owners_sum(d_pairs, row_count, reach)
    down_u = added(down_sums[1], from_down_d)
    block_slots = back_to_slots(rounded(block_sum), safe_place, ranks)
    d_own, down_u, block_slots, part_d_u = fence(d_own, down_u, block_slots, part_d_u)
    home_out = exchange(block_slots)
    from_down_u, part_d = plane.first(down_u), plane.second(part_d_u)
    grad_out = dot_rows(mixed, after(d_branch, block_slots))
    out_terms = [p.reshape(depth * part_rows, model_width) for p in by_rows(grad_out)]
    out_swaps = [plane.swap(term) for term in out_terms[4:]]
    d_kv_lin = rounded(
        jnp.concatenate([unrotate(d_own[:, :HD], cosine, sine), d_own[:, HD:]], axis=1)
    )
    grad_query = dot_rows(normed, after(d_query_lin, *out_terms))
    grad_kv = dot_rows(normed, d_kv_lin)
    d_normed = dot_across(d_query_lin, query_w) + dot_across(d_kv_lin, kv_w)
    unused_normed, attn_norm_pull = jax.vjp(rms_scale, packed_f, gain_attn)
    d_packed_norm, grad_gain_attn = attn_norm_pull(d_normed)
    grad_rows = rounded(d_hidden + d_packed_norm)
    gain_rows = jnp.concatenate(
        [
            rounded(grad_gain_attn).reshape(depth, 1, shard_rows),
            rounded(grad_gain_ffn).reshape(depth, 1, shard_rows),
        ],
        axis=2,
    )
    gain_rows = jnp.pad(gain_rows, ((0, 0), (0, 15), (0, split - 2 * shard_rows)))
    early_terms = [
        jnp.concatenate([jnp.concatenate([q, k], axis=2), gain_rows], axis=1).reshape(
            depth * (part_rows + 16), split
        )
        for q, k in zip(by_rows(grad_query), by_rows(grad_kv))
    ]
    grad_slots = back_to_slots(after(grad_rows, *early_terms), safe_place, ranks)
    from_down_u, part_d, early_terms, out_swaps, grad_slots, home_out = fence(
        from_down_u, part_d, early_terms, out_swaps, grad_slots, home_out
    )

    home_grad = exchange(grad_slots)
    early_swaps = [plane.swap(term) for term in early_terms[4:]]
    out_d, out_v = added(out_terms[3], out_swaps[3]), added(out_terms[2], out_swaps[1])
    out_from_d, out_from_v = plane.second(out_d), plane.second(out_v)
    total = added(after(down_sums[0], out_d, out_v), from_down_v, from_down_u)
    mine_down = plane.down_columns(total)
    early_d = added(early_terms[3], early_swaps[3])
    early_v = added(early_terms[2], early_swaps[1])
    block_arrived = home_out.reshape(-1, model_width)[send_slot]
    out_from_d, out_from_v, early_d, early_v, early_swaps, part_0, block_arrived = fence(
        out_from_d, out_from_v, early_d, early_v, early_swaps, part_0, block_arrived
    )

    mine_gate_up = added(part_0, part_d)
    early_from_d, early_from_v = plane.second(early_d), plane.second(early_v)
    out_from_u = plane.first(added(out_terms[1], out_swaps[2], out_from_d))
    gate_up_u, gate_up_v, gate_up_0 = (
        plane.first(mine_gate_up),
        plane.second(mine_gate_up),
        plane.swap(mine_gate_up),
    )
    total = added(out_terms[0], out_swaps[0], out_from_v, out_from_u)
    mine_out = plane.down_columns(total)
    early_from_d, early_from_v, total, gate_up_u, gate_up_v, gate_up_0, home_grad = fence(
        early_from_d, early_from_v, total, gate_up_u, gate_up_v, gate_up_0, home_grad
    )

    early_from_u = plane.first(added(early_terms[1], early_swaps[2], early_from_d))
    gate_up_d, gate_up_2, gate_up_1 = (
        plane.second(gate_up_u),
        plane.swap(gate_up_u),
        plane.swap(gate_up_v),
    )
    grad_arrived = home_grad.reshape(-1, model_width)[send_slot]
    early_from_u, gate_up_d, gate_up_2, gate_up_1, mine_down, mine_out, grad_arrived = fence(
        early_from_u, gate_up_d, gate_up_2, gate_up_1, mine_down, mine_out, grad_arrived
    )

    total = added(early_terms[0], early_swaps[0], early_from_v, early_from_u)
    mine_early = plane.down_columns(total)
    gate_up_3 = plane.swap(gate_up_d)
    down_own = [mine_down, plane.first(mine_down), plane.second(mine_down)]
    total_gate_up = spread(
        [mine_gate_up, gate_up_u, gate_up_v, gate_up_d]
        + [gate_up_0, gate_up_1, gate_up_2, gate_up_3],
        after(plane.sources, total),
        (shard_rows, 2 * FF),
        lambda p: (0, (p % 2) * 4 + p // 2),
    )
    out_own = [mine_out, plane.first(mine_out), plane.second(mine_out)]
    down_own, out_own, total_gate_up = fence(down_own, out_own, total_gate_up)

    down_own.append(plane.second(down_own[1]))
    down_swaps = [plane.swap(piece) for piece in down_own[:3]]
    out_own.append(plane.second(out_own[1]))
    down_own, down_swaps, out_own, mine_early = fence(down_own, down_swaps, out_own, mine_early)

    down_swaps.append(plane.swap(down_own[3]))
    piece = mine_early[:part_rows]
    early_own = [piece, plane.first(piece), plane.second(piece)]
    total_down = spread(
        down_own + [down_swaps[i] for i in (0, 2, 1, 3)],
        plane.sources,
        (2 * half_rows, model_width),
        lambda p: (p % 2, p // 2),
    )
    early_own, total_down = fence(early_own, total_down)
    early_own.append(plane.second(early_own[1]))
    total_out = spread(
        out_own + second_halves(out_own),
        plane.sources,
        (shard_rows, model_width),
        lambda p: (p, 0),
    )
    early_own, total_out = fence(early_own, total_out)
    total_early = spread(
        early_own + second_halves(early_own),
        plane.sources,
        (shard_rows, split),
        lambda p: (p, 0),
    )
    return (
        block_arrived[None],
        grad_arrived[None],
        widened(mine_early[part_rows, :shard_rows]),
        total_early[:, :model_width],
        total_early[:, model_width:],
        total_out,
        widened(mine_early[part_rows, shard_rows : 2 * shard_rows]),
        total_gate_up,
        total_down,
    )


def solution(mesh):
    placed = (
        P("fsdp", "seq", None),
        P("fsdp", "seq", None),
        P("fsdp", "seq"),
        P("fsdp", None),
        P("fsdp"),
        P("fsdp", None),
        P("fsdp", None),
        P("fsdp", None),
        P("fsdp"),
        P("fsdp", None),
        P("fsdp", None),
    )
    return jax.shard_map(
        body,
        mesh=mesh,
        in_specs=placed,
        out_specs=(
            P("fsdp", "seq", None),
            P("fsdp", "seq", None),
            P("fsdp"),
            P("fsdp", None),
            P("fsdp", None),
            P("fsdp", None),
            P("fsdp"),
            P("fsdp", None),
            P("fsdp", None),
        ),
        check_vma=False,
    )
```

```python
import jax
import jax.numpy as jnp
from jax import lax
from jax.experimental import pallas as pl
from jax.experimental.pallas import tpu as pltpu
from jax.sharding import PartitionSpec as P

HD = 192
FF = 4608
WINDOW = 1024


EPSILON = 1e-06
ROPE_BASE = 10000.0
MASKED = -1e30


def passed_along(x, axis, by):
    length = lax.axis_size(axis)
    pairs = [(i, i + by) for i in range(length) if 0 <= i + by < length]
    return lax.ppermute(x, axis, pairs)


def rms_scale(values, gain):
    return values * lax.rsqrt(jnp.mean(values * values, axis=-1, keepdims=True) + EPSILON) * gain


def rotate(heads, cosine, sine):
    half = heads.shape[-1] // 2
    first_half = heads[..., :half]
    second_half = heads[..., half:]
    return jnp.concatenate(
        [first_half * cosine - second_half * sine, second_half * cosine + first_half * sine],
        axis=-1,
    )


def unrotate(heads, cosine, sine):
    half = heads.shape[-1] // 2
    first_half = heads[..., :half]
    second_half = heads[..., half:]
    return jnp.concatenate(
        [first_half * cosine + second_half * sine, second_half * cosine - first_half * sine],
        axis=-1,
    )


def angles(places, head_width):
    steps_half = jnp.arange(head_width // 2, dtype=jnp.float32)
    inverse = ROPE_BASE ** (-2.0 * steps_half / head_width)
    theta = places[:, None] * inverse[None, :]
    return (jnp.cos(theta), jnp.sin(theta))


def layout(lengths, places):
    ends = jnp.cumsum(lengths)
    starts = ends - lengths
    inside = (places[:, None] >= starts[None, :]) & (places[:, None] < ends[None, :])
    numbers = jnp.arange(1, lengths.shape[0] + 1, dtype=jnp.int32)
    document = jnp.sum(jnp.where(inside, numbers[None, :], 0), axis=1) - 1
    offset = places - jnp.sum(jnp.where(inside, starts[None, :], 0), axis=1)
    return (document, offset)


def after(x, *done):
    return lax.optimization_barrier((x, *done))[0]


def fence(*xs):
    return lax.optimization_barrier(xs)


def rounded(x):
    return x.astype(jnp.bfloat16)


def widened(x):
    return x.astype(jnp.float32)


def added(*terms):
    return rounded(sum(widened(term) for term in terms))


def added_apart(*terms):
    rows, width = terms[0].shape
    steps = 4

    def kernel(*refs):
        refs[-1][...] = rounded(sum(widened(ref[...]) for ref in refs[:-1]))

    block = pl.BlockSpec((rows // steps, width), lambda i: (i, 0))
    return pl.pallas_call(
        kernel,
        grid=(steps,),
        in_specs=[block] * len(terms),
        out_specs=block,
        out_shape=jax.ShapeDtypeStruct((rows, width), jnp.bfloat16),
        compiler_params=pltpu.CompilerParams(vmem_limit_bytes=32 * 2**20),
        cost_estimate=pl.CostEstimate(flops=10**6, bytes_accessed=10**5, transcendentals=0),
    )(*terms)


def dot(a, b):
    return jnp.dot(a, b, preferred_element_type=jnp.float32)


def dot_rows(a, b):
    return jnp.einsum("td,tf->df", a, b, preferred_element_type=jnp.float32)


def dot_across(a, b):
    return jnp.einsum("tf,df->td", a, b, preferred_element_type=jnp.float32)


def turn(x, tables, back):
    width = x.shape[-1]
    half = HD // 2
    later = pltpu.roll(x, width - half, axis=1)
    sooner = pltpu.roll(x, half, axis=1)
    turned = later * tables[1] + sooner * tables[2]
    return x * tables[0] - turned if back else x * tables[0] + turned


def tables_of(cosine, sine, heads, still):
    none = jnp.zeros_like(sine)
    ones = jnp.ones_like(sine)
    return (
        jnp.concatenate([cosine, cosine] * heads + [ones, ones] * still, axis=1),
        jnp.concatenate([-sine, none] * heads + [none, none] * still, axis=1),
        jnp.concatenate([none, sine] * heads + [none, none] * still, axis=1),
    )


def rows_first(arrays):
    def kernel(*refs):
        for source, target in zip(refs, refs[len(arrays) :]):
            target[...] = source[...]

    return pl.pallas_call(
        kernel, out_shape=[jax.ShapeDtypeStruct(x.shape, x.dtype) for x in arrays]
    )(*arrays)


def no_entry(doc_query, doc_key, rows, keys):
    key = lax.broadcasted_iota(jnp.int32, (keys, rows), 0)
    row = lax.broadcasted_iota(jnp.int32, (keys, rows), 1)
    gap = WINDOW + row - key
    seen = (doc_key == doc_query) & (doc_key >= 0) & (gap >= 0) & (gap < WINDOW)
    return jnp.where(seen, 0.0, MASKED)


def dot_last(a, b):
    return lax.dot_general(a, b, (((1,), (1,)), ((), ())), preferred_element_type=jnp.float32)


def attend(query_lin, tables, pairs, pairs_across, doc_query, doc_key):
    rows, width = query_lin.shape
    block = 256
    keys = WINDOW + block
    couples = width // (2 * HD)

    def kernel(q_ref, t0, t1, t2, pairs_ref, across_ref, dq_ref, dk_ref, turned_ref, mixed_ref, total_ref, bias):
        start = pl.multiple_of(pl.program_id(0) * block, block)
        window = pl.ds(start, keys)

        @pl.when(pl.program_id(1) == 0)
        def fill():
            bias[...] = no_entry(dq_ref[...], dk_ref[window, :], block, keys)

        queries = turn(q_ref[...], (t0[...], t1[...], t2[...]), False) * HD ** (-0.5)
        queries = queries.astype(jnp.bfloat16)
        turned_ref[...] = queries
        own_keys = pairs_ref[window, :][:, :HD]
        values = across_ref[pl.ds(HD, HD), window]
        mixed, totals = [], []
        for head in range(2):
            scores = dot_last(own_keys, queries[:, head * HD : (head + 1) * HD]) + bias[...]
            top = jnp.max(scores, axis=0, keepdims=True)
            weights = jnp.exp(scores - top)
            total = jnp.sum(weights, axis=0, keepdims=True)
            totals.append(top + jnp.log(total))
            mixed.append(dot(values, weights.astype(jnp.bfloat16)) * (1.0 / total))
        mixed_ref[...] = jnp.concatenate(mixed, axis=0).T.astype(jnp.bfloat16)
        total_ref[0] = jnp.concatenate(totals, axis=0)

    tile = pl.BlockSpec((block, 2 * HD), lambda i, j: (i, j))
    table = pl.BlockSpec((block, 2 * HD), lambda i, j: (i, 0))
    return pl.pallas_call(
        kernel,
        grid=(rows // block, couples),
        in_specs=[
            tile,
            table,
            table,
            table,
            pl.BlockSpec(pairs.shape, lambda i, j: (0, 0)),
            pl.BlockSpec(pairs_across.shape, lambda i, j: (0, 0)),
            pl.BlockSpec((1, block), lambda i, j: (0, i)),
            pl.BlockSpec(doc_key.shape, lambda i, j: (0, 0)),
        ],
        out_specs=[tile, tile, pl.BlockSpec((1, 2, block), lambda i, j: (j, 0, i))],
        out_shape=[
            jax.ShapeDtypeStruct((rows, width), jnp.bfloat16),
            jax.ShapeDtypeStruct((rows, width), jnp.bfloat16),
            jax.ShapeDtypeStruct((couples, 2, rows), jnp.float32),
        ],
        scratch_shapes=[pltpu.VMEM((keys, block), jnp.float32)],
        compiler_params=pltpu.CompilerParams(vmem_limit_bytes=48 * 2**20),
        cost_estimate=pl.CostEstimate(flops=10**8, bytes_accessed=10**5, transcendentals=0),
    )(query_lin, *tables, pairs, pairs_across, doc_query, doc_key)


def attend_back(queries, d_mixed, totals, tables, pairs, pairs_across, doc_query, doc_key):
    rows, width = queries.shape
    block = 256
    keys = WINDOW + block
    couples = width // (2 * HD)
    last = (rows // block - 1, couples - 1)

    def kernel(q_ref, do_ref, total_ref, t0, t1, t2, pairs_ref, across_ref, dq_ref, dk_ref, d_lin_ref, d_pairs_ref, bias, d_keys, d_values, values):
        start = pl.multiple_of(pl.program_id(0) * block, block)
        window = pl.ds(start, keys)

        @pl.when((pl.program_id(0) == 0) & (pl.program_id(1) == 0))
        def clear():
            d_keys[...] = jnp.zeros_like(d_keys)
            d_values[...] = jnp.zeros_like(d_values)
            values[...] = pairs_ref[...][:, HD:]

        @pl.when(pl.program_id(1) == 0)
        def fill():
            bias[...] = no_entry(dq_ref[...], dk_ref[window, :], block, keys)

        own_keys = pairs_ref[window, :][:, :HD]
        own_values = values[window, :]
        keys_across = across_ref[pl.ds(0, HD), window]
        d_turned = []
        for head in range(2):
            part = slice(head * HD, (head + 1) * HD)
            q, do = q_ref[...][:, part], do_ref[...][:, part]
            scores = dot_last(own_keys, q) + bias[...]
            probs = jnp.exp(scores - total_ref[0][head : head + 1, :])
            d_probs = dot_last(own_values, do)
            product = probs * d_probs
            weighted = jnp.sum(product, axis=0, keepdims=True)
            d_scores = (product - probs * weighted).astype(jnp.bfloat16)
            d_turned.append(dot(keys_across, d_scores))
            d_keys[window, :] += dot(d_scores, q)
            d_values[window, :] += dot(probs.astype(jnp.bfloat16), do)
        d_turned = jnp.concatenate(d_turned, axis=0).T
        d_lin = turn(d_turned, (t0[...], t1[...], t2[...]), True) * HD ** (-0.5)
        d_lin_ref[...] = d_lin.astype(jnp.bfloat16)

        @pl.when((pl.program_id(0) == last[0]) & (pl.program_id(1) == last[1]))
        def finish():
            d_pairs_ref[...] = jnp.concatenate([d_keys[...], d_values[...]], axis=1)

    tile = pl.BlockSpec((block, 2 * HD), lambda i, j: (i, j))
    table = pl.BlockSpec((block, 2 * HD), lambda i, j: (i, 0))
    return pl.pallas_call(
        kernel,
        grid=(rows // block, couples),
        in_specs=[
            tile,
            tile,
            pl.BlockSpec((1, 2, block), lambda i, j: (j, 0, i)),
            table,
            table,
            table,
            pl.BlockSpec(pairs.shape, lambda i, j: (0, 0)),
            pl.BlockSpec(pairs_across.shape, lambda i, j: (0, 0)),
            pl.BlockSpec((1, block), lambda i, j: (0, i)),
            pl.BlockSpec(doc_key.shape, lambda i, j: (0, 0)),
        ],
        out_specs=[tile, pl.BlockSpec(pairs.shape, lambda i, j: (0, 0))],
        out_shape=[
            jax.ShapeDtypeStruct((rows, width), jnp.bfloat16),
            jax.ShapeDtypeStruct(pairs.shape, jnp.float32),
        ],
        scratch_shapes=[
            pltpu.VMEM((keys, block), jnp.float32),
            pltpu.VMEM((pairs.shape[0], HD), jnp.float32),
            pltpu.VMEM((pairs.shape[0], HD), jnp.float32),
            pltpu.VMEM((pairs.shape[0], HD), jnp.bfloat16),
        ],
        compiler_params=pltpu.CompilerParams(vmem_limit_bytes=48 * 2**20),
        cost_estimate=pl.CostEstimate(flops=10**8, bytes_accessed=10**5, transcendentals=0),
    )(queries, d_mixed, totals, *tables, pairs, pairs_across, doc_query, doc_key)


def put_pieces(pieces, positions, shards):
    count = len(pieces)
    others, rows, unused_width = pieces[0].shape
    depth = others + 1
    widths = [shard.shape[2] for shard in shards]

    def kernel(positions_ref, *refs):
        i, j = pl.program_id(0), pl.program_id(1)
        sources, locals_, targets = (
            refs[:count],
            refs[count : count + len(shards)],
            refs[count + len(shards) :],
        )
        for at in range(count):

            @pl.when((i == at) & (j < others))
            def take():
                start = 0
                for target, width in zip(targets, widths):
                    target[0, 0] = sources[at][j, :, pl.ds(start, width)]
                    start += width

        @pl.when(j == others)
        def keep():
            for target, source in zip(targets, locals_):
                target[0, 0] = source[0]

    return pl.pallas_call(
        kernel,
        out_shape=[
            jax.ShapeDtypeStruct((depth, count, rows, width), pieces[0].dtype) for width in widths
        ],
        grid_spec=pltpu.PrefetchScalarGridSpec(
            num_scalar_prefetch=1,
            grid=(count, depth),
            in_specs=[pl.BlockSpec(p.shape, lambda i, j, at: (0, 0, 0)) for p in pieces]
            + [pl.BlockSpec((1, rows, width), lambda i, j, at: (at[i], 0, 0)) for width in widths],
            out_specs=[
                pl.BlockSpec(
                    (1, 1, rows, width),
                    lambda i, j, at: (at[count + j], at[i], 0, 0),
                )
                for width in widths
            ],
        ),
        compiler_params=pltpu.CompilerParams(vmem_limit_bytes=40 * 2**20),
    )(positions, *pieces, *shards)


def rest(x, level):
    depth = x.shape[0]
    block = (1,) + x.shape[1:]
    zeros = (0,) * (x.ndim - 1)

    def kernel(level_ref, source, target):
        target[...] = source[...]

    return pl.pallas_call(
        kernel,
        out_shape=jax.ShapeDtypeStruct((depth - 1,) + x.shape[1:], x.dtype),
        grid_spec=pltpu.PrefetchScalarGridSpec(
            num_scalar_prefetch=1,
            grid=(depth - 1,),
            in_specs=[
                pl.BlockSpec(block, lambda i, at: (lax.rem(at[0] + i + 1, depth), *zeros))
            ],
            out_specs=pl.BlockSpec(block, lambda i, at: (i, *zeros)),
        ),
    )(level[None], x)


def spread(pieces, positions, shape, place):
    count = len(pieces)
    rows, width = pieces[0].shape

    def kernel(positions_ref, *refs):
        for at in range(count):

            @pl.when(pl.program_id(0) == at)
            def take():
                refs[-1][...] = refs[at][...].astype(jnp.float32)

    return pl.pallas_call(
        kernel,
        out_shape=jax.ShapeDtypeStruct(shape, jnp.float32),
        grid_spec=pltpu.PrefetchScalarGridSpec(
            num_scalar_prefetch=1,
            grid=(count,),
            in_specs=[pl.BlockSpec((rows, width), lambda i, at: (0, 0))] * count,
            out_specs=pl.BlockSpec((rows, width), lambda i, at: place(at[i])),
        ),
        compiler_params=pltpu.CompilerParams(vmem_limit_bytes=40 * 2**20),
    )(positions, *pieces)


GELU_SCALE = 0.7978845608028654
GELU_CUBE = 0.044715


def dot_first(a, b):
    return lax.dot_general(a, b, (((0,), (0,)), ((), ())), preferred_element_type=jnp.float32)


def feed(facts, x, grad, first_w, second_w, shard, down_pieces, down_shard, block_sum, back_sum, terms):
    rows, width = x.shape
    hidden = first_w.shape[1]
    half = hidden // 2
    column = width // 4
    depth = down_pieces[0].shape[0] + 1
    level_rows = width // depth
    full = depth * hidden
    started = back_sum is not None
    pieces = 8
    f32, bf16 = jnp.float32, jnp.bfloat16

    def kernel(facts_ref, x_ref, g_ref, *refs):
        wa_in, wb_in, shard_in, down_in, block_in = refs[:5]
        down_pieces_in = refs[5 : 5 + pieces]
        refs = refs[5 + pieces :]
        if started:
            back_in = refs[0]
            refs = refs[1 + pieces :]
        block_out, back_out, ga_out, gb_out = refs[:4]
        term_out = refs[4 : 4 + pieces]
        wa, wb, wd, a, b, d, act, da, db, block, back, ga, gb, gd, sems = refs[4 + pieces :]
        chip = facts_ref[1]
        core, level = facts_ref[2], facts_ref[7]

        def rows_of(source, target, side, sem):
            copies = []
            for i in range(1, depth):
                place = pl.multiple_of(lax.rem(level + i, depth) * level_rows, 16)
                copies.append(
                    pltpu.make_async_copy(
                        source.at[pl.ds((i - 1) * level_rows, level_rows)],
                        target.at[pl.ds(place, level_rows)],
                        sem,
                    )
                )
            place = pl.multiple_of(level * level_rows, 16)
            start = pl.multiple_of(side * full + chip * hidden, 128)
            copies.append(
                pltpu.make_async_copy(
                    shard_in.at[:, pl.ds(start, hidden)],
                    target.at[pl.ds(place, level_rows)],
                    sem,
                )
            )
            return copies

        for copy in rows_of(wa_in, wa, core, sems.at[0]):
            copy.start()
        for copy in rows_of(wb_in, wb, 1 - core, sems.at[1]):
            copy.start()

        @pl.when(chip == level)
        def here():
            pltpu.make_async_copy(down_in, wd, sems.at[2]).start()

        @pl.when(chip != level)
        def elsewhere():
            step = lax.rem(chip - level + depth - 1, depth)
            for i in range(pieces):
                side = jnp.where(i < 4, core, 1 - core)
                pltpu.make_async_copy(
                    down_pieces_in[i].at[step],
                    wd.at[
                        pl.ds(pl.multiple_of(side * half, 16), half),
                        pl.ds(pl.multiple_of(facts_ref[3 + i % 4] * column, 128), column),
                    ],
                    sems.at[2],
                ).start()

        load_block = pltpu.make_async_copy(block_in, block, sems.at[3])
        load_block.start()
        if started:
            load_back = pltpu.make_async_copy(back_in, back, sems.at[4])
            load_back.start()
        pltpu.make_async_copy(wa, wa, sems.at[0]).wait()
        a[...] = dot(x_ref[...], wa[...])
        pltpu.make_async_copy(wb, wb, sems.at[1]).wait()
        b[...] = dot(x_ref[...], wb[...])
        pltpu.make_async_copy(wd, wd, sems.at[2]).wait()
        d[...] = dot_last(g_ref[...], wd[...])
        swapped = facts_ref[0] == 1

        @pl.loop(0, rows // 16)
        def glu(i):
            part = pl.ds(pl.multiple_of(i * 16, 16), 16)
            for j in range(hidden // 384):
                lanes = slice(j * 384, (j + 1) * 384)
                one, two, slope = a[part, lanes], b[part, lanes], d[part, lanes]
                gate = jnp.where(swapped, two, one)
                up = jnp.where(swapped, one, two)
                square = gate * gate
                inner = gate * (square * (GELU_SCALE * GELU_CUBE) + GELU_SCALE)
                share = 0.5 * jnp.tanh(inner) + 0.5
                gelu = gate * share
                bend = square * (6.0 * GELU_SCALE * GELU_CUBE) + 2.0 * GELU_SCALE
                rise = share + gelu * (1.0 - share) * bend
                d_gate = (slope * up) * rise
                d_up = slope * gelu
                act[part, lanes] = (gelu * up).astype(bf16)
                da[part, lanes] = jnp.where(swapped, d_up, d_gate).astype(bf16)
                db[part, lanes] = jnp.where(swapped, d_gate, d_up).astype(bf16)

        for i in range(width // 384):
            part = pl.ds(i * 384, 384)
            gb[part, :] = dot_first(x_ref[:, i * 384 : (i + 1) * 384], db[...]).astype(bf16)
            pltpu.make_async_copy(gb.at[part], gb_out.at[part], sems.at[5]).start()
        for i in range(width // 384):
            part = pl.ds(i * 384, 384)
            ga[part, :] = dot_first(x_ref[:, i * 384 : (i + 1) * 384], da[...]).astype(bf16)
            pltpu.make_async_copy(ga.at[part], ga_out.at[part], sems.at[6]).start()
        for i in range(hidden // 384):
            part = pl.ds(i * 384, 384)
            gd[part, :] = dot_first(act[:, i * 384 : (i + 1) * 384], g_ref[...]).astype(bf16)
        stores = []
        for i in range(pieces):
            side = jnp.where(i < 4, core, 1 - core)
            stores.append(
                pltpu.make_async_copy(
                    gd.at[
                        pl.ds(pl.multiple_of(side * half, 16), half),
                        pl.ds(pl.multiple_of(facts_ref[3 + i % 4] * column, 128), column),
                    ],
                    term_out[i].at[chip],
                    sems.at[7 + i],
                )
            )
        for store in stores:
            store.start()
        if started:
            load_back.wait()

            back[...] += dot_last(da[...], wa[...])
            back[...] += dot_last(db[...], wb[...])
        else:
            back[...] = dot_last(da[...], wa[...])
            back[...] += dot_last(db[...], wb[...])
        store_back = pltpu.make_async_copy(back, back_out, sems.at[15])
        store_back.start()
        load_block.wait()
        for i in range(2):
            part = pl.ds(i * (rows // 2), rows // 2)
            block[part, :] += dot(act[part, :], wd[...])
            pltpu.make_async_copy(block.at[part], block_out.at[part], sems.at[16]).start()
        for store in stores:
            store.wait()
        pltpu.make_async_copy(gb, gb_out, sems.at[5]).wait()
        pltpu.make_async_copy(ga, ga_out, sems.at[6]).wait()
        store_back.wait()
        pltpu.make_async_copy(block, block_out, sems.at[16]).wait()

    anywhere = pl.BlockSpec(memory_space=pl.ANY)
    inside = pl.BlockSpec(memory_space=pltpu.VMEM)
    operands = [facts, x, grad, first_w, second_w, shard, down_shard, block_sum, *down_pieces]
    aliases = {}
    if started:
        aliases[7] = 0
        aliases[len(operands)] = 1
        operands.append(back_sum)
        for i, term in enumerate(terms):
            aliases[len(operands)] = 4 + i
            operands.append(term)
    sums = jax.ShapeDtypeStruct((rows, width), f32)
    grads = jax.ShapeDtypeStruct((width, hidden), bf16)
    results = pl.pallas_call(
        kernel,
        in_specs=[pl.BlockSpec(memory_space=pltpu.SMEM), inside, inside]
        + [anywhere] * (len(operands) - 3),
        out_specs=[anywhere] * (4 + pieces),
        out_shape=[sums, sums, grads, grads]
        + [jax.ShapeDtypeStruct((depth, half, column), bf16)] * pieces,
        input_output_aliases=aliases,
        scratch_shapes=[
            pltpu.VMEM((width, hidden), bf16),
            pltpu.VMEM((width, hidden), bf16),
            pltpu.VMEM((hidden, width), bf16),
            pltpu.VMEM((rows, hidden), f32),
            pltpu.VMEM((rows, hidden), f32),
            pltpu.VMEM((rows, hidden), f32),
            pltpu.VMEM((rows, hidden), bf16),
            pltpu.VMEM((rows, hidden), bf16),
            pltpu.VMEM((rows, hidden), bf16),
            pltpu.VMEM((rows, width), f32),
            pltpu.VMEM((rows, width), f32),
            pltpu.VMEM((width, hidden), bf16),
            pltpu.VMEM((width, hidden), bf16),
            pltpu.VMEM((hidden, width), bf16),
            pltpu.SemaphoreType.DMA((17,)),
        ],
        compiler_params=pltpu.CompilerParams(vmem_limit_bytes=56 * 2**20),
        cost_estimate=pl.CostEstimate(flops=10**8, bytes_accessed=10**5, transcendentals=0),
    )(*operands)
    return results[0], results[1], results[2], results[3], results[4:]


class Plane:
    def __init__(self):
        self.me = lax.axis_index("seq")
        self.core = self.me % 2
        self.chip = self.me // 2
        first = jnp.where(self.core == 0, 1, 2)
        self.chips = [self.chip, self.chip ^ first, self.chip ^ (3 - first), self.chip ^ 3]
        self.first_pairs = [(i, i ^ (2 if i % 2 == 0 else 4)) for i in range(8)]
        self.second_pairs = [(i, i ^ (4 if i % 2 == 0 else 2)) for i in range(8)]
        self.core_pairs = [(i, i ^ 1) for i in range(8)]
        self.sources = jnp.stack(
            [chip * 2 + self.core for chip in self.chips]
            + [chip * 2 + 1 - self.core for chip in self.chips]
        )

    def first(self, x):
        return lax.ppermute(x, "seq", self.first_pairs)

    def second(self, x):
        return lax.ppermute(x, "seq", self.second_pairs)

    def along(self, x):
        depth = lax.axis_size("fsdp")
        return [
            lax.ppermute(x, "fsdp", [((i + k) % depth, i) for i in range(depth)])
            for k in range(1, depth)
        ]

    def swap(self, x):
        return lax.ppermute(x, "seq", self.core_pairs)

    def down_columns(self, x):
        return lax.psum_scatter(x, "fsdp", scatter_dimension=0, tiled=True)


def places_of(arrival_order, ranks):
    row_count = arrival_order.shape[1]
    capacity = 2 * row_count // ranks
    arrived_at = arrival_order[0]
    owner = arrived_at // row_count
    owner_hits = (owner[:, None] == jnp.arange(ranks, dtype=jnp.int32)[None, :]).astype(jnp.int32)
    within = jnp.sum(jnp.cumsum(owner_hits, axis=0) * owner_hits, axis=1) - 1
    return owner * capacity + within, arrived_at % row_count


def to_slots(rows, slots, ranks, empty=0):
    capacity = 2 * rows.shape[0] // ranks
    out = jnp.full((ranks * capacity,) + rows.shape[1:], empty, rows.dtype)
    return out.at[slots].set(rows).reshape((ranks, capacity) + rows.shape[1:])


def from_slots(slots, landing):
    flat = slots.reshape((-1, slots.shape[-1]))
    out = jnp.zeros((flat.shape[0] // 2, flat.shape[1]), flat.dtype)
    return out.at[landing].set(flat, mode="drop")


def back_to_slots(rows, safe_place, ranks):
    return rows[safe_place].reshape(ranks, -1, rows.shape[1])


def exchange(x):
    return lax.all_to_all(x, "seq", split_axis=0, concat_axis=0, tiled=True)


def positions_of(lengths, row_count):
    position = lax.axis_index("seq")
    places = position * row_count + jnp.arange(row_count, dtype=jnp.int32)
    doc_query, offset_query = layout(lengths[0], places)
    key_places = (
        position * row_count - WINDOW + jnp.arange(WINDOW + row_count, dtype=jnp.int32)
    )
    doc_key, unused_offset = layout(lengths[0], key_places)
    cosine, sine = angles(offset_query.astype(jnp.float32), HD)
    return (doc_query[None, :], doc_key[:, None]), cosine, sine


def pair_of(kv_lin, cosine, sine):
    own_keys = rounded(rotate(kv_lin[:, :HD], cosine, sine))
    return jnp.concatenate([own_keys, rounded(kv_lin[:, HD:])], axis=1)


def with_earlier(pair, reach):
    return jnp.concatenate(
        [passed_along(pair, "seq", distance) for distance in range(reach, 0, -1)] + [pair], axis=0
    )


def owners_sum(d_pairs, row_count, reach):
    parts = [
        passed_along(
            rounded(d_pairs[(reach - distance) * row_count :][:row_count]), "seq", -distance
        )
        for distance in range(reach, 0, -1)
    ]
    own = d_pairs[reach * row_count :]
    for part in parts:
        own = own + widened(part)
    return own


def body(*operands):
    return square_body(*operands) if lax.axis_size("seq") == 8 else plain_body(*operands)


def plain_body(
    tokens,
    cotangent,
    arrival_order,
    lengths,
    norm_gain,
    w_query,
    w_kv,
    w_out,
    ffn_gain,
    w_gate_up,
    w_down,
):
    row_count = tokens.shape[1]
    ranks = lax.axis_size("seq")
    reach = WINDOW // row_count
    position = lax.axis_index("seq")

    def whole(shard):
        part = shard.shape[0] // ranks
        mine = lax.dynamic_slice_in_dim(shard, position * part, part, axis=0)
        return lax.all_gather(mine, ("fsdp", "seq"), axis=0, tiled=True)

    def summed(grad):
        mine = lax.psum_scatter(rounded(grad), ("fsdp", "seq"), scatter_dimension=0, tiled=True)
        return widened(lax.all_gather(mine, "seq", axis=0, tiled=True))

    send_slot, send_place = places_of(arrival_order, ranks)
    got_tokens = exchange(to_slots(tokens[0], send_slot, ranks))
    got_cotangent = exchange(to_slots(cotangent[0], send_slot, ranks))
    recv_place = exchange(to_slots(send_place, send_slot, ranks, -1)).reshape(-1)
    is_live = recv_place >= 0
    landing = jnp.where(is_live, recv_place, row_count)
    safe_place = jnp.where(is_live, recv_place, 0)
    packed_f = widened(from_slots(got_tokens, landing))
    packed_grad = from_slots(got_cotangent, landing)
    query_w, kv_w, out_w, down_w, gate_up_w = (
        whole(w_query),
        whole(w_kv),
        whole(w_out),
        whole(w_down),
        whole(w_gate_up),
    )
    gain_attn, gain_ffn = (
        widened(lax.all_gather(gain, "fsdp", axis=0, tiled=True)) for gain in (norm_gain, ffn_gain)
    )
    docs, cosine, sine = positions_of(lengths, row_count)
    tables = tables_of(cosine, sine, 2, 0)

    normed = rounded(rms_scale(packed_f, gain_attn))
    pair_rows = with_earlier(pair_of(dot(normed, kv_w), cosine, sine), reach)
    queries, mixed, totals = attend(dot(normed, query_w), tables, pair_rows, pair_rows.T, *docs)
    hidden_state = packed_f + dot(mixed, out_w)
    ffn_in = rounded(rms_scale(hidden_state, gain_ffn))
    gate, up = dot(ffn_in, gate_up_w[:, :FF]), dot(ffn_in, gate_up_w[:, FF:])
    activated, pull = jax.vjp(lambda g, u: jax.nn.gelu(g, approximate=True) * u, gate, up)
    activated = rounded(activated)
    block_rows = rounded(hidden_state + dot(activated, down_w))

    d_gate, d_up = pull(dot_across(packed_grad, down_w))
    d_gate_up = jnp.concatenate([rounded(d_gate), rounded(d_up)], axis=1)
    unused_scaled, ffn_norm_pull = jax.vjp(rms_scale, hidden_state, gain_ffn)
    d_hidden_norm, grad_gain_ffn = ffn_norm_pull(dot_across(d_gate_up, gate_up_w))
    d_hidden = widened(packed_grad) + d_hidden_norm
    d_branch = rounded(d_hidden)
    d_mixed = rounded(dot_across(d_branch, out_w))
    d_query_lin, d_pairs = attend_back(
        queries, d_mixed, totals, tables, pair_rows, pair_rows.T, *docs
    )
    d_own = owners_sum(d_pairs, row_count, reach)
    d_kv_lin = rounded(
        jnp.concatenate([unrotate(d_own[:, :HD], cosine, sine), d_own[:, HD:]], axis=1)
    )
    d_normed = dot_across(d_query_lin, query_w) + dot_across(d_kv_lin, kv_w)
    unused_normed, attn_norm_pull = jax.vjp(rms_scale, packed_f, gain_attn)
    d_packed_norm, grad_gain_attn = attn_norm_pull(d_normed)
    grad_rows = rounded(d_hidden + d_packed_norm)
    block_arrived, grad_arrived = (
        exchange(back_to_slots(rows, safe_place, ranks)).reshape(-1, rows.shape[1])[
            send_slot
        ]
        for rows in (block_rows, grad_rows)
    )
    total_gain_attn, total_gain_ffn = (
        lax.psum(lax.psum_scatter(gain, "fsdp", scatter_dimension=0, tiled=True), "seq")
        for gain in (grad_gain_attn, grad_gain_ffn)
    )
    return (
        block_arrived[None],
        grad_arrived[None],
        total_gain_attn,
        summed(dot_rows(normed, d_query_lin)),
        summed(dot_rows(normed, d_kv_lin)),
        summed(dot_rows(mixed, d_branch)),
        total_gain_ffn,
        summed(dot_rows(ffn_in, d_gate_up)),
        summed(dot_rows(activated, packed_grad)),
    )


def square_body(
    tokens,
    cotangent,
    arrival_order,
    lengths,
    norm_gain,
    w_query,
    w_kv,
    w_out,
    ffn_gain,
    w_gate_up,
    w_down,
):
    row_count = tokens.shape[1]
    model_width = tokens.shape[2]
    ranks = lax.axis_size("seq")
    depth = lax.axis_size("fsdp")
    reach = WINDOW // row_count
    shard_rows = w_query.shape[0]
    part_rows = shard_rows // ranks
    quarter = FF // 4
    column = model_width // 4
    half_rows = w_down.shape[0] // 2
    split = model_width + 2 * HD
    plane = Plane()
    level = lax.axis_index("fsdp").astype(jnp.int32)
    levels = (level + 1 + jnp.arange(depth, dtype=jnp.int32)) % depth
    at = jnp.concatenate([plane.sources, levels]).astype(jnp.int32)

    def my_rows(shard):
        return lax.dynamic_slice_in_dim(shard, plane.me * part_rows, part_rows, axis=0)

    def by_parts(shard):
        return shard.reshape(ranks, part_rows, shard.shape[1])

    def second_halves(slots):
        return [plane.swap(slots[i]) for i in (0, 2, 1, 3)]


    gains = jnp.concatenate([norm_gain, ffn_gain]).reshape(part_rows, -1)
    gain_width = gains.shape[1]
    early = plane.along(
        jnp.concatenate(
            [my_rows(w_query), my_rows(w_kv), jnp.pad(gains, ((0, 0), (0, 128 - gain_width)))],
            axis=1,
        )
    )
    send_slot, send_place = places_of(arrival_order, ranks)
    labels = jnp.stack([send_place // 2, send_place % 2, jnp.ones_like(send_place)], axis=1)
    labels = jnp.pad(labels.astype(jnp.bfloat16), ((0, 0), (0, 125)))
    token_slots = to_slots(jnp.concatenate([tokens[0], labels], axis=1), send_slot, ranks)
    got_tokens = exchange(token_slots)
    *early, cotangent_rows, out_mine, down_mine, gate_up_mine = fence(
        *early, after(cotangent[0], token_slots), my_rows(w_out), w_down, w_gate_up
    )
    early = jnp.stack(early)
    gain_rows = early[:, :, split : split + gain_width].reshape(depth - 1, 2, shard_rows)
    early = early[:, :, :split]

    def down_of(shard, chip):
        piece = lax.dynamic_slice(
            shard, (plane.core * half_rows, chip * column), (half_rows, column)
        )
        return lax.all_gather(piece, "fsdp", axis=0, tiled=False)

    down_piece = down_of(down_mine, plane.chip)
    gate_up_piece = lax.dynamic_slice(
        gate_up_mine, (0, plane.core * FF + plane.chip * quarter), (shard_rows, quarter)
    )
    gate_up_piece = lax.all_gather(gate_up_piece, "fsdp", axis=0, tiled=False)

    early_u, early_v, early_0 = plane.first(early), plane.second(early), plane.swap(early)
    out = plane.along(out_mine)
    docs, cosine, sine = positions_of(lengths, row_count)
    tables = rows_first(tables_of(cosine, sine, 2, 0))
    cotangent_slots = to_slots(cotangent_rows, send_slot, ranks)
    early_u, early_v, early_0, got_tokens, out, cotangent_slots, tables = fence(
        early_u, early_v, early_0, got_tokens, out, cotangent_slots, tables
    )
    got_cotangent = exchange(cotangent_slots)

    out = jnp.stack(out)
    early_d, early_2, early_1 = plane.second(early_u), plane.swap(early_u), plane.swap(early_v)
    out_u, out_v, out_0 = plane.first(out), plane.second(out), plane.swap(out)
    labels = got_tokens.reshape(-1, model_width + 128)[:, model_width:].astype(jnp.int32)
    safe_place = labels[:, 0] * 2 + labels[:, 1]
    is_live = labels[:, 2] == 1
    landing = jnp.where(is_live, safe_place, row_count)
    packed_f = widened(from_slots(got_tokens, landing)[:, :model_width])
    gain_rows = jnp.concatenate([gain_rows, gains.reshape(1, 2, shard_rows)], axis=0)
    gain_rows = gain_rows[(jnp.arange(depth, dtype=jnp.int32) + depth - 1 - level) % depth]
    gain_attn = widened(gain_rows[:, 0].reshape(model_width))
    gain_ffn = widened(gain_rows[:, 1].reshape(model_width))
    normed = rounded(rms_scale(packed_f, gain_attn))
    early_d, early_2, early_1, out_u, out_v, out_0, normed = fence(
        early_d, early_2, early_1, out_u, out_v, out_0, normed
    )

    early_3, out_d, out_2, out_1 = (
        plane.swap(early_d),
        plane.second(out_u),
        plane.swap(out_u),
        plane.swap(out_v),
    )
    down_piece = rest(after(down_piece, normed), level)
    early_3, out_d, out_2, out_1, down_piece = fence(early_3, out_d, out_2, out_1, down_piece)

    down_u, down_v, down_0 = (
        plane.first(down_piece),
        plane.second(down_piece),
        plane.swap(down_piece),
    )
    out_3 = plane.swap(out_d)
    query_w, kv_w = put_pieces(
        [early, early_u, early_v, early_d, early_0, early_1, early_2, early_3],
        after(at, down_piece),
        [by_parts(w_query), by_parts(w_kv)],
    )
    query_w = query_w.reshape(model_width, model_width)
    kv_w = kv_w.reshape(model_width, 2 * HD)
    query_lin = dot(normed, query_w)
    pair = pair_of(dot(normed, kv_w), cosine, sine)
    (out_w,) = put_pieces(
        [out, out_u, out_v, out_d, out_0, out_1, out_2, out_3],
        after(at, pair),
        [by_parts(w_out)],
    )
    out_w = out_w.reshape(model_width, model_width)
    down_u, down_v, down_0, out_w, query_lin, pair = fence(
        down_u, down_v, down_0, out_w, query_lin, pair
    )

    pair_rows = with_earlier(pair, reach)
    down_2, down_1 = plane.swap(down_u), plane.swap(down_v)
    down_d = down_of(after(w_down, gate_up_piece), plane.chips[3])
    gate_up_piece = rest(gate_up_piece, level)
    gate_up_piece = gate_up_piece.reshape((depth - 1) * shard_rows, quarter)
    packed_grad = from_slots(after(got_cotangent, gate_up_piece), landing)
    pair_rows, down_2, down_1, gate_up_piece, packed_grad = fence(
        pair_rows, down_2, down_1, gate_up_piece, packed_grad
    )

    gate_up_u, gate_up_v, gate_up_0 = (
        plane.first(gate_up_piece),
        plane.second(gate_up_piece),
        plane.swap(gate_up_piece),
    )
    pairs_across = pair_rows.T
    queries, mixed, totals = attend(query_lin, tables, pair_rows, pairs_across, *docs)
    down_d = rest(after(down_d, mixed), level)
    down_3 = plane.swap(down_d)
    hidden_state = packed_f + dot(after(mixed, down_d), out_w)
    ffn_in = rounded(rms_scale(hidden_state, gain_ffn))

    def chunk(slot, first_w, second_w, chunk_in, block_sum, back_sum, terms):
        facts = [plane.core, plane.chips[slot], plane.core, *plane.chips, level]
        return feed(
            jnp.stack(facts).astype(jnp.int32),
            chunk_in,
            packed_grad,
            first_w,
            second_w,
            w_gate_up,
            [down_piece, down_u, down_v, down_d, down_0, down_1, down_2, down_3],
            w_down,
            block_sum,
            back_sum,
            terms,
        )

    block_sum, back_sum, own_0, other_0, terms = chunk(
        0, gate_up_piece, gate_up_0, ffn_in, hidden_state, None, None
    )
    gate_up_u, gate_up_v, block_sum, back_sum, own_0, other_0 = fence(
        gate_up_u, gate_up_v, block_sum, back_sum, own_0, other_0
    )

    gate_up_2, gate_up_1 = plane.swap(gate_up_u), plane.swap(gate_up_v)
    gate_up_2, gate_up_1, gate_up_u, back_sum = fence(gate_up_2, gate_up_1, gate_up_u, back_sum)
    gate_up_d, swap_0 = plane.second(gate_up_u), plane.swap(other_0)
    block_sum, back_sum, own_u, other_u, terms = chunk(
        1, gate_up_u, gate_up_1, ffn_in, block_sum, back_sum, terms
    )
    gate_up_d, swap_0, block_sum, back_sum, own_u, other_u = fence(
        gate_up_d, swap_0, block_sum, back_sum, own_u, other_u
    )
    gate_up_3, swap_u = plane.swap(gate_up_d), plane.swap(other_u)
    block_sum, back_sum, own_v, other_v, terms = chunk(
        2, gate_up_v, gate_up_2, ffn_in, block_sum, back_sum, terms
    )
    gate_up_3, swap_u, block_sum, back_sum, own_v, other_v = fence(
        gate_up_3, swap_u, block_sum, back_sum, own_v, other_v
    )
    sum_v, other_v, back_sum = fence(added(own_v, swap_u), other_v, back_sum)
    from_v, swap_v = plane.second(sum_v), plane.swap(other_v)
    block_sum, back_sum, own_d, other_d, terms = chunk(
        3, gate_up_d, gate_up_3, ffn_in, block_sum, back_sum, terms
    )
    sum_u = added(own_u, swap_v)
    from_v, sum_u, block_sum, back_sum, own_d, other_d, terms = fence(
        from_v, sum_u, block_sum, back_sum, own_d, other_d, terms
    )

    from_u, swap_d = plane.first(sum_u), plane.swap(other_d)
    terms = [term.reshape(depth * half_rows, column) for term in terms]
    down_swaps = [plane.swap(term) for term in terms[4:]]
    unused_scaled, ffn_norm_pull = jax.vjp(rms_scale, hidden_state, gain_ffn)
    d_hidden_norm, grad_gain_ffn = ffn_norm_pull(back_sum)
    d_hidden = widened(packed_grad) + d_hidden_norm
    d_branch = rounded(d_hidden)
    d_mixed = rounded(dot_across(d_branch, out_w))
    sum_d = added_apart(after(own_d, d_mixed), swap_d)
    part_d = plane.down_columns(sum_d)
    down_sums = [
        added_apart(after(term, sum_d), down_swaps[match])
        for term, match in zip(terms[:4], (0, 2, 1, 3))
    ]
    from_u, d_branch, d_mixed, down_sums = fence(from_u, d_branch, d_mixed, down_sums)
    from_down_d, from_down_v = plane.second(down_sums[3]), plane.second(down_sums[2])
    total = added(own_0, swap_0, from_v, from_u)
    part_0 = plane.down_columns(total)
    d_query_lin, d_pairs = attend_back(
        queries, after(d_mixed, total), totals, tables, pair_rows, pairs_across, *docs
    )
    from_down_d, from_down_v, d_query_lin, d_pairs, block_sum, part_d = fence(
        from_down_d, from_down_v, d_query_lin, d_pairs, block_sum, part_d
    )
    part_d_u = plane.first(part_d)

    def by_rows(grad):
        pieces = rounded(grad).reshape(depth, ranks, part_rows, grad.shape[1])
        return [
            lax.dynamic_index_in_dim(pieces, plane.sources[i], axis=1, keepdims=False)
            for i in range(8)
        ]

    d_own = owners_sum(d_pairs, row_count, reach)
    down_u = added(down_sums[1], from_down_d)
    block_slots = back_to_slots(rounded(block_sum), safe_place, ranks)
    d_own, down_u, block_slots, part_d_u = fence(d_own, down_u, block_slots, part_d_u)
    home_out = exchange(block_slots)
    from_down_u, part_d = plane.first(down_u), plane.second(part_d_u)
    grad_out = dot_rows(mixed, after(d_branch, block_slots))
    out_terms = [p.reshape(depth * part_rows, model_width) for p in by_rows(grad_out)]
    out_swaps = [plane.swap(term) for term in out_terms[4:]]
    d_kv_lin = rounded(
        jnp.concatenate([unrotate(d_own[:, :HD], cosine, sine), d_own[:, HD:]], axis=1)
    )
    grad_query = dot_rows(normed, after(d_query_lin, *out_terms))
    grad_kv = dot_rows(normed, d_kv_lin)
    d_normed = dot_across(d_query_lin, query_w) + dot_across(d_kv_lin, kv_w)
    unused_normed, attn_norm_pull = jax.vjp(rms_scale, packed_f, gain_attn)
    d_packed_norm, grad_gain_attn = attn_norm_pull(d_normed)
    grad_rows = rounded(d_hidden + d_packed_norm)
    gain_rows = jnp.concatenate(
        [
            rounded(grad_gain_attn).reshape(depth, 1, shard_rows),
            rounded(grad_gain_ffn).reshape(depth, 1, shard_rows),
        ],
        axis=2,
    )
    gain_rows = jnp.pad(gain_rows, ((0, 0), (0, 15), (0, split - 2 * shard_rows)))
    early_terms = [
        jnp.concatenate([jnp.concatenate([q, k], axis=2), gain_rows], axis=1).reshape(
            depth * (part_rows + 16), split
        )
        for q, k in zip(by_rows(grad_query), by_rows(grad_kv))
    ]
    grad_slots = back_to_slots(after(grad_rows, *early_terms), safe_place, ranks)
    from_down_u, part_d, early_terms, out_swaps, grad_slots, home_out = fence(
        from_down_u, part_d, early_terms, out_swaps, grad_slots, home_out
    )

    home_grad = exchange(grad_slots)
    early_swaps = [plane.swap(term) for term in early_terms[4:]]
    out_d, out_v = added(out_terms[3], out_swaps[3]), added(out_terms[2], out_swaps[1])
    out_from_d, out_from_v = plane.second(out_d), plane.second(out_v)
    total = added(after(down_sums[0], out_d, out_v), from_down_v, from_down_u)
    mine_down = plane.down_columns(total)
    early_d = added(early_terms[3], early_swaps[3])
    early_v = added(early_terms[2], early_swaps[1])
    block_arrived = home_out.reshape(-1, model_width)[send_slot]
    out_from_d, out_from_v, early_d, early_v, early_swaps, part_0, block_arrived = fence(
        out_from_d, out_from_v, early_d, early_v, early_swaps, part_0, block_arrived
    )

    mine_gate_up = added(part_0, part_d)
    early_from_d, early_from_v = plane.second(early_d), plane.second(early_v)
    out_from_u = plane.first(added(out_terms[1], out_swaps[2], out_from_d))
    gate_up_u, gate_up_v, gate_up_0 = (
        plane.first(mine_gate_up),
        plane.second(mine_gate_up),
        plane.swap(mine_gate_up),
    )
    total = added(out_terms[0], out_swaps[0], out_from_v, out_from_u)
    mine_out = plane.down_columns(total)
    early_from_d, early_from_v, total, gate_up_u, gate_up_v, gate_up_0, home_grad = fence(
        early_from_d, early_from_v, total, gate_up_u, gate_up_v, gate_up_0, home_grad
    )

    early_from_u = plane.first(added(early_terms[1], early_swaps[2], early_from_d))
    gate_up_d, gate_up_2, gate_up_1 = (
        plane.second(gate_up_u),
        plane.swap(gate_up_u),
        plane.swap(gate_up_v),
    )
    grad_arrived = home_grad.reshape(-1, model_width)[send_slot]
    early_from_u, gate_up_d, gate_up_2, gate_up_1, mine_down, grad_arrived = fence(
        early_from_u, gate_up_d, gate_up_2, gate_up_1, mine_down, grad_arrived
    )

    total = added(early_terms[0], early_swaps[0], early_from_v, early_from_u)
    mine_early = plane.down_columns(total)
    gate_up_3 = plane.swap(gate_up_d)
    down_own = [mine_down, plane.first(mine_down), plane.second(mine_down)]
    total_gate_up = spread(
        [mine_gate_up, gate_up_u, gate_up_v, gate_up_d]
        + [gate_up_0, gate_up_1, gate_up_2, gate_up_3],
        after(plane.sources, total),
        (shard_rows, 2 * FF),
        lambda p: (0, (p % 2) * 4 + p // 2),
    )
    down_own, total_gate_up, mine_out = fence(down_own, total_gate_up, mine_out)

    down_own.append(plane.second(down_own[1]))
    down_swaps = [plane.swap(piece) for piece in down_own[:3]]
    out_own = [mine_out, plane.first(mine_out), plane.second(mine_out)]
    down_own, down_swaps, out_own, mine_early = fence(down_own, down_swaps, out_own, mine_early)

    down_swaps.append(plane.swap(down_own[3]))
    out_own.append(plane.second(out_own[1]))
    piece = mine_early[:part_rows]
    early_own = [piece, plane.first(piece), plane.second(piece)]
    total_down = spread(
        down_own + [down_swaps[i] for i in (0, 2, 1, 3)],
        plane.sources,
        (2 * half_rows, model_width),
        lambda p: (p % 2, p // 2),
    )
    early_own, out_own, total_down = fence(early_own, out_own, total_down)
    early_own.append(plane.second(early_own[1]))
    total_out = spread(
        out_own + second_halves(out_own),
        plane.sources,
        (shard_rows, model_width),
        lambda p: (p, 0),
    )
    early_own, total_out = fence(early_own, total_out)
    total_early = spread(
        early_own + second_halves(early_own),
        plane.sources,
        (shard_rows, split),
        lambda p: (p, 0),
    )
    return (
        block_arrived[None],
        grad_arrived[None],
        widened(mine_early[part_rows, :shard_rows]),
        total_early[:, :model_width],
        total_early[:, model_width:],
        total_out,
        widened(mine_early[part_rows, shard_rows : 2 * shard_rows]),
        total_gate_up,
        total_down,
    )


def solution(mesh):
    placed = (
        P("fsdp", "seq", None),
        P("fsdp", "seq", None),
        P("fsdp", "seq"),
        P("fsdp", None),
        P("fsdp"),
        P("fsdp", None),
        P("fsdp", None),
        P("fsdp", None),
        P("fsdp"),
        P("fsdp", None),
        P("fsdp", None),
    )
    return jax.shard_map(
        body,
        mesh=mesh,
        in_specs=placed,
        out_specs=(
            P("fsdp", "seq", None),
            P("fsdp", "seq", None),
            P("fsdp"),
            P("fsdp", None),
            P("fsdp", None),
            P("fsdp", None),
            P("fsdp"),
            P("fsdp", None),
            P("fsdp", None),
        ),
        check_vma=False,
    )
```
